32 devices in a mesh: comp: 8 (over z, y), rank: 4 (over x, core).
Axes of the slice: x: 2, y: 2, z: 4, core: 2. Of those that a mesh axis runs over, the one named last changes fastest.
Arguments:
- density: float32 [32, 16384], P('comp'), may hold values from 0.1 to 1
- row_left: float32 [8, 32], replicated, may hold values from -4 to 4
- col_left: float32 [8, 16384], replicated, may hold values from -4 to 4
- row_right: float32 [8, 32], replicated, may hold values from -4 to 4
- col_right: float32 [8, 16384], replicated, may hold values from -4 to 4
Outputs:
- gain: float32 [32, 16384], P(('comp', 'rank'))
The draws below stay inside these ranges and needn't reach their ends.
All inputs are finite; a program needn't handle non-finite values.
Results may differ from the reference program's by a relative error of at most 0.00021.
Values sent between devices are 32-bit elements; how exact they have to be, the bound alone decides.
No kernel may reach another device: no remote copies, remote signals or barrier semaphores. Data moves between devices by JAX's collectives and lax.ppermute only.
A program may use at most 192 MiB of HBM per device.

```python
import math
import jax
import jax.numpy as jnp

NB = 16384
R = 8
NA = 32


def shard_levels(rng, extent, pieces, least, high):
    gain = 1.0
    for dim, blocks in pieces:
        heights = jax.random.uniform(jax.random.fold_in(jax.random.fold_in(rng, 6), dim), (blocks,), jnp.float32, least / len(pieces), high / len(pieces))
        gain = gain * jnp.repeat(jnp.exp(heights), extent[dim] // blocks).reshape((-1,) + (1,) * (len(extent) - 1 - dim))
    return gain


def normal_values(own_key, extent, deviation, bound, dtype=jnp.bfloat16):
    drawn = deviation * jax.random.normal(own_key, extent, jnp.float32)
    return jnp.clip(drawn, min=-bound, max=bound).astype(dtype)


def setup_inputs(seed: int = 0) -> dict:
    key_list = jax.random.split(jax.random.key(seed), 6)
    return {
        "density": jnp.clip(jnp.exp(math.log(1.0) - 2.3025851 * jax.random.uniform(key_list[0], (NA, NB), jnp.float32) ** shard_levels(key_list[0], (NA, NB), ((0, 8),), -0.2, 0.2)), 0.1, 1.0),
        "row_left": normal_values(key_list[1], (R, NA), 1.0, 4.0, jnp.float32),
        "col_left": normal_values(key_list[2], (R, NB), 1.0, 4.0, jnp.float32),
        "row_right": normal_values(key_list[3], (R, NA), 1.0, 4.0, jnp.float32),
        "col_right": normal_values(key_list[4], (R, NB), 1.0, 4.0, jnp.float32),
    }


def reference(density, row_left, col_left, row_right, col_right):
    padded_shape = (2 * NA, 2 * NB)
    running_sum = jnp.zeros((NA, NB), jnp.float32)
    for rank_term in range(R):
        left_field = row_left[rank_term][:, None] * density * col_left[rank_term][None, :]
        right_field = row_right[rank_term][:, None] * density * col_right[rank_term][None, :]
        left_spectrum = jnp.fft.rfft2(left_field, s=padded_shape)
        right_spectrum = jnp.fft.rfft2(right_field, s=padded_shape)
        product = jnp.fft.irfft2(left_spectrum * right_spectrum, s=padded_shape)
        running_sum = running_sum + product[:NA, :NB]
    return (running_sum * (0.5 / math.sqrt(NA * NB))).astype(jnp.float32)
```

```python
import math

import jax
import jax.numpy as jnp
import numpy as np
from jax import lax
from jax.experimental import pallas as pl
from jax.experimental.pallas import tpu as pltpu
from jax.sharding import PartitionSpec as P

LANES = 128
VMEM_BYTES = 56 * 1024 * 1024
AXES = ("comp", "rank")
PAD = 4
PRODUCT_ROWS = 256


def split_parts(values):
    high = values.astype(jnp.bfloat16)
    low = (values - high.astype(jnp.float32)).astype(jnp.bfloat16)
    return high, low


def host_split(values):
    return split_parts(jnp.asarray(values, jnp.float32))


def dot_split(rows, table_high, table_low):
    high, low = split_parts(rows)
    total = jnp.dot(high, table_high, preferred_element_type=jnp.float32)
    total += jnp.dot(low, table_high, preferred_element_type=jnp.float32)
    total += jnp.dot(high, table_low, preferred_element_type=jnp.float32)
    return total


def forward_table():
    angles = 2.0 * np.pi * np.outer(np.arange(LANES), np.arange(LANES)) / LANES
    cosine, sine = np.cos(angles), np.sin(angles)
    return np.block([[cosine, -sine], [sine, cosine]])


def inverse_table():
    angles = 2.0 * np.pi * np.outer(np.arange(LANES), np.arange(LANES)) / LANES
    return np.concatenate([np.cos(angles), -np.sin(angles)], axis=0)


def block_twiddles(blocks):
    angles = 2.0 * np.pi * np.outer(np.arange(blocks), np.arange(LANES)) / (blocks * LANES)
    table = np.stack([np.cos(angles), -np.sin(angles)], axis=1)
    return jnp.asarray(
        np.broadcast_to(table[:, :, None, :], (blocks, 2, 8, LANES)), jnp.float32
    )


def final_tables(devices, groups, blocks, width):
    owner = np.arange(devices) % groups
    frequency = (owner[:, None] + groups * np.arange(blocks)[None, :]).astype(np.float64) + 0.25
    frequency = np.broadcast_to(frequency[:, None, :], (devices, 2, blocks))
    inner = 2.0 * np.pi * frequency[..., None] * np.arange(LANES) / width
    rows = devices * 2 * blocks
    inner_cos = np.cos(inner).reshape(rows, LANES)
    inner_sin = np.sin(inner).reshape(rows, LANES)
    outer_count = width // LANES
    outer = 2.0 * np.pi * frequency * LANES / width
    outer = np.arange(outer_count)[:, None] * outer.reshape(1, rows)
    is_real = np.broadcast_to(np.array([True, False])[None, :, None], (devices, 2, blocks))
    is_real = is_real.reshape(1, rows)
    with_cos = np.where(is_real, np.cos(outer), -np.sin(outer))
    with_sin = np.where(is_real, -np.sin(outer), -np.cos(outer))
    return inner_cos, inner_sin, np.concatenate([with_cos, with_sin], axis=1)


def block_fourier(reals, imags):
    count = len(reals)
    if count == 1:
        return reals, imags
    if count == 2:
        return (
            [reals[0] + reals[1], reals[0] - reals[1]],
            [imags[0] + imags[1], imags[0] - imags[1]],
        )
    even_real, odd_real = reals[0] + reals[2], reals[0] - reals[2]
    even_imag, odd_imag = imags[0] + imags[2], imags[0] - imags[2]
    pair_real, gap_real = reals[1] + reals[3], reals[1] - reals[3]
    pair_imag, gap_imag = imags[1] + imags[3], imags[1] - imags[3]
    return (
        [even_real + pair_real, odd_real + gap_imag, even_real - pair_real, odd_real - gap_imag],
        [even_imag + pair_imag, odd_imag - gap_real, even_imag - pair_imag, odd_imag + gap_real],
    )


def main_kernel(
    blocks,
    rho,
    left_cos,
    left_sin,
    right_cos,
    right_sin,
    row_factor,
    twiddle,
    table_high,
    table_low,
    back_high,
    back_low,
    out,
    partial,
    rows,
    spectrum,
    product,
    mixed,
):
    row_tiles = rho.shape[0]
    total_rows = row_tiles * 8
    width = rho.shape[2]
    inner = blocks * LANES
    outer = width // inner
    weights = (left_cos, left_sin, right_cos, right_sin)
    unroll = 4

    def reduce_tile(index, carry):
        block = lax.rem(index, blocks)
        row_tile = lax.div(index, blocks)

        def step(at, sums):
            sums = list(sums)
            for extra in range(unroll):
                lane = pl.multiple_of((at * unroll + extra) * inner + block * LANES, LANES)
                factors = [ref[:, pl.ds(lane, LANES)] for ref in weights]
                for row in range(8):
                    value = rho[row_tile, pl.ds(row, 1), pl.ds(lane, LANES)]
                    value = jnp.broadcast_to(value, (8, LANES))
                    for part in range(4):
                        sums[row * 4 + part] += value * factors[part]
            return tuple(sums)

        zero = jnp.zeros((8, LANES), jnp.float32)
        sums = lax.fori_loop(0, outer // unroll, step, (zero,) * 32)
        for row in range(8):
            for part in range(4):
                partial[part, block, row_tile * 8 + row] = sums[row * 4 + part]
        return carry

    lax.fori_loop(0, row_tiles * blocks, reduce_tile, 0)

    def butterfly(at, carry):
        for extra in range(2):
            row = at * 2 + extra
            for side in range(2):
                factor = row_factor[side, row]
                reals = [partial[2 * side, block, row] * factor for block in range(blocks)]
                imags = [partial[2 * side + 1, block, row] * factor for block in range(blocks)]
                reals, imags = block_fourier(reals, imags)
                for block in range(blocks):
                    real, imag = reals[block], imags[block]
                    if block > 0:
                        cosine, sine = twiddle[block, 0], twiddle[block, 1]
                        real, imag = real * cosine - imag * sine, real * sine + imag * cosine
                    place = pl.ds(pl.multiple_of(row * 8, 8), 8)
                    rows[block * 2 + side, place, pl.ds(0, LANES)] = real
                    rows[block * 2 + side, place, pl.ds(LANES, LANES)] = imag
        return carry

    lax.fori_loop(0, total_rows // 2, butterfly, 0)

    chunk_tiles = PRODUCT_ROWS // 8
    chunks = total_rows // chunk_tiles
    spectrum[:, :, pl.ds(0, PAD)] = jnp.zeros((2 * blocks, 3, PAD, 8, LANES), jnp.float32)

    def transform(at, carry):
        plane = lax.div(at, chunks)
        chunk = lax.rem(at, chunks)
        place = pl.ds(pl.multiple_of(chunk * PRODUCT_ROWS, PRODUCT_ROWS), PRODUCT_ROWS)
        result = dot_split(rows[plane, place, :], table_high[...], table_low[...])
        result = result.reshape(chunk_tiles, 8, 2 * LANES)
        real, imag = result[:, :, :LANES], result[:, :, LANES:]
        place = pl.ds(PAD + chunk * chunk_tiles, chunk_tiles)
        spectrum[plane, 0, place] = real
        spectrum[plane, 1, place] = imag
        spectrum[plane, 2, place] = real + imag
        return carry

    lax.fori_loop(0, 2 * blocks * chunks, transform, 0)

    def convolve(index, carry):
        block = lax.rem(index, blocks)
        out_tile = lax.div(index, blocks)

        def step(at, sums):
            sums = list(sums)
            left_base = PAD + 4 * at
            right_base = PAD + 4 * (out_tile - at)
            for part in range(3):
                left = [spectrum[2 * block, part, left_base + k] for k in range(4)]
                right = {k: spectrum[2 * block + 1, part, right_base + k] for k in range(-3, 4)}
                for row in range(4):
                    for k in range(4):
                        sums[row * 3 + part] += left[k] * right[row - k]
            return tuple(sums)

        zero = jnp.zeros((8, LANES), jnp.float32)
        sums = lax.fori_loop(0, out_tile + 1, step, (zero,) * 12)
        for row in range(4):
            both_real, both_imag, crossed = sums[row * 3 : row * 3 + 3]
            base = (out_tile * 4 + row) * 2 * blocks + block
            product[base] = both_real - both_imag
            product[base + blocks] = crossed - both_real - both_imag
        return carry

    lax.fori_loop(0, (total_rows // 4) * blocks, convolve, 0)

    def gather_terms(at, carry):
        tiles = [product[at * 8 + k] for k in range(8)]
        swapped = []
        for k in range(8):
            if (k // blocks) % 2 == 0:
                swapped.append(tiles[k + blocks])
            else:
                swapped.append(-tiles[k - blocks])
        place = pl.ds(pl.multiple_of(at * 8, 8), 8)
        mixed[place, pl.ds(0, LANES)] = jnp.sum(jnp.stack(tiles), axis=1)
        mixed[place, pl.ds(LANES, LANES)] = jnp.sum(jnp.stack(swapped), axis=1)
        return carry

    lax.fori_loop(0, total_rows * 2 * blocks // 8, gather_terms, 0)
    out[...] = dot_split(mixed[...], back_high[...], back_low[...])


def final_kernel(scaling, spread, inner_cos, inner_sin, outer_table, out):
    values = spread[...]
    stacked = jnp.concatenate([values * inner_cos[...], values * inner_sin[...]], axis=0)
    total = jnp.dot(
        outer_table[...],
        stacked,
        precision=lax.Precision.HIGHEST,
        preferred_element_type=jnp.float32,
    )
    out[...] = total * scaling


def whole_call(kernel, out_shape, scratch, count):
    return pl.pallas_call(
        kernel,
        out_shape=jax.ShapeDtypeStruct(out_shape, jnp.float32),
        in_specs=[pl.BlockSpec(memory_space=pltpu.VMEM)] * count,
        out_specs=pl.BlockSpec(memory_space=pltpu.VMEM),
        scratch_shapes=[pltpu.VMEM(shape, jnp.float32) for shape in scratch],
        compiler_params=pltpu.CompilerParams(vmem_limit_bytes=VMEM_BYTES),
    )


def body(density, row_left, col_left, row_right, col_right):
    rows_here, width = density.shape
    devices = lax.axis_size("comp") * lax.axis_size("rank")
    total_rows = rows_here * lax.axis_size("comp")
    terms = row_left.shape[0]
    groups = min(devices, width // LANES)
    term_groups = devices // groups
    blocks = width // (groups * LANES)
    device_at = lax.axis_index(AXES)
    group_at = lax.rem(device_at, groups)

    gathered = lax.all_gather(density, "comp", axis=0, tiled=True)
    rho = gathered.reshape(total_rows // 8, 8, width)

    cells = lax.broadcasted_iota(jnp.int32, (1, width), 1)
    turns = lax.rem(cells * (4 * group_at + 1), 4 * width)
    angles = turns.astype(jnp.float32) * (2.0 * math.pi / (4 * width))
    cosine, sine = jnp.cos(angles), -jnp.sin(angles)
    if term_groups > 1:
        term_at = lax.broadcasted_iota(jnp.int32, (terms, 1), 0)
        chosen = lax.div(term_at, terms // term_groups) == lax.div(device_at, groups)
        col_left = jnp.where(chosen, col_left, 0.0)
        col_right = jnp.where(chosen, col_right, 0.0)
    row_factor = jnp.broadcast_to(
        jnp.stack([row_left.T, row_right.T])[..., None], (2, total_rows, terms, LANES)
    )

    out_rows = total_rows * 2 * blocks
    sent = whole_call(
        lambda *refs: main_kernel(blocks, *refs),
        (out_rows, LANES),
        [
            (4, blocks, total_rows, terms, LANES),
            (2 * blocks, total_rows * terms, 2 * LANES),
            (2 * blocks, 3, PAD + total_rows, terms, LANES),
            (out_rows, terms, LANES),
            (out_rows, 2 * LANES),
        ],
        11,
    )(
        rho,
        col_left * cosine,
        col_left * sine,
        col_right * cosine,
        col_right * sine,
        row_factor,
        block_twiddles(blocks),
        *host_split(forward_table()),
        *host_split(inverse_table()),
    )
    spread = lax.all_to_all(sent, AXES, split_axis=0, concat_axis=0, tiled=True)
    inner_cos, inner_sin, outer_table = final_tables(devices, groups, blocks, width)
    scaling = 0.5 / (math.sqrt(total_rows * width) * width)
    result = whole_call(
        lambda *refs: final_kernel(scaling, *refs), (width // LANES, LANES), [], 4
    )(
        spread,
        jnp.asarray(inner_cos, jnp.float32),
        jnp.asarray(inner_sin, jnp.float32),
        jnp.asarray(outer_table, jnp.float32),
    )
    return result.reshape(1, width)


def solution(mesh):
    return jax.shard_map(
        body,
        mesh=mesh,
        in_specs=(P("comp", None), P(), P(), P(), P()),
        out_specs=P(AXES, None),
        check_vma=False,
    )
```

```python
import math

import jax
import jax.numpy as jnp
import numpy as np
from jax import lax
from jax.experimental import pallas as pl
from jax.experimental.pallas import tpu as pltpu
from jax.sharding import PartitionSpec as P

LANES = 128
VMEM_BYTES = 56 * 1024 * 1024
AXES = ("comp", "rank")
PAD = 4
PRODUCT_ROWS = 256


def split_parts(values):
    high = values.astype(jnp.bfloat16)
    low = (values - high.astype(jnp.float32)).astype(jnp.bfloat16)
    return high, low


def host_split(values):
    return split_parts(jnp.asarray(values, jnp.float32))


def dot_split(rows, table_high, table_low):
    high, low = split_parts(rows)
    total = jnp.dot(high, table_high, preferred_element_type=jnp.float32)
    total += jnp.dot(low, table_high, preferred_element_type=jnp.float32)
    total += jnp.dot(high, table_low, preferred_element_type=jnp.float32)
    return total


def forward_table():
    angles = 2.0 * np.pi * np.outer(np.arange(LANES), np.arange(LANES)) / LANES
    cosine, sine = np.cos(angles), np.sin(angles)
    return np.block([[cosine, -sine], [sine, cosine]])


def inverse_table():
    angles = 2.0 * np.pi * np.outer(np.arange(LANES), np.arange(LANES)) / LANES
    return np.concatenate([np.cos(angles), -np.sin(angles)], axis=0)


def block_twiddles(blocks):
    angles = 2.0 * np.pi * np.outer(np.arange(blocks), np.arange(LANES)) / (blocks * LANES)
    table = np.stack([np.cos(angles), -np.sin(angles)], axis=1)
    return jnp.asarray(
        np.broadcast_to(table[:, :, None, :], (blocks, 2, 8, LANES)), jnp.float32
    )


def final_tables(devices, groups, blocks, width):
    owner = np.arange(devices) % groups
    frequency = (owner[:, None] + groups * np.arange(blocks)[None, :]).astype(np.float64) + 0.25
    frequency = np.broadcast_to(frequency[:, None, :], (devices, 2, blocks))
    inner = 2.0 * np.pi * frequency[..., None] * np.arange(LANES) / width
    rows = devices * 2 * blocks
    inner_cos = np.cos(inner).reshape(rows, LANES)
    inner_sin = np.sin(inner).reshape(rows, LANES)
    outer_count = width // LANES
    outer = 2.0 * np.pi * frequency * LANES / width
    outer = np.arange(outer_count)[:, None] * outer.reshape(1, rows)
    is_real = np.broadcast_to(np.array([True, False])[None, :, None], (devices, 2, blocks))
    is_real = is_real.reshape(1, rows)
    with_cos = np.where(is_real, np.cos(outer), -np.sin(outer))
    with_sin = np.where(is_real, -np.sin(outer), -np.cos(outer))
    return inner_cos, inner_sin, np.concatenate([with_cos, with_sin], axis=1)


def block_fourier(reals, imags):
    count = len(reals)
    if count == 1:
        return reals, imags
    if count == 2:
        return (
            [reals[0] + reals[1], reals[0] - reals[1]],
            [imags[0] + imags[1], imags[0] - imags[1]],
        )
    even_real, odd_real = reals[0] + reals[2], reals[0] - reals[2]
    even_imag, odd_imag = imags[0] + imags[2], imags[0] - imags[2]
    pair_real, gap_real = reals[1] + reals[3], reals[1] - reals[3]
    pair_imag, gap_imag = imags[1] + imags[3], imags[1] - imags[3]
    return (
        [even_real + pair_real, odd_real + gap_imag, even_real - pair_real, odd_real - gap_imag],
        [even_imag + pair_imag, odd_imag - gap_real, even_imag - pair_imag, odd_imag + gap_real],
    )


def prepare_kernel(left, right, row_left, row_right, cosine, sine, weights, row_factor):
    for side, column in enumerate((left, right)):
        weights[2 * side] = column[...] * cosine[...]
        weights[2 * side + 1] = column[...] * sine[...]
    terms, total_rows = row_left.shape
    for side, factor in enumerate((row_left, row_right)):
        for row in range(total_rows):
            row_factor[side, row] = jnp.broadcast_to(factor[:, row : row + 1], (terms, LANES))


def main_kernel(blocks, piece_count, starts, *refs):
    pieces = refs[:piece_count]
    weights, row_factor, twiddle, table_high, table_low, back_high, back_low = refs[
        piece_count : piece_count + 7
    ]
    out, partial, rows, spectrum, product, mixed = refs[piece_count + 7 :]
    comps, parts, rows_here, part_width = pieces[0].shape
    total_rows = comps * rows_here
    inner = blocks * LANES
    part_outer = part_width // inner
    unroll = math.gcd(4, part_outer)

    def reduce_tile(index, carry):
        block = lax.rem(index, blocks)
        row_tile = lax.div(index, blocks)
        sums = (jnp.zeros((8, LANES), jnp.float32),) * 32
        for number, piece in enumerate(pieces):
            for part in range(parts):
                start = starts[number * parts + part]

                def step(at, sums, piece=piece, part=part, start=start):
                    sums = list(sums)
                    for extra in range(unroll):
                        lane = (at * unroll + extra) * inner + block * LANES
                        place = pl.ds(pl.multiple_of(start + lane, LANES), LANES)
                        factors = [weights[k, :, place] for k in range(4)]
                        place = pl.ds(pl.multiple_of(lane, LANES), LANES)
                        for row in range(8):
                            comp = row_tile * (8 // rows_here) + row // rows_here
                            value = piece[comp, part, pl.ds(row % rows_here, 1), place]
                            value = jnp.broadcast_to(value, (8, LANES))
                            for k in range(4):
                                sums[row * 4 + k] += value * factors[k]
                    return tuple(sums)

                sums = lax.fori_loop(0, part_outer // unroll, step, sums)
        for row in range(8):
            for k in range(4):
                partial[k, block, row_tile * 8 + row] = sums[row * 4 + k]
        return carry

    lax.fori_loop(0, total_rows // 8 * blocks, reduce_tile, 0)

    def butterfly(at, carry):
        for extra in range(2):
            row = at * 2 + extra
            for side in range(2):
                factor = row_factor[side, row]
                reals = [partial[2 * side, block, row] * factor for block in range(blocks)]
                imags = [partial[2 * side + 1, block, row] * factor for block in range(blocks)]
                reals, imags = block_fourier(reals, imags)
                for block in range(blocks):
                    real, imag = reals[block], imags[block]
                    if block > 0:
                        cosine, sine = twiddle[block, 0], twiddle[block, 1]
                        real, imag = real * cosine - imag * sine, real * sine + imag * cosine
                    place = pl.ds(pl.multiple_of(row * 8, 8), 8)
                    rows[block * 2 + side, place, pl.ds(0, LANES)] = real
                    rows[block * 2 + side, place, pl.ds(LANES, LANES)] = imag
        return carry

    lax.fori_loop(0, total_rows // 2, butterfly, 0)

    chunk_tiles = PRODUCT_ROWS // 8
    chunks = total_rows // chunk_tiles
    spectrum[:, :, pl.ds(0, PAD)] = jnp.zeros((2 * blocks, 3, PAD, 8, LANES), jnp.float32)

    def transform(at, carry):
        plane = lax.div(at, chunks)
        chunk = lax.rem(at, chunks)
        place = pl.ds(pl.multiple_of(chunk * PRODUCT_ROWS, PRODUCT_ROWS), PRODUCT_ROWS)
        result = dot_split(rows[plane, place, :], table_high[...], table_low[...])
        result = result.reshape(chunk_tiles, 8, 2 * LANES)
        real, imag = result[:, :, :LANES], result[:, :, LANES:]
        place = pl.ds(PAD + chunk * chunk_tiles, chunk_tiles)
        spectrum[plane, 0, place] = real
        spectrum[plane, 1, place] = imag
        spectrum[plane, 2, place] = real + imag
        return carry

    lax.fori_loop(0, 2 * blocks * chunks, transform, 0)

    def convolve(index, carry):
        block = lax.rem(index, blocks)
        out_tile = lax.div(index, blocks)

        def step(at, sums):
            sums = list(sums)
            left_base = PAD + 4 * at
            right_base = PAD + 4 * (out_tile - at)
            for part in range(3):
                left = [spectrum[2 * block, part, left_base + k] for k in range(4)]
                right = {k: spectrum[2 * block + 1, part, right_base + k] for k in range(-3, 4)}
                for row in range(4):
                    for k in range(4):
                        sums[row * 3 + part] += left[k] * right[row - k]
            return tuple(sums)

        zero = jnp.zeros((8, LANES), jnp.float32)
        sums = lax.fori_loop(0, out_tile + 1, step, (zero,) * 12)
        for row in range(4):
            both_real, both_imag, crossed = sums[row * 3 : row * 3 + 3]
            base = (out_tile * 4 + row) * 2 * blocks + block
            product[base] = both_real - both_imag
            product[base + blocks] = crossed - both_real - both_imag
        return carry

    lax.fori_loop(0, (total_rows // 4) * blocks, convolve, 0)

    def gather_terms(at, carry):
        tiles = [product[at * 8 + k] for k in range(8)]
        swapped = []
        for k in range(8):
            if (k // blocks) % 2 == 0:
                swapped.append(tiles[k + blocks])
            else:
                swapped.append(-tiles[k - blocks])
        place = pl.ds(pl.multiple_of(at * 8, 8), 8)
        mixed[place, pl.ds(0, LANES)] = jnp.sum(jnp.stack(tiles), axis=1)
        mixed[place, pl.ds(LANES, LANES)] = jnp.sum(jnp.stack(swapped), axis=1)
        return carry

    lax.fori_loop(0, total_rows * 2 * blocks // 8, gather_terms, 0)
    out[...] = dot_split(mixed[...], back_high[...], back_low[...])


def final_kernel(scaling, spread, inner_cos, inner_sin, outer_table, out):
    values = spread[...]
    stacked = jnp.concatenate([values * inner_cos[...], values * inner_sin[...]], axis=0)
    total = jnp.dot(
        outer_table[...],
        stacked,
        precision=lax.Precision.HIGHEST,
        preferred_element_type=jnp.float32,
    )
    out[...] = total * scaling


def whole_call(kernel, outs, scratch, count, scalars=0):
    return pl.pallas_call(
        kernel,
        out_shape=[jax.ShapeDtypeStruct(shape, jnp.float32) for shape in outs],
        in_specs=[pl.BlockSpec(memory_space=pltpu.SMEM)] * scalars
        + [pl.BlockSpec(memory_space=pltpu.VMEM)] * count,
        out_specs=[pl.BlockSpec(memory_space=pltpu.VMEM)] * len(outs),
        scratch_shapes=[pltpu.VMEM(shape, jnp.float32) for shape in scratch],
        compiler_params=pltpu.CompilerParams(vmem_limit_bytes=VMEM_BYTES),
    )


def gather_density(density):
    rows_here, width = density.shape
    ranks = lax.axis_size("rank")
    part = width // ranks
    mine = lax.dynamic_slice_in_dim(density, lax.axis_index("rank") * part, part, 1)
    gathered = lax.all_gather(mine, AXES, axis=0)
    pieces = gathered.reshape(lax.axis_size("comp"), ranks, rows_here, part)
    return [pieces], jnp.arange(ranks, dtype=jnp.int32) * part


def body(density, row_left, col_left, row_right, col_right):
    rows_here, width = density.shape
    devices = lax.axis_size("comp") * lax.axis_size("rank")
    total_rows = rows_here * lax.axis_size("comp")
    terms = row_left.shape[0]
    groups = min(devices, width // LANES)
    term_groups = devices // groups
    blocks = width // (groups * LANES)
    device_at = lax.axis_index(AXES)
    group_at = lax.rem(device_at, groups)

    pieces, starts = gather_density(density)

    cells = lax.broadcasted_iota(jnp.int32, (1, width), 1)
    turns = lax.rem(cells * (4 * group_at + 1), 4 * width)
    angles = turns.astype(jnp.float32) * (2.0 * math.pi / (4 * width))
    cosine, sine = jnp.cos(angles), -jnp.sin(angles)
    if term_groups > 1:
        term_at = lax.broadcasted_iota(jnp.int32, (terms, 1), 0)
        chosen = lax.div(term_at, terms // term_groups) == lax.div(device_at, groups)
        col_left = jnp.where(chosen, col_left, 0.0)
        col_right = jnp.where(chosen, col_right, 0.0)
    weights, row_factor = whole_call(
        prepare_kernel, [(4, terms, width), (2, total_rows, terms, LANES)], [], 6
    )(col_left, col_right, row_left, row_right, cosine, sine)

    out_rows = total_rows * 2 * blocks
    (sent,) = whole_call(
        lambda *refs: main_kernel(blocks, len(pieces), *refs),
        [(out_rows, LANES)],
        [
            (4, blocks, total_rows, terms, LANES),
            (2 * blocks, total_rows * terms, 2 * LANES),
            (2 * blocks, 3, PAD + total_rows, terms, LANES),
            (out_rows, terms, LANES),
            (out_rows, 2 * LANES),
        ],
        len(pieces) + 7,
        1,
    )(
        starts,
        *pieces,
        weights,
        row_factor,
        block_twiddles(blocks),
        *host_split(forward_table()),
        *host_split(inverse_table()),
    )
    spread = lax.all_to_all(sent, AXES, split_axis=0, concat_axis=0, tiled=True)
    inner_cos, inner_sin, outer_table = final_tables(devices, groups, blocks, width)
    scaling = 0.5 / (math.sqrt(total_rows * width) * width)
    (result,) = whole_call(
        lambda *refs: final_kernel(scaling, *refs), [(width // LANES, LANES)], [], 4
    )(
        spread,
        jnp.asarray(inner_cos, jnp.float32),
        jnp.asarray(inner_sin, jnp.float32),
        jnp.asarray(outer_table, jnp.float32),
    )
    return result.reshape(1, width)


def solution(mesh):
    return jax.shard_map(
        body,
        mesh=mesh,
        in_specs=(P("comp", None), P(), P(), P(), P()),
        out_specs=P(AXES, None),
        check_vma=False,
    )
```

```python
import math

import jax
import jax.numpy as jnp
import numpy as np
from jax import lax
from jax.experimental import pallas as pl
from jax.experimental.pallas import tpu as pltpu
from jax.sharding import PartitionSpec as P

LANES = 128
VMEM_BYTES = 56 * 1024 * 1024
AXES = ("comp", "rank")
PAD = 4
PRODUCT_ROWS = 256


def split_parts(values):
    high = values.astype(jnp.bfloat16)
    low = (values - high.astype(jnp.float32)).astype(jnp.bfloat16)
    return high, low


def host_split(values):
    return split_parts(jnp.asarray(values, jnp.float32))


def dot_split(rows, table_high, table_low):
    high, low = split_parts(rows)
    total = jnp.dot(high, table_high, preferred_element_type=jnp.float32)
    total += jnp.dot(low, table_high, preferred_element_type=jnp.float32)
    total += jnp.dot(high, table_low, preferred_element_type=jnp.float32)
    return total


def forward_table():
    angles = 2.0 * np.pi * np.outer(np.arange(LANES), np.arange(LANES)) / LANES
    cosine, sine = np.cos(angles), np.sin(angles)
    return np.block([[cosine, -sine], [sine, cosine]])


def inverse_table():
    angles = 2.0 * np.pi * np.outer(np.arange(LANES), np.arange(LANES)) / LANES
    return np.concatenate([np.cos(angles), -np.sin(angles)], axis=0)


def block_twiddles(blocks):
    angles = 2.0 * np.pi * np.outer(np.arange(blocks), np.arange(LANES)) / (blocks * LANES)
    table = np.stack([np.cos(angles), -np.sin(angles)], axis=1)
    return jnp.asarray(
        np.broadcast_to(table[:, :, None, :], (blocks, 2, 8, LANES)), jnp.float32
    )


def final_tables(devices, groups, blocks, width):
    owner = np.arange(devices) % groups
    frequency = (owner[:, None] + groups * np.arange(blocks)[None, :]).astype(np.float64) + 0.25
    frequency = np.broadcast_to(frequency[:, None, :], (devices, 2, blocks))
    inner = 2.0 * np.pi * frequency[..., None] * np.arange(LANES) / width
    rows = devices * 2 * blocks
    inner_cos = np.cos(inner).reshape(rows, LANES)
    inner_sin = np.sin(inner).reshape(rows, LANES)
    outer_count = width // LANES
    outer = 2.0 * np.pi * frequency * LANES / width
    outer = np.arange(outer_count)[:, None] * outer.reshape(1, rows)
    is_real = np.broadcast_to(np.array([True, False])[None, :, None], (devices, 2, blocks))
    is_real = is_real.reshape(1, rows)
    with_cos = np.where(is_real, np.cos(outer), -np.sin(outer))
    with_sin = np.where(is_real, -np.sin(outer), -np.cos(outer))
    return inner_cos, inner_sin, np.concatenate([with_cos, with_sin], axis=1)


def block_fourier(reals, imags):
    count = len(reals)
    if count == 1:
        return reals, imags
    if count == 2:
        return (
            [reals[0] + reals[1], reals[0] - reals[1]],
            [imags[0] + imags[1], imags[0] - imags[1]],
        )
    even_real, odd_real = reals[0] + reals[2], reals[0] - reals[2]
    even_imag, odd_imag = imags[0] + imags[2], imags[0] - imags[2]
    pair_real, gap_real = reals[1] + reals[3], reals[1] - reals[3]
    pair_imag, gap_imag = imags[1] + imags[3], imags[1] - imags[3]
    return (
        [even_real + pair_real, odd_real + gap_imag, even_real - pair_real, odd_real - gap_imag],
        [even_imag + pair_imag, odd_imag - gap_real, even_imag - pair_imag, odd_imag + gap_real],
    )


def prepare_kernel(left, right, row_left, row_right, cosine, sine, weights, row_factor):
    for side, column in enumerate((left, right)):
        weights[2 * side] = column[...] * cosine[...]
        weights[2 * side + 1] = column[...] * sine[...]
    terms, total_rows = row_left.shape
    for side, factor in enumerate((row_left, row_right)):
        for row in range(total_rows):
            row_factor[side, row] = jnp.broadcast_to(factor[:, row : row + 1], (terms, LANES))


def reduce_rows(blocks, terms_here, fetch, starts, span, weights, partial, row_at):
    inner = blocks * LANES
    outer = span // inner
    unroll = math.gcd(4, outer)

    def reduce_block(block, carry):
        sums = (jnp.zeros((terms_here, LANES), jnp.float32),) * 32
        for part, start in enumerate(starts):

            def step(at, sums, part=part, start=start):
                sums = list(sums)
                for extra in range(unroll):
                    lane = (at * unroll + extra) * inner + block * LANES
                    place = pl.ds(pl.multiple_of(start + lane, LANES), LANES)
                    factors = [weights[k, :, place] for k in range(4)]
                    for row in range(8):
                        value = jnp.broadcast_to(fetch(part, row, lane), (terms_here, LANES))
                        for k in range(4):
                            sums[row * 4 + k] += value * factors[k]
                return tuple(sums)

            sums = lax.fori_loop(0, outer // unroll, step, sums)
        for row in range(8):
            for k in range(4):
                partial[k, block, row_at(row)] = sums[row * 4 + k]
        return carry

    lax.fori_loop(0, blocks, reduce_block, 0)


def reduce_gathered(blocks, pieces, weights, partial):
    comps, parts, rows_here, span = pieces.shape
    terms = weights.shape[1]

    def reduce_tile(tile, carry):
        def fetch(part, row, lane):
            comp = tile * (8 // rows_here) + row // rows_here
            place = pl.ds(pl.multiple_of(lane, LANES), LANES)
            return pieces[comp, part, pl.ds(row % rows_here, 1), place]

        starts = [part * span for part in range(parts)]
        reduce_rows(
            blocks, terms, fetch, starts, span, weights, partial, lambda row: tile * 8 + row
        )
        return carry

    lax.fori_loop(0, comps * rows_here // 8, reduce_tile, 0)


def reduce_pieces(blocks, own, near, far, places, weights, partial):
    rows_here = own.shape[0]
    span = own.shape[1] // 2
    terms = weights.shape[1]
    starts = [places[0], places[1]]
    sources = [None] + list(zip(near, far))
    per_tile = 8 // rows_here
    for first in range(0, len(sources), per_tile):

        def fetch(part, row, lane, first=first):
            source = first + row // rows_here
            if source == 0:
                ref, lane = own, starts[part] + lane
            else:
                ref = sources[source][part]
            place = pl.ds(pl.multiple_of(lane, LANES), LANES)
            return ref[pl.ds(row % rows_here, 1), place]

        def row_at(row, first=first):
            return places[2 + first + row // rows_here] * rows_here + row % rows_here

        reduce_rows(blocks, terms, fetch, starts, span, weights, partial, row_at)


def main_kernel(blocks, total_rows, piece_count, places, *refs):
    pieces = refs[:piece_count]
    weights, row_factor, twiddle, table_high, table_low, back_high, back_low = refs[
        piece_count : piece_count + 7
    ]
    out, partial, rows, spectrum, product, mixed = refs[piece_count + 7 :]
    if piece_count == 1:
        reduce_gathered(blocks, pieces[0], weights, partial)
    else:
        half = (piece_count + 1) // 2
        reduce_pieces(blocks, pieces[0], pieces[1:half], pieces[half:], places, weights, partial)

    def butterfly(at, carry):
        for extra in range(2):
            row = at * 2 + extra
            for side in range(2):
                factor = row_factor[side, row]
                reals = [partial[2 * side, block, row] * factor for block in range(blocks)]
                imags = [partial[2 * side + 1, block, row] * factor for block in range(blocks)]
                reals, imags = block_fourier(reals, imags)
                for block in range(blocks):
                    real, imag = reals[block], imags[block]
                    if block > 0:
                        cosine, sine = twiddle[block, 0], twiddle[block, 1]
                        real, imag = real * cosine - imag * sine, real * sine + imag * cosine
                    place = pl.ds(pl.multiple_of(row * 8, 8), 8)
                    rows[block * 2 + side, place, pl.ds(0, LANES)] = real
                    rows[block * 2 + side, place, pl.ds(LANES, LANES)] = imag
        return carry

    lax.fori_loop(0, total_rows // 2, butterfly, 0)

    chunk_tiles = PRODUCT_ROWS // 8
    chunks = total_rows // chunk_tiles
    spectrum[:, :, pl.ds(0, PAD)] = jnp.zeros((2 * blocks, 3, PAD, 8, LANES), jnp.float32)

    def transform(at, carry):
        plane = lax.div(at, chunks)
        chunk = lax.rem(at, chunks)
        place = pl.ds(pl.multiple_of(chunk * PRODUCT_ROWS, PRODUCT_ROWS), PRODUCT_ROWS)
        result = dot_split(rows[plane, place, :], table_high[...], table_low[...])
        result = result.reshape(chunk_tiles, 8, 2 * LANES)
        real, imag = result[:, :, :LANES], result[:, :, LANES:]
        place = pl.ds(PAD + chunk * chunk_tiles, chunk_tiles)
        spectrum[plane, 0, place] = real
        spectrum[plane, 1, place] = imag
        spectrum[plane, 2, place] = real + imag
        return carry

    lax.fori_loop(0, 2 * blocks * chunks, transform, 0)

    def convolve(index, carry):
        block = lax.rem(index, blocks)
        out_tile = lax.div(index, blocks)

        def step(at, sums):
            sums = list(sums)
            left_base = PAD + 4 * at
            right_base = PAD + 4 * (out_tile - at)
            for part in range(3):
                left = [spectrum[2 * block, part, left_base + k] for k in range(4)]
                right = {k: spectrum[2 * block + 1, part, right_base + k] for k in range(-3, 4)}
                for row in range(4):
                    for k in range(4):
                        sums[row * 3 + part] += left[k] * right[row - k]
            return tuple(sums)

        zero = jnp.zeros((8, LANES), jnp.float32)
        sums = lax.fori_loop(0, out_tile + 1, step, (zero,) * 12)
        for row in range(4):
            both_real, both_imag, crossed = sums[row * 3 : row * 3 + 3]
            base = (out_tile * 4 + row) * 2 * blocks + block
            product[base] = both_real - both_imag
            product[base + blocks] = crossed - both_real - both_imag
        return carry

    lax.fori_loop(0, (total_rows // 4) * blocks, convolve, 0)

    def gather_terms(at, carry):
        tiles = [product[at * 8 + k] for k in range(8)]
        swapped = []
        for k in range(8):
            if (k // blocks) % 2 == 0:
                swapped.append(tiles[k + blocks])
            else:
                swapped.append(-tiles[k - blocks])
        place = pl.ds(pl.multiple_of(at * 8, 8), 8)
        mixed[place, pl.ds(0, LANES)] = jnp.sum(jnp.stack(tiles), axis=1)
        mixed[place, pl.ds(LANES, LANES)] = jnp.sum(jnp.stack(swapped), axis=1)
        return carry

    lax.fori_loop(0, total_rows * 2 * blocks // 8, gather_terms, 0)
    out[...] = dot_split(mixed[...], back_high[...], back_low[...])


def final_kernel(scaling, spread, inner_cos, inner_sin, outer_table, out):
    values = spread[...]
    stacked = jnp.concatenate([values * inner_cos[...], values * inner_sin[...]], axis=0)
    total = jnp.dot(
        outer_table[...],
        stacked,
        precision=lax.Precision.HIGHEST,
        preferred_element_type=jnp.float32,
    )
    out[...] = total * scaling


def whole_call(kernel, outs, scratch, count, scalars=0):
    return pl.pallas_call(
        kernel,
        out_shape=[jax.ShapeDtypeStruct(shape, jnp.float32) for shape in outs],
        in_specs=[pl.BlockSpec(memory_space=pltpu.SMEM)] * scalars
        + [pl.BlockSpec(memory_space=pltpu.VMEM)] * count,
        out_specs=[pl.BlockSpec(memory_space=pltpu.VMEM)] * len(outs),
        scratch_shapes=[pltpu.VMEM(shape, jnp.float32) for shape in scratch],
        compiler_params=pltpu.CompilerParams(vmem_limit_bytes=VMEM_BYTES),
    )


def gather_density(density):
    rows_here, width = density.shape
    comps, ranks = lax.axis_size("comp"), lax.axis_size("rank")
    comp_at, rank_at = lax.axis_index("comp"), lax.axis_index("rank")
    if comps > 8:
        part = width // ranks
        mine = lax.dynamic_slice_in_dim(density, rank_at * part, part, 1)
        gathered = lax.all_gather(mine, AXES, axis=0)
        return [gathered.reshape(comps, ranks, rows_here, part)], jnp.zeros((2,), jnp.int32)
    half = width // 2
    core = lax.rem(rank_at, 2)
    lines = comps // 2
    line_at, side_at = lax.div(comp_at, 2), lax.rem(comp_at, 2)
    mine = lax.dynamic_slice_in_dim(density, core * half, half, 1)

    def along(block, step):
        pairs = [(c, ((c // 2 + step) % lines) * 2 + c % 2) for c in range(comps)]
        return lax.ppermute(block, "comp", pairs)

    def across(block):
        return lax.ppermute(block, "comp", [(c, c ^ 1) for c in range(comps)])

    def beside(block):
        return lax.ppermute(block, "rank", [(r, r ^ 1) for r in range(ranks)])

    same_side = [mine] + [along(mine, step) for step in range(1, lines)]
    other_side = [across(block) for block in same_side]
    near, places = [], [core * half, (1 - core) * half]
    for step in range(lines):
        line = lax.rem(line_at + lines - step, lines)
        places += [line * 2 + side_at, line * 2 + 1 - side_at]
        near += ([] if step == 0 else [same_side[step]]) + [other_side[step]]
    far = [beside(block) for block in near]
    return [density, *near, *far], jnp.stack(places)


def body(density, row_left, col_left, row_right, col_right):
    rows_here, width = density.shape
    devices = lax.axis_size("comp") * lax.axis_size("rank")
    total_rows = rows_here * lax.axis_size("comp")
    terms = row_left.shape[0]
    groups = min(devices, width // LANES)
    term_groups = devices // groups
    blocks = width // (groups * LANES)
    device_at = lax.axis_index(AXES)
    group_at = lax.rem(device_at, groups)

    pieces, places = gather_density(density)

    cells = lax.broadcasted_iota(jnp.int32, (1, width), 1)
    turns = lax.rem(cells * (4 * group_at + 1), 4 * width)
    angles = turns.astype(jnp.float32) * (2.0 * math.pi / (4 * width))
    cosine, sine = jnp.cos(angles), -jnp.sin(angles)
    if term_groups > 1:
        term_at = lax.broadcasted_iota(jnp.int32, (terms, 1), 0)
        chosen = lax.div(term_at, terms // term_groups) == lax.div(device_at, groups)
        col_left = jnp.where(chosen, col_left, 0.0)
        col_right = jnp.where(chosen, col_right, 0.0)
    weights, row_factor = whole_call(
        prepare_kernel, [(4, terms, width), (2, total_rows, terms, LANES)], [], 6
    )(col_left, col_right, row_left, row_right, cosine, sine)

    out_rows = total_rows * 2 * blocks
    (sent,) = whole_call(
        lambda *refs: main_kernel(blocks, total_rows, len(pieces), *refs),
        [(out_rows, LANES)],
        [
            (4, blocks, total_rows, terms, LANES),
            (2 * blocks, total_rows * terms, 2 * LANES),
            (2 * blocks, 3, PAD + total_rows, terms, LANES),
            (out_rows, terms, LANES),
            (out_rows, 2 * LANES),
        ],
        len(pieces) + 7,
        1,
    )(
        places,
        *pieces,
        weights,
        row_factor,
        block_twiddles(blocks),
        *host_split(forward_table()),
        *host_split(inverse_table()),
    )
    spread = lax.all_to_all(sent, AXES, split_axis=0, concat_axis=0, tiled=True)
    inner_cos, inner_sin, outer_table = final_tables(devices, groups, blocks, width)
    scaling = 0.5 / (math.sqrt(total_rows * width) * width)
    (result,) = whole_call(
        lambda *refs: final_kernel(scaling, *refs), [(width // LANES, LANES)], [], 4
    )(
        spread,
        jnp.asarray(inner_cos, jnp.float32),
        jnp.asarray(inner_sin, jnp.float32),
        jnp.asarray(outer_table, jnp.float32),
    )
    return result.reshape(1, width)


def solution(mesh):
    return jax.shard_map(
        body,
        mesh=mesh,
        in_specs=(P("comp", None), P(), P(), P(), P()),
        out_specs=P(AXES, None),
        check_vma=False,
    )
```

```python
import math

import jax
import jax.numpy as jnp
import numpy as np
from jax import lax
from jax.experimental import pallas as pl
from jax.experimental.pallas import tpu as pltpu
from jax.sharding import PartitionSpec as P

LANES = 128
VMEM_BYTES = 56 * 1024 * 1024
AXES = ("comp", "rank")
PAD = 4


def split_parts(values):
    high = values.astype(jnp.bfloat16)
    low = (values - high.astype(jnp.float32)).astype(jnp.bfloat16)
    return high, low


def host_split(values):
    return split_parts(jnp.asarray(values, jnp.float32))


def dot_split(rows, table_high, table_low):
    high, low = split_parts(rows)
    total = jnp.dot(high, table_high, preferred_element_type=jnp.float32)
    total += jnp.dot(low, table_high, preferred_element_type=jnp.float32)
    total += jnp.dot(high, table_low, preferred_element_type=jnp.float32)
    return total


def forward_table():
    angles = 2.0 * np.pi * np.outer(np.arange(LANES), np.arange(LANES)) / LANES
    cosine, sine = np.cos(angles), np.sin(angles)
    return np.block([[cosine, -sine], [sine, cosine]])


def inverse_table():
    angles = 2.0 * np.pi * np.outer(np.arange(LANES), np.arange(LANES)) / LANES
    return np.concatenate([np.cos(angles), -np.sin(angles)], axis=0)


def block_twiddles(blocks):
    angles = 2.0 * np.pi * np.outer(np.arange(blocks), np.arange(LANES)) / (blocks * LANES)
    table = np.stack([np.cos(angles), -np.sin(angles)], axis=1)
    return jnp.asarray(
        np.broadcast_to(table[:, :, None, :], (blocks, 2, 8, LANES)), jnp.float32
    )


def final_tables(devices, groups, blocks, width):
    owner = np.arange(devices) % groups
    frequency = (owner[:, None] + groups * np.arange(blocks)[None, :]).astype(np.float64) + 0.25
    frequency = np.broadcast_to(frequency[:, None, :], (devices, 2, blocks))
    inner = 2.0 * np.pi * frequency[..., None] * np.arange(LANES) / width
    rows = devices * 2 * blocks
    inner_cos = np.cos(inner).reshape(rows, LANES)
    inner_sin = np.sin(inner).reshape(rows, LANES)
    outer_count = width // LANES
    outer = 2.0 * np.pi * frequency * LANES / width
    outer = np.arange(outer_count)[:, None] * outer.reshape(1, rows)
    is_real = np.broadcast_to(np.array([True, False])[None, :, None], (devices, 2, blocks))
    is_real = is_real.reshape(1, rows)
    with_cos = np.where(is_real, np.cos(outer), -np.sin(outer))
    with_sin = np.where(is_real, -np.sin(outer), -np.cos(outer))
    return inner_cos, inner_sin, np.concatenate([with_cos, with_sin], axis=1)


def block_fourier(reals, imags):
    count = len(reals)
    if count == 1:
        return reals, imags
    if count == 2:
        return (
            [reals[0] + reals[1], reals[0] - reals[1]],
            [imags[0] + imags[1], imags[0] - imags[1]],
        )
    even_real, odd_real = reals[0] + reals[2], reals[0] - reals[2]
    even_imag, odd_imag = imags[0] + imags[2], imags[0] - imags[2]
    pair_real, gap_real = reals[1] + reals[3], reals[1] - reals[3]
    pair_imag, gap_imag = imags[1] + imags[3], imags[1] - imags[3]
    return (
        [even_real + pair_real, odd_real + gap_imag, even_real - pair_real, odd_real - gap_imag],
        [even_imag + pair_imag, odd_imag - gap_real, even_imag - pair_imag, odd_imag + gap_real],
    )


def prepare_kernel(left, right, row_left, row_right, cosine, sine, weights, row_factor):
    terms, total_rows = row_left.shape

    def scale_chunk(at, carry):
        place = pl.ds(pl.multiple_of(at * LANES, LANES), LANES)
        phases = [jnp.broadcast_to(ref[pl.ds(at, 1), :], (terms, LANES)) for ref in (cosine, sine)]
        for side, column in enumerate((left, right)):
            values = column[:, place]
            for part in range(2):
                weights[2 * side + part, :, place] = values * phases[part]
        return carry

    lax.fori_loop(0, left.shape[1] // LANES, scale_chunk, 0, unroll=8)
    for side, factor in enumerate((row_left, row_right)):
        for row in range(total_rows):
            row_factor[side, row] = jnp.broadcast_to(factor[:, row : row + 1], (terms, LANES))


def reduce_rows(blocks, fetch, starts, span, weights, partial):
    terms = weights.shape[1]
    inner = blocks * LANES
    outer = span // inner
    unroll = math.gcd(4, outer)

    def reduce_block(block, carry):
        sums = (jnp.zeros((terms, LANES), jnp.float32),) * 32
        for part, start in enumerate(starts):

            def step(at, sums, part=part, start=start):
                sums = list(sums)
                for extra in range(unroll):
                    lane = (at * unroll + extra) * inner + block * LANES
                    place = pl.ds(pl.multiple_of(start + lane, LANES), LANES)
                    factors = [weights[k, :, place] for k in range(4)]
                    for row in range(8):
                        value = jnp.broadcast_to(fetch(part, row, lane), (terms, LANES))
                        for k in range(4):
                            sums[row * 4 + k] += value * factors[k]
                return tuple(sums)

            sums = lax.fori_loop(0, outer // unroll, step, sums)
        for row in range(8):
            for k in range(4):
                partial[k, block, row] = sums[row * 4 + k]
        return carry

    lax.fori_loop(0, blocks, reduce_block, 0)


def transform_rows(blocks, row_at, row_factor, twiddle, table_high, table_low, out, partial, rows):
    terms = row_factor.shape[2]

    def butterfly(row, carry):
        place = row_at(row)
        for side in range(2):
            factor = row_factor[side, place]
            reals = [partial[2 * side, block, row] * factor for block in range(blocks)]
            imags = [partial[2 * side + 1, block, row] * factor for block in range(blocks)]
            reals, imags = block_fourier(reals, imags)
            for block in range(blocks):
                real, imag = reals[block], imags[block]
                if block > 0:
                    cosine, sine = twiddle[block, 0], twiddle[block, 1]
                    real, imag = real * cosine - imag * sine, real * sine + imag * cosine
                rows[block * 2 + side, row, :, pl.ds(0, LANES)] = real
                rows[block * 2 + side, row, :, pl.ds(LANES, LANES)] = imag
        return carry

    lax.fori_loop(0, 8, butterfly, 0, unroll=2)
    flat = rows[...].reshape(2 * blocks * 8 * terms, 2 * LANES)
    result = dot_split(flat, table_high[...], table_low[...])
    result = result.reshape(2 * blocks, 8, terms, 2 * LANES)
    out[:, 0] = result[..., :LANES]
    out[:, 1] = result[..., LANES:]


def tile_kernel(blocks, first, places, *refs):
    if first:
        own, near, far = refs[:3]
        refs = refs[3:]
    else:
        near, far = refs[:2]
        refs = refs[2:]
    weights, row_factor, twiddle, table_high, table_low, out, partial, rows = refs
    rows_here = near.shape[-2]
    span = near.shape[-1]
    starts = [places[0], places[1]]
    bases = [places[2] * rows_here, places[3] * rows_here]

    def fetch(part, row, lane):
        source, row = divmod(row, rows_here)
        if first and source == 0:
            lane = starts[part] + lane
        place = pl.ds(pl.multiple_of(lane, LANES), LANES)
        if first and source == 0:
            return own[pl.ds(row, 1), place]
        ref = (near, far)[part]
        return ref[source - first, pl.ds(row, 1), place]

    def row_at(row):
        return jnp.where(row < rows_here, bases[0] + row, bases[1] + row - rows_here)

    reduce_rows(blocks, fetch, starts, span, weights, partial)
    transform_rows(blocks, row_at, row_factor, twiddle, table_high, table_low, out, partial, rows)


def gathered_kernel(
    blocks, pieces, weights, row_factor, twiddle, table_high, table_low, out, partial, rows
):
    parts, rows_here, span = pieces.shape[1:]

    def fetch(part, row, lane):
        place = pl.ds(pl.multiple_of(lane, LANES), LANES)
        return pieces[row // rows_here, part, pl.ds(row % rows_here, 1), place]

    starts = [part * span for part in range(parts)]
    reduce_rows(blocks, fetch, starts, span, weights, partial)
    transform_rows(
        blocks,
        lambda row: row,
        row_factor,
        twiddle,
        table_high,
        table_low,
        out.at[0],
        partial,
        rows,
    )


def convolve_kernel(blocks, rows_here, tile_count, places, *refs):
    tiles = refs[:tile_count]
    back_high, back_low, out, spectrum, product, mixed = refs[tile_count:]
    total_rows = spectrum.shape[2] - PAD
    terms = spectrum.shape[3]
    spectrum[:, :, pl.ds(0, PAD)] = jnp.zeros((2 * blocks, 3, PAD, terms, LANES), jnp.float32)

    def collect(plane, carry):
        for number, tile in enumerate(tiles):
            for at in range(tile.shape[0]):
                for half in range(8 // rows_here):
                    comp = (number * tile.shape[0] + at) * (8 // rows_here) + half
                    if tile_count > 1:
                        comp = places[comp]
                    real = tile[at, plane, 0, pl.ds(half * rows_here, rows_here)]
                    imag = tile[at, plane, 1, pl.ds(half * rows_here, rows_here)]
                    place = pl.ds(PAD + comp * rows_here, rows_here)
                    spectrum[plane, 0, place] = real
                    spectrum[plane, 1, place] = imag
                    spectrum[plane, 2, place] = real + imag
        return carry

    lax.fori_loop(0, 2 * blocks, collect, 0)

    def convolve(index, carry):
        block = lax.rem(index, blocks)
        out_tile = lax.div(index, blocks)

        def step(at, sums):
            sums = list(sums)
            left_base = PAD + 4 * at
            right_base = PAD + 4 * (out_tile - at)
            for part in range(3):
                left = [spectrum[2 * block, part, left_base + k] for k in range(4)]
                right = {k: spectrum[2 * block + 1, part, right_base + k] for k in range(-3, 4)}
                for row in range(4):
                    for k in range(4):
                        sums[row * 3 + part] += left[k] * right[row - k]
            return tuple(sums)

        zero = jnp.zeros((terms, LANES), jnp.float32)
        sums = lax.fori_loop(0, out_tile + 1, step, (zero,) * 12)
        for row in range(4):
            both_real, both_imag, crossed = sums[row * 3 : row * 3 + 3]
            base = (out_tile * 4 + row) * 2 * blocks + block
            product[base] = both_real - both_imag
            product[base + blocks] = crossed - both_real - both_imag
        return carry

    lax.fori_loop(0, (total_rows // 4) * blocks, convolve, 0)

    def gather_terms(at, carry):
        tiles = [product[at * 8 + k] for k in range(8)]
        swapped = []
        for k in range(8):
            if (k // blocks) % 2 == 0:
                swapped.append(tiles[k + blocks])
            else:
                swapped.append(-tiles[k - blocks])
        place = pl.ds(pl.multiple_of(at * 8, 8), 8)
        mixed[place, pl.ds(0, LANES)] = jnp.sum(jnp.stack(tiles), axis=1)
        mixed[place, pl.ds(LANES, LANES)] = jnp.sum(jnp.stack(swapped), axis=1)
        return carry

    lax.fori_loop(0, total_rows * 2 * blocks // 8, gather_terms, 0)
    out[...] = dot_split(mixed[...], back_high[...], back_low[...])


def final_kernel(scaling, spread, inner_cos, inner_sin, outer_table, out):
    values = spread[...]
    stacked = jnp.concatenate([values * inner_cos[...], values * inner_sin[...]], axis=0)
    total = jnp.dot(
        outer_table[...],
        stacked,
        precision=lax.Precision.HIGHEST,
        preferred_element_type=jnp.float32,
    )
    out[...] = total * scaling


def whole_call(kernel, outs, scratch, count, scalars=0):
    return pl.pallas_call(
        kernel,
        out_shape=[jax.ShapeDtypeStruct(shape, jnp.float32) for shape in outs],
        in_specs=[pl.BlockSpec(memory_space=pltpu.SMEM)] * scalars
        + [pl.BlockSpec(memory_space=pltpu.VMEM)] * count,
        out_specs=[pl.BlockSpec(memory_space=pltpu.VMEM)] * len(outs),
        scratch_shapes=[pltpu.VMEM(shape, jnp.float32) for shape in scratch],
        compiler_params=pltpu.CompilerParams(vmem_limit_bytes=VMEM_BYTES),
    )


def exchange_pieces(density):
    rows_here, width = density.shape
    comps, ranks = lax.axis_size("comp"), lax.axis_size("rank")
    comp_at, core = lax.axis_index("comp"), lax.rem(lax.axis_index("rank"), 2)
    half = width // 2
    lines = comps // 2
    line_at, side_at = lax.div(comp_at, 2), lax.rem(comp_at, 2)
    mine = lax.dynamic_slice_in_dim(density, core * half, half, 1)

    def along(block, step):
        pairs = [(c, ((c // 2 + step) % lines) * 2 + c % 2) for c in range(comps)]
        return lax.ppermute(block, "comp", pairs)

    def across(block):
        return lax.ppermute(block, "comp", [(c, c ^ 1) for c in range(comps)])

    def beside(block):
        return lax.ppermute(block, "rank", [(r, r ^ 1) for r in range(ranks)])

    same_side = [mine] + [along(mine, step) for step in range(1, lines)]
    other_side = [across(block) for block in same_side]
    sources, places = [], []
    for step in range(lines):
        line = lax.rem(line_at + lines - step, lines)
        places.append((line * 2 + side_at, line * 2 + 1 - side_at))
        if step == 0:
            near = other_side[0][None]
            sources.append((density, near, beside(near)))
        else:
            near = jnp.stack([same_side[step], other_side[step]])
            sources.append((near, beside(near)))
    return sources, places, (core * half, (1 - core) * half)


def body(density, row_left, col_left, row_right, col_right):
    rows_here, width = density.shape
    comps, ranks = lax.axis_size("comp"), lax.axis_size("rank")
    devices = comps * ranks
    total_rows = rows_here * comps
    terms = row_left.shape[0]
    groups = min(devices, width // LANES)
    term_groups = devices // groups
    blocks = width // (groups * LANES)
    device_at = lax.axis_index(AXES)
    group_at = lax.rem(device_at, groups)

    direct = comps <= 8
    if direct:
        sources, places, starts = exchange_pieces(density)
    else:
        part = width // ranks
        mine = lax.dynamic_slice_in_dim(density, lax.axis_index("rank") * part, part, 1)
        gathered = lax.all_gather(mine, AXES, axis=0).reshape(comps, ranks, rows_here, part)

    cells = lax.broadcasted_iota(jnp.int32, (width // LANES, LANES), 0) * LANES
    cells = cells + lax.broadcasted_iota(jnp.int32, (width // LANES, LANES), 1)
    turns = lax.rem(cells * (4 * group_at + 1), 4 * width)
    angles = turns.astype(jnp.float32) * (2.0 * math.pi / (4 * width))
    cosine, sine = jnp.cos(angles), -jnp.sin(angles)
    if term_groups > 1:
        term_at = lax.broadcasted_iota(jnp.int32, (terms, 1), 0)
        chosen = lax.div(term_at, terms // term_groups) == lax.div(device_at, groups)
        col_left = jnp.where(chosen, col_left, 0.0)
        col_right = jnp.where(chosen, col_right, 0.0)
    weights, row_factor = whole_call(
        prepare_kernel, [(4, terms, width), (2, total_rows, terms, LANES)], [], 6
    )(col_left, col_right, row_left, row_right, cosine, sine)

    tables = (block_twiddles(blocks), *host_split(forward_table()))
    tile_shape = (2 * blocks, 2, 8, terms, LANES)
    tile_scratch = [(4, blocks, 8, terms, LANES), (2 * blocks, 8, terms, 2 * LANES)]
    if direct:
        tiles = []
        for pieces, place in zip(sources, places):
            first = len(pieces) == 3
            (tile,) = whole_call(
                lambda *refs, first=first: tile_kernel(blocks, first, *refs),
                [tile_shape],
                tile_scratch,
                len(pieces) + 5,
                1,
            )(jnp.stack([*starts, *place]), *pieces, weights, row_factor, *tables)
            tiles.append(tile[None])
        order = jnp.stack([comp for place in places for comp in place])
    else:
        row_tiles = total_rows // 8
        whole = pl.BlockSpec(memory_space=pltpu.VMEM)
        tiles = [
            pl.pallas_call(
                lambda *refs: gathered_kernel(blocks, *refs),
                grid=(row_tiles,),
                out_shape=jax.ShapeDtypeStruct((row_tiles, *tile_shape), jnp.float32),
                in_specs=[
                    pl.BlockSpec((8 // rows_here, ranks, rows_here, part), lambda t: (t, 0, 0, 0)),
                    whole,
                    pl.BlockSpec((2, 8, terms, LANES), lambda t: (0, t, 0, 0)),
                    whole,
                    whole,
                    whole,
                ],
                out_specs=pl.BlockSpec((1, *tile_shape), lambda t: (t, 0, 0, 0, 0, 0)),
                scratch_shapes=[pltpu.VMEM(shape, jnp.float32) for shape in tile_scratch],
                compiler_params=pltpu.CompilerParams(vmem_limit_bytes=VMEM_BYTES),
            )(gathered, weights, row_factor, *tables)
        ]
        order = jnp.zeros((1,), jnp.int32)

    out_rows = total_rows * 2 * blocks
    (sent,) = whole_call(
        lambda *refs: convolve_kernel(blocks, rows_here, len(tiles), *refs),
        [(out_rows, LANES)],
        [
            (2 * blocks, 3, PAD + total_rows, terms, LANES),
            (out_rows, terms, LANES),
            (out_rows, 2 * LANES),
        ],
        len(tiles) + 2,
        1,
    )(order, *tiles, *host_split(inverse_table()))
    spread = lax.all_to_all(sent, AXES, split_axis=0, concat_axis=0, tiled=True)
    inner_cos, inner_sin, outer_table = final_tables(devices, groups, blocks, width)
    scaling = 0.5 / (math.sqrt(total_rows * width) * width)
    (result,) = whole_call(
        lambda *refs: final_kernel(scaling, *refs), [(width // LANES, LANES)], [], 4
    )(
        spread,
        jnp.asarray(inner_cos, jnp.float32),
        jnp.asarray(inner_sin, jnp.float32),
        jnp.asarray(outer_table, jnp.float32),
    )
    return result.reshape(1, width)


def solution(mesh):
    return jax.shard_map(
        body,
        mesh=mesh,
        in_specs=(P("comp", None), P(), P(), P(), P()),
        out_specs=P(AXES, None),
        check_vma=False,
    )
```

```python
import math

import jax
import jax.numpy as jnp
import numpy as np
from jax import lax
from jax.experimental import pallas as pl
from jax.experimental.pallas import tpu as pltpu
from jax.sharding import PartitionSpec as P

LANES = 128
VMEM_BYTES = 56 * 1024 * 1024
AXES = ("comp", "rank")
PAD = 4


def split_parts(values):
    high = values.astype(jnp.bfloat16)
    low = (values - high.astype(jnp.float32)).astype(jnp.bfloat16)
    return high, low


def host_split(values):
    return split_parts(jnp.asarray(values, jnp.float32))


def dot_split(rows, table_high, table_low):
    high, low = split_parts(rows)
    total = jnp.dot(high, table_high, preferred_element_type=jnp.float32)
    total += jnp.dot(low, table_high, preferred_element_type=jnp.float32)
    total += jnp.dot(high, table_low, preferred_element_type=jnp.float32)
    return total


def forward_table():
    angles = 2.0 * np.pi * np.outer(np.arange(LANES), np.arange(LANES)) / LANES
    cosine, sine = np.cos(angles), np.sin(angles)
    return np.block([[cosine, -sine], [sine, cosine]])


def inverse_table():
    angles = 2.0 * np.pi * np.outer(np.arange(LANES), np.arange(LANES)) / LANES
    return np.concatenate([np.cos(angles), -np.sin(angles)], axis=0)


def block_twiddles(blocks):
    angles = 2.0 * np.pi * np.outer(np.arange(blocks), np.arange(LANES)) / (blocks * LANES)
    table = np.stack([np.cos(angles), -np.sin(angles)], axis=1)
    return jnp.asarray(
        np.broadcast_to(table[:, :, None, :], (blocks, 2, 8, LANES)), jnp.float32
    )


def final_tables(devices, groups, blocks, width):
    owner = np.arange(devices) % groups
    frequency = (owner[:, None] + groups * np.arange(blocks)[None, :]).astype(np.float64) + 0.25
    frequency = np.broadcast_to(frequency[:, None, :], (devices, 2, blocks))
    inner = 2.0 * np.pi * frequency[..., None] * np.arange(LANES) / width
    rows = devices * 2 * blocks
    inner_cos = np.cos(inner).reshape(rows, LANES)
    inner_sin = np.sin(inner).reshape(rows, LANES)
    outer_count = width // LANES
    outer = 2.0 * np.pi * frequency * LANES / width
    outer = np.arange(outer_count)[:, None] * outer.reshape(1, rows)
    is_real = np.broadcast_to(np.array([True, False])[None, :, None], (devices, 2, blocks))
    is_real = is_real.reshape(1, rows)
    with_cos = np.where(is_real, np.cos(outer), -np.sin(outer))
    with_sin = np.where(is_real, -np.sin(outer), -np.cos(outer))
    return inner_cos, inner_sin, np.concatenate([with_cos, with_sin], axis=1)


def block_fourier(reals, imags):
    count = len(reals)
    if count == 1:
        return reals, imags
    if count == 2:
        return (
            [reals[0] + reals[1], reals[0] - reals[1]],
            [imags[0] + imags[1], imags[0] - imags[1]],
        )
    even_real, odd_real = reals[0] + reals[2], reals[0] - reals[2]
    even_imag, odd_imag = imags[0] + imags[2], imags[0] - imags[2]
    pair_real, gap_real = reals[1] + reals[3], reals[1] - reals[3]
    pair_imag, gap_imag = imags[1] + imags[3], imags[1] - imags[3]
    return (
        [even_real + pair_real, odd_real + gap_imag, even_real - pair_real, odd_real - gap_imag],
        [even_imag + pair_imag, odd_imag - gap_real, even_imag - pair_imag, odd_imag + gap_real],
    )


def reduce_rows(blocks, rows, fetch, starts, span, columns, phases, partial):
    terms = columns[0].shape[0]
    inner = blocks * LANES
    outer = span // inner
    unroll = math.gcd(4, outer)

    def reduce_block(block, carry):
        for first in range(0, rows, 8):
            sums = (jnp.zeros((terms, LANES), jnp.float32),) * 32
            for part, start in enumerate(starts):

                def step(at, sums, first=first, part=part, start=start):
                    sums = list(sums)
                    for extra in range(unroll):
                        lane = (at * unroll + extra) * inner + block * LANES
                        place = pl.ds(pl.multiple_of(start + lane, LANES), LANES)
                        turn = lax.div(start + lane, LANES)
                        factors = [
                            column[:, place]
                            * jnp.broadcast_to(phase[pl.ds(turn, 1), :], (terms, LANES))
                            for column in columns
                            for phase in phases
                        ]
                        for row in range(8):
                            value = fetch(part, first + row, lane)
                            value = jnp.broadcast_to(value, (terms, LANES))
                            for k in range(4):
                                sums[row * 4 + k] += value * factors[k]
                    return tuple(sums)

                sums = lax.fori_loop(0, outer // unroll, step, sums)
            for row in range(8):
                for k in range(4):
                    partial[k, block, first + row] = sums[row * 4 + k]
        return carry

    lax.fori_loop(0, blocks, reduce_block, 0)


def transform_rows(blocks, rows, row_at, row_factors, twiddle, tables, out, partial, high, low):
    terms, total_rows = row_factors[0].shape
    lanes = lax.broadcasted_iota(jnp.int32, (terms, total_rows), 1)

    def butterfly(row, side):
        picked = jnp.where(lanes == row_at(row), row_factors[side][...], 0.0)
        factor = jnp.sum(picked, axis=1, keepdims=True)
        factor = jnp.broadcast_to(factor, (terms, LANES))
        reals = [partial[2 * side, block, row] * factor for block in range(blocks)]
        imags = [partial[2 * side + 1, block, row] * factor for block in range(blocks)]
        reals, imags = block_fourier(reals, imags)
        for block in range(1, blocks):
            real, imag = reals[block], imags[block]
            cosine, sine = twiddle[block, 0], twiddle[block, 1]
            reals[block] = real * cosine - imag * sine
            imags[block] = real * sine + imag * cosine
        return reals, imags

    def butterfly_pair(pair, carry):
        for side in range(2):
            both = [butterfly(pair * 2 + extra, side) for extra in range(2)]
            for block in range(blocks):
                base = ((block * 2 + side) * rows + pair * 2) * terms
                place = pl.ds(pl.multiple_of(base, 16), 2 * terms)
                for part in range(2):
                    values = jnp.concatenate([both[0][part][block], both[1][part][block]], axis=0)
                    lane = pl.ds(part * LANES, LANES)
                    high[place, lane], low[place, lane] = split_parts(values)
        return carry

    lax.fori_loop(0, rows // 2, butterfly_pair, 0)
    table_high, table_low = tables
    planes = 2 * blocks
    step = planes * rows * terms
    while step > 512:
        step //= 2
    plane_step = step // (rows * terms)

    def transform(at, carry):
        place = pl.ds(pl.multiple_of(at * step, 16), step)
        total = jnp.dot(high[place, :], table_high[...], preferred_element_type=jnp.float32)
        total += jnp.dot(low[place, :], table_high[...], preferred_element_type=jnp.float32)
        total += jnp.dot(high[place, :], table_low[...], preferred_element_type=jnp.float32)
        total = total.reshape(plane_step, rows, terms, 2 * LANES)
        place = pl.ds(at * plane_step, plane_step)
        out[place, 0] = total[..., :LANES]
        out[place, 1] = total[..., LANES:]
        return carry

    lax.fori_loop(0, planes // plane_step, transform, 0)


def comp_of(step, flipped):
    lines = lax.axis_size("comp") // 2
    comp_at = lax.axis_index("comp")
    line = lax.rem(lax.div(comp_at, 2) + lines - step, lines)
    side = lax.rem(comp_at, 2)
    return line * 2 + (1 - side if flipped else side)


def pieces_kernel(blocks, sources, count, *refs):
    pieces, refs = refs[:count], refs[count:]
    columns, phases, row_factors = refs[0:2], refs[2:4], refs[4:6]
    twiddle, table_high, table_low, out, partial, high, low = refs[6:]
    rows_here = pieces[0].shape[-2]
    half = columns[0].shape[1] // 2
    core = lax.rem(lax.axis_index("rank"), 2)
    starts = [core * half, (1 - core) * half]
    rows = len(sources) * rows_here

    def fetch(part, row, lane):
        near, far, index, _, _ = sources[row // rows_here]
        row = pl.ds(row % rows_here, 1)
        if far is None:
            return pieces[near][row, pl.ds(pl.multiple_of(starts[part] + lane, LANES), LANES)]
        ref = pieces[far if part else near]
        return ref[index, row, pl.ds(pl.multiple_of(lane, LANES), LANES)]

    bases = [comp_of(step, flipped) * rows_here for _, _, _, step, flipped in sources]

    def row_at(row):
        place = bases[0] + row
        for number in range(1, len(sources)):
            first = number * rows_here
            place = jnp.where(row >= first, bases[number] + row - first, place)
        return place

    reduce_rows(blocks, rows, fetch, starts, half, columns, phases, partial)
    tables = (table_high, table_low)
    transform_rows(
        blocks, rows, row_at, row_factors, twiddle, tables, out, partial, high, low
    )


def gathered_kernel(blocks, pieces, *refs):
    columns, phases, row_factors = refs[0:2], refs[2:4], refs[4:6]
    twiddle, table_high, table_low, out, partial, high, low = refs[6:]
    parts, rows_here, span = pieces.shape[1:]

    def fetch(part, row, lane):
        place = pl.ds(pl.multiple_of(lane, LANES), LANES)
        return pieces[row // rows_here, part, pl.ds(row % rows_here, 1), place]

    base = pl.program_id(0) * 8
    starts = [part * span for part in range(parts)]
    reduce_rows(blocks, 8, fetch, starts, span, columns, phases, partial)
    transform_rows(
        blocks,
        8,
        lambda row: base + row,
        row_factors,
        twiddle,
        (table_high, table_low),
        out.at[0],
        partial,
        high,
        low,
    )


def pass_kernel(value, earlier, out):
    del value, earlier, out


def after(value, earlier):
    anywhere = pl.BlockSpec(memory_space=pl.ANY)
    return pl.pallas_call(
        pass_kernel,
        out_shape=jax.ShapeDtypeStruct(value.shape, value.dtype),
        in_specs=[anywhere, anywhere],
        out_specs=anywhere,
        input_output_aliases={0: 0},
    )(value, earlier)


def convolve_kernel(blocks, rows_here, layout, tile_count, *refs):
    tiles = refs[:tile_count]
    back_high, back_low, out, spectrum, product, mixed = refs[tile_count:]
    total_rows = spectrum.shape[2] - PAD
    terms = spectrum.shape[3]
    spectrum[:, :, pl.ds(0, PAD)] = jnp.zeros((2 * blocks, 3, PAD, terms, LANES), jnp.float32)
    moves = []
    for number, tile in enumerate(tiles):
        for at in range(tile.shape[0]):
            for first in range(0, tile.shape[3], rows_here):
                moves.append((tile, at, first))
    comps = [comp_of(*layout[k]) if layout else k for k in range(len(moves))]

    def collect(plane, carry):
        for (tile, at, first), comp in zip(moves, comps):
            real = tile[at, plane, 0, pl.ds(first, rows_here)]
            imag = tile[at, plane, 1, pl.ds(first, rows_here)]
            place = pl.ds(PAD + comp * rows_here, rows_here)
            spectrum[plane, 0, place] = real
            spectrum[plane, 1, place] = imag
            spectrum[plane, 2, place] = real + imag
        return carry

    lax.fori_loop(0, 2 * blocks, collect, 0)

    def step(at, sums, block, out_tile, whole):
        sums = list(sums)
        left_base = PAD + 4 * at
        right_base = PAD + 4 * (out_tile - at)
        for part in range(3):
            left = [spectrum[2 * block, part, left_base + k] for k in range(4)]
            right = {
                k: spectrum[2 * block + 1, part, right_base + k]
                for k in range(-3 if whole else 0, 4)
            }
            for row in range(4):
                for k in range(4 if whole else row + 1):
                    sums[row * 3 + part] += left[k] * right[row - k]
        return tuple(sums)

    def finish(sums, block, out_tile):
        for row in range(4):
            both_real, both_imag, crossed = sums[row * 3 : row * 3 + 3]
            base = (out_tile * 4 + row) * 2 * blocks + block
            product[base] = both_real - both_imag
            product[base + blocks] = crossed - both_real - both_imag

    zeros = (jnp.zeros((terms, LANES), jnp.float32),) * 12
    out_tiles = total_rows // 4

    def convolve_block(block, carry):
        for out_tile in range(out_tiles):
            sums = zeros
            for at in range(out_tile + 1):
                sums = step(at, sums, block, out_tile, at < out_tile)
            finish(sums, block, out_tile)
        return carry

    def convolve_tile(index, carry):
        block = lax.rem(index, blocks)
        out_tile = lax.div(index, blocks)
        sums = lax.fori_loop(
            0, out_tile + 1, lambda at, sums: step(at, sums, block, out_tile, True), zeros
        )
        finish(sums, block, out_tile)
        return carry

    if total_rows <= 32:
        lax.fori_loop(0, blocks, convolve_block, 0)
    else:
        lax.fori_loop(0, out_tiles * blocks, convolve_tile, 0)

    def gather_terms(at, carry):
        tiles = [product[at * 8 + k] for k in range(8)]
        summed = jnp.sum(jnp.stack(tiles), axis=1)
        if blocks == 4:
            turned = jnp.concatenate([summed[blocks:], -summed[:blocks]], axis=0)
        else:
            swapped = [
                tiles[k + blocks] if (k // blocks) % 2 == 0 else -tiles[k - blocks]
                for k in range(8)
            ]
            turned = jnp.sum(jnp.stack(swapped), axis=1)
        place = pl.ds(pl.multiple_of(at * 8, 8), 8)
        mixed[place, pl.ds(0, LANES)] = summed
        mixed[place, pl.ds(LANES, LANES)] = turned
        return carry

    lax.fori_loop(0, total_rows * 2 * blocks // 8, gather_terms, 0, unroll=4)
    out[...] = dot_split(mixed[...], back_high[...], back_low[...])


def final_kernel(scaling, spread, inner_cos, inner_sin, outer_high, outer_low, out):
    values = spread[...]
    stacked = jnp.concatenate([values * inner_cos[...], values * inner_sin[...]], axis=0)
    high, low = split_parts(stacked)
    total = jnp.dot(outer_high[...], high, preferred_element_type=jnp.float32)
    total += jnp.dot(outer_high[...], low, preferred_element_type=jnp.float32)
    total += jnp.dot(outer_low[...], high, preferred_element_type=jnp.float32)
    out[...] = total * scaling


def whole_call(kernel, out_shape, scratch, count):
    return pl.pallas_call(
        kernel,
        out_shape=jax.ShapeDtypeStruct(out_shape, jnp.float32),
        in_specs=[pl.BlockSpec(memory_space=pltpu.VMEM)] * count,
        out_specs=pl.BlockSpec(memory_space=pltpu.VMEM),
        scratch_shapes=[pltpu.VMEM(*shape) for shape in scratch],
        compiler_params=pltpu.CompilerParams(vmem_limit_bytes=VMEM_BYTES),
    )


def row_scratch(blocks, rows, terms):
    return [
        ((4, blocks, rows, terms, LANES), jnp.float32),
        ((2 * blocks * rows * terms, 2 * LANES), jnp.bfloat16),
        ((2 * blocks * rows * terms, 2 * LANES), jnp.bfloat16),
    ]


def spectra_by_exchange(density, blocks, shared):
    rows_here, width = density.shape
    comps, ranks = lax.axis_size("comp"), lax.axis_size("rank")
    core = lax.rem(lax.axis_index("rank"), 2)
    half = width // 2
    lines = comps // 2
    terms = shared[0].shape[0]
    mine = lax.dynamic_slice_in_dim(density, core * half, half, 1)

    def along(block, step):
        pairs = [(c, ((c // 2 + step) % lines) * 2 + c % 2) for c in range(comps)]
        return lax.ppermute(block, "comp", pairs)

    def across(block):
        return lax.ppermute(block, "comp", [(c, c ^ 1) for c in range(comps)])

    def beside(block):
        return lax.ppermute(block, "rank", [(r, r ^ 1) for r in range(ranks)])

    def spectra(pieces, sources):
        rows = rows_here * len(sources)
        return whole_call(
            lambda *refs: pieces_kernel(blocks, sources, len(pieces), *refs),
            (2 * blocks, 2, rows, terms, LANES),
            row_scratch(blocks, rows, terms),
            len(pieces) + 9,
        )(*pieces, *shared)

    lined = [along(mine, step) for step in range(1, lines)]
    flipped_own = across(mine)
    line_near = jnp.stack(lined)
    near = jnp.concatenate([flipped_own[None], line_near])
    far = beside(near)
    flipped_near = across(line_near)
    ready = [(0, None, 0, 0, False), (1, 2, 0, 0, True)]
    ready += [(1, 2, step, step, False) for step in range(1, lines)]
    ahead = comps // 2
    early, late = ready[:ahead], ready[ahead:]
    first = spectra([density, near, far], early)
    flipped_near = after(flipped_near, first)
    flipped_far = beside(flipped_near)
    late = [(near - 1, far - 1, index, *rest) for near, far, index, *rest in late]
    late += [(2, 3, step - 1, step, True) for step in range(1, lines)]
    second = spectra([near, far, flipped_near, flipped_far], late)
    layout = [source[3:] for source in early + late]
    return [first[None], second[None]], layout


def spectra_by_gather(density, blocks, shared):
    rows_here, width = density.shape
    comps, ranks = lax.axis_size("comp"), lax.axis_size("rank")
    terms = shared[0].shape[0]
    total_rows = rows_here * comps
    part = width // ranks
    mine = lax.dynamic_slice_in_dim(density, lax.axis_index("rank") * part, part, 1)
    gathered = lax.all_gather(mine, AXES, axis=0).reshape(comps, ranks, rows_here, part)
    tile_shape = (2 * blocks, 2, 8, terms, LANES)
    spectra = pl.pallas_call(
        lambda *refs: gathered_kernel(blocks, *refs),
        grid=(total_rows // 8,),
        out_shape=jax.ShapeDtypeStruct((total_rows // 8, *tile_shape), jnp.float32),
        in_specs=[pl.BlockSpec((8 // rows_here, ranks, rows_here, part), lambda t: (t, 0, 0, 0))]
        + [pl.BlockSpec(memory_space=pltpu.VMEM)] * 9,
        out_specs=pl.BlockSpec((1, *tile_shape), lambda t: (t, 0, 0, 0, 0, 0)),
        scratch_shapes=[pltpu.VMEM(*shape) for shape in row_scratch(blocks, 8, terms)],
        compiler_params=pltpu.CompilerParams(vmem_limit_bytes=VMEM_BYTES),
    )(gathered, *shared)
    return [spectra], None


def body(density, row_left, col_left, row_right, col_right):
    rows_here, width = density.shape
    comps = lax.axis_size("comp")
    devices = comps * lax.axis_size("rank")
    total_rows = rows_here * comps
    terms = row_left.shape[0]
    groups = min(devices, width // LANES)
    term_groups = devices // groups
    blocks = width // (groups * LANES)
    device_at = lax.axis_index(AXES)
    group_at = lax.rem(device_at, groups)

    cells = lax.broadcasted_iota(jnp.int32, (width // LANES, LANES), 0) * LANES
    cells = cells + lax.broadcasted_iota(jnp.int32, (width // LANES, LANES), 1)
    turns = lax.rem(cells * (4 * group_at + 1), 4 * width)
    angles = turns.astype(jnp.float32) * (2.0 * math.pi / (4 * width))
    if term_groups > 1:
        term_at = lax.broadcasted_iota(jnp.int32, (terms, 1), 0)
        chosen = lax.div(term_at, terms // term_groups) == lax.div(device_at, groups)
        col_left = jnp.where(chosen, col_left, 0.0)
        col_right = jnp.where(chosen, col_right, 0.0)
    shared = (
        col_left,
        col_right,
        jnp.cos(angles),
        -jnp.sin(angles),
        row_left,
        row_right,
        block_twiddles(blocks),
        *host_split(forward_table()),
    )
    if comps <= 8:
        tiles, layout = spectra_by_exchange(density, blocks, shared)
    else:
        tiles, layout = spectra_by_gather(density, blocks, shared)

    out_rows = total_rows * 2 * blocks
    sent = whole_call(
        lambda *refs: convolve_kernel(blocks, rows_here, layout, len(tiles), *refs),
        (out_rows, LANES),
        [
            ((2 * blocks, 3, PAD + total_rows, terms, LANES), jnp.float32),
            ((out_rows, terms, LANES), jnp.float32),
            ((out_rows, 2 * LANES), jnp.float32),
        ],
        len(tiles) + 2,
    )(*tiles, *host_split(inverse_table()))
    spread = lax.all_to_all(sent, AXES, split_axis=0, concat_axis=0, tiled=True)
    inner_cos, inner_sin, outer_table = final_tables(devices, groups, blocks, width)
    scaling = 0.5 / (math.sqrt(total_rows * width) * width)
    result = whole_call(
        lambda *refs: final_kernel(scaling, *refs), (width // LANES, LANES), [], 5
    )(
        spread,
        jnp.asarray(inner_cos, jnp.float32),
        jnp.asarray(inner_sin, jnp.float32),
        *host_split(outer_table),
    )
    return result.reshape(1, width)


def solution(mesh):
    return jax.shard_map(
        body,
        mesh=mesh,
        in_specs=(P("comp", None), P(), P(), P(), P()),
        out_specs=P(AXES, None),
        check_vma=False,
    )
```

```python
import math

import jax
import jax.numpy as jnp
import numpy as np
from jax import lax
from jax.experimental import pallas as pl
from jax.experimental.pallas import tpu as pltpu
from jax.sharding import PartitionSpec as P

LANES = 128
VMEM_BYTES = 28 * 1024 * 1024
AXES = ("comp", "rank")
PAD = 4


def split_parts(values):
    high = values.astype(jnp.bfloat16)
    low = (values - high.astype(jnp.float32)).astype(jnp.bfloat16)
    return high, low


def split_rows(table):
    high, low = split_parts(jnp.asarray(table, jnp.float32))
    return jnp.concatenate([high, high, low], axis=0)


def split_columns(table):
    high, low = split_parts(jnp.asarray(table, jnp.float32))
    return jnp.concatenate([high, high, low], axis=1)


def dot_split(rows, table):
    high, low = split_parts(rows)
    joined = jnp.concatenate([high, low, high], axis=1)
    return jnp.dot(joined, table, preferred_element_type=jnp.float32)


def forward_table():
    angles = 2.0 * np.pi * np.outer(np.arange(LANES), np.arange(LANES)) / LANES
    cosine, sine = np.cos(angles), np.sin(angles)
    return np.block([[cosine, -sine], [sine, cosine]])


def inverse_table():
    angles = 2.0 * np.pi * np.outer(np.arange(LANES), np.arange(LANES)) / LANES
    return np.concatenate([np.cos(angles), -np.sin(angles)], axis=0)


def block_twiddles(blocks):
    angles = 2.0 * np.pi * np.outer(np.arange(blocks), np.arange(LANES)) / (blocks * LANES)
    table = np.stack([np.cos(angles), -np.sin(angles)], axis=1)
    return jnp.asarray(
        np.broadcast_to(table[:, :, None, :], (blocks, 2, 8, LANES)), jnp.float32
    )


def final_tables(devices, groups, blocks, width):
    owner = np.arange(devices) % groups
    frequency = (owner[:, None] + groups * np.arange(blocks)[None, :]).astype(np.float64) + 0.25
    frequency = np.broadcast_to(frequency[:, None, :], (devices, 2, blocks))
    inner = 2.0 * np.pi * frequency[..., None] * np.arange(LANES) / width
    rows = devices * 2 * blocks
    inner_cos = np.cos(inner).reshape(rows, LANES)
    inner_sin = np.sin(inner).reshape(rows, LANES)
    outer_count = width // LANES
    outer = 2.0 * np.pi * frequency * LANES / width
    outer = np.arange(outer_count)[:, None] * outer.reshape(1, rows)
    is_real = np.broadcast_to(np.array([True, False])[None, :, None], (devices, 2, blocks))
    is_real = is_real.reshape(1, rows)
    with_cos = np.where(is_real, np.cos(outer), -np.sin(outer))
    with_sin = np.where(is_real, -np.sin(outer), -np.cos(outer))
    return inner_cos, inner_sin, np.concatenate([with_cos, with_sin], axis=1)


def block_fourier(reals, imags):
    count = len(reals)
    if count == 1:
        return reals, imags
    if count == 2:
        return (
            [reals[0] + reals[1], reals[0] - reals[1]],
            [imags[0] + imags[1], imags[0] - imags[1]],
        )
    even_real, odd_real = reals[0] + reals[2], reals[0] - reals[2]
    even_imag, odd_imag = imags[0] + imags[2], imags[0] - imags[2]
    pair_real, gap_real = reals[1] + reals[3], reals[1] - reals[3]
    pair_imag, gap_imag = imags[1] + imags[3], imags[1] - imags[3]
    return (
        [even_real + pair_real, odd_real + gap_imag, even_real - pair_real, odd_real - gap_imag],
        [even_imag + pair_imag, odd_imag - gap_real, even_imag - pair_imag, odd_imag + gap_real],
    )


def reduce_rows(blocks, rows, fetch, starts, span, columns, phases, partial):
    terms = columns[0].shape[0]
    inner = blocks * LANES
    outer = span // inner
    unroll = math.gcd(4, outer)

    def reduce_block(block, carry):
        for first in range(0, rows, 8):
            sums = (jnp.zeros((terms, LANES), jnp.float32),) * 32
            for part, start in enumerate(starts):

                def step(at, sums, first=first, part=part, start=start):
                    sums = list(sums)
                    for extra in range(unroll):
                        lane = (at * unroll + extra) * inner + block * LANES
                        place = pl.ds(pl.multiple_of(start + lane, LANES), LANES)
                        turn = lax.div(start + lane, LANES)
                        factors = [
                            column[:, place]
                            * jnp.broadcast_to(phase[pl.ds(turn, 1), :], (terms, LANES))
                            for column in columns
                            for phase in phases
                        ]
                        for row in range(8):
                            value = fetch(part, first + row, lane)
                            value = jnp.broadcast_to(value, (terms, LANES))
                            for k in range(4):
                                sums[row * 4 + k] += value * factors[k]
                    return tuple(sums)

                sums = lax.fori_loop(0, outer // unroll, step, sums)
            for row in range(8):
                for k in range(4):
                    partial[k, block, first + row] = sums[row * 4 + k]
        return carry

    lax.fori_loop(0, blocks, reduce_block, 0)


def transform_rows(blocks, rows, row_at, row_factors, twiddle, table, out, partial, joined):
    terms, total_rows = row_factors[0].shape
    lanes = lax.broadcasted_iota(jnp.int32, (terms, total_rows), 1)

    def butterfly(row, side):
        picked = jnp.where(lanes == row_at(row), row_factors[side][...], 0.0)
        factor = jnp.sum(picked, axis=1, keepdims=True)
        factor = jnp.broadcast_to(factor, (terms, LANES))
        reals = [partial[2 * side, block, row] * factor for block in range(blocks)]
        imags = [partial[2 * side + 1, block, row] * factor for block in range(blocks)]
        reals, imags = block_fourier(reals, imags)
        for block in range(1, blocks):
            real, imag = reals[block], imags[block]
            cosine, sine = twiddle[block, 0], twiddle[block, 1]
            reals[block] = real * cosine - imag * sine
            imags[block] = real * sine + imag * cosine
        return reals, imags

    def butterfly_pair(pair, carry):
        for side in range(2):
            both = [butterfly(pair * 2 + extra, side) for extra in range(2)]
            for block in range(blocks):
                base = ((block * 2 + side) * rows + pair * 2) * terms
                place = pl.ds(pl.multiple_of(base, 16), 2 * terms)
                for part in range(2):
                    values = jnp.concatenate([both[0][part][block], both[1][part][block]], axis=0)
                    high, low = split_parts(values)
                    for third, piece in enumerate((high, low, high)):
                        joined[place, pl.ds((third * 2 + part) * LANES, LANES)] = piece
        return carry

    lax.fori_loop(0, rows // 2, butterfly_pair, 0)
    planes = 2 * blocks
    step = planes * rows * terms
    while step > 512:
        step //= 2
    plane_step = step // (rows * terms)

    def transform(at, carry):
        place = pl.ds(pl.multiple_of(at * step, 16), step)
        total = jnp.dot(joined[place, :], table[...], preferred_element_type=jnp.float32)
        total = total.reshape(plane_step, rows, terms, 2 * LANES)
        place = pl.ds(at * plane_step, plane_step)
        out[place, 0] = total[..., :LANES]
        out[place, 1] = total[..., LANES:]
        return carry

    lax.fori_loop(0, planes // plane_step, transform, 0)


def comp_of(step, flipped):
    lines = lax.axis_size("comp") // 2
    comp_at = lax.axis_index("comp")
    line = lax.rem(lax.div(comp_at, 2) + lines - step, lines)
    side = lax.rem(comp_at, 2)
    return line * 2 + (1 - side if flipped else side)


def pieces_kernel(blocks, sources, count, *refs):
    pieces, refs = refs[:count], refs[count:]
    columns, phases, row_factors = refs[0:2], refs[2:4], refs[4:6]
    twiddle, table, out, partial, joined = refs[6:]
    rows_here = pieces[0].shape[-2]
    half = columns[0].shape[1] // 2
    core = lax.rem(lax.axis_index("rank"), 2)
    starts = [core * half, (1 - core) * half]
    rows = len(sources) * rows_here

    def fetch(part, row, lane):
        near, far, index, _, _ = sources[row // rows_here]
        row = pl.ds(row % rows_here, 1)
        if far is None:
            return pieces[near][row, pl.ds(pl.multiple_of(starts[part] + lane, LANES), LANES)]
        ref = pieces[far if part else near]
        return ref[index, row, pl.ds(pl.multiple_of(lane, LANES), LANES)]

    bases = [comp_of(step, flipped) * rows_here for _, _, _, step, flipped in sources]

    def row_at(row):
        place = bases[0] + row
        for number in range(1, len(sources)):
            first = number * rows_here
            place = jnp.where(row >= first, bases[number] + row - first, place)
        return place

    reduce_rows(blocks, rows, fetch, starts, half, columns, phases, partial)
    transform_rows(blocks, rows, row_at, row_factors, twiddle, table, out, partial, joined)


def gathered_kernel(blocks, pieces, *refs):
    columns, phases, row_factors = refs[0:2], refs[2:4], refs[4:6]
    twiddle, table, out, partial, joined = refs[6:]
    parts, rows_here, span = pieces.shape[1:]

    def fetch(part, row, lane):
        place = pl.ds(pl.multiple_of(lane, LANES), LANES)
        return pieces[row // rows_here, part, pl.ds(row % rows_here, 1), place]

    base = pl.program_id(0) * 8
    starts = [part * span for part in range(parts)]
    reduce_rows(blocks, 8, fetch, starts, span, columns, phases, partial)
    transform_rows(
        blocks,
        8,
        lambda row: base + row,
        row_factors,
        twiddle,
        table,
        out.at[0],
        partial,
        joined,
    )


def pass_kernel(value, earlier, out):
    del value, earlier, out


def after(value, earlier):
    anywhere = pl.BlockSpec(memory_space=pl.ANY)
    return pl.pallas_call(
        pass_kernel,
        out_shape=jax.ShapeDtypeStruct(value.shape, value.dtype),
        in_specs=[anywhere, anywhere],
        out_specs=anywhere,
        input_output_aliases={0: 0},
    )(*[pltpu.with_memory_space_constraint(array, pltpu.VMEM) for array in (value, earlier)])


def convolve_kernel(blocks, rows_here, layout, tile_count, *refs):
    tiles = refs[:tile_count]
    back, out, spectrum, product, mixed = refs[tile_count:]
    total_rows = spectrum.shape[2] - PAD
    terms = spectrum.shape[3]
    spectrum[:, :, pl.ds(0, PAD)] = jnp.zeros((2 * blocks, 3, PAD, terms, LANES), jnp.float32)
    moves = []
    for number, tile in enumerate(tiles):
        for at in range(tile.shape[0]):
            for first in range(0, tile.shape[3], rows_here):
                moves.append((tile, at, first))
    comps = [comp_of(*layout[k]) if layout else k for k in range(len(moves))]

    def collect(plane, carry):
        for (tile, at, first), comp in zip(moves, comps):
            real = tile[at, plane, 0, pl.ds(first, rows_here)]
            imag = tile[at, plane, 1, pl.ds(first, rows_here)]
            place = pl.ds(PAD + comp * rows_here, rows_here)
            spectrum[plane, 0, place] = real
            spectrum[plane, 1, place] = imag
            spectrum[plane, 2, place] = real + imag
        return carry

    lax.fori_loop(0, 2 * blocks, collect, 0)

    def step(at, sums, block, out_tile, whole):
        sums = list(sums)
        left_base = PAD + 4 * at
        right_base = PAD + 4 * (out_tile - at)
        for part in range(3):
            left = [spectrum[2 * block, part, left_base + k] for k in range(4)]
            right = {
                k: spectrum[2 * block + 1, part, right_base + k]
                for k in range(-3 if whole else 0, 4)
            }
            for row in range(4):
                for k in range(4 if whole else row + 1):
                    sums[row * 3 + part] += left[k] * right[row - k]
        return tuple(sums)

    def finish(sums, block, out_tile):
        for row in range(4):
            both_real, both_imag, crossed = sums[row * 3 : row * 3 + 3]
            base = (out_tile * 4 + row) * 2 * blocks + block
            product[base] = both_real - both_imag
            product[base + blocks] = crossed - both_real - both_imag

    zeros = (jnp.zeros((terms, LANES), jnp.float32),) * 12
    out_tiles = total_rows // 4

    def convolve_block(block, carry):
        for out_tile in range(out_tiles):
            sums = zeros
            for at in range(out_tile + 1):
                sums = step(at, sums, block, out_tile, at < out_tile)
            finish(sums, block, out_tile)
        return carry

    def convolve_tile(index, carry):
        block = lax.rem(index, blocks)
        out_tile = lax.div(index, blocks)
        sums = lax.fori_loop(
            0, out_tile + 1, lambda at, sums: step(at, sums, block, out_tile, True), zeros
        )
        finish(sums, block, out_tile)
        return carry

    if total_rows <= 32:
        lax.fori_loop(0, blocks, convolve_block, 0)
    else:
        lax.fori_loop(0, out_tiles * blocks, convolve_tile, 0)

    def gather_terms(at, carry):
        tiles = [product[at * 8 + k] for k in range(8)]
        summed = jnp.sum(jnp.stack(tiles), axis=1)
        if blocks == 4:
            turned = jnp.concatenate([summed[blocks:], -summed[:blocks]], axis=0)
        else:
            swapped = [
                tiles[k + blocks] if (k // blocks) % 2 == 0 else -tiles[k - blocks]
                for k in range(8)
            ]
            turned = jnp.sum(jnp.stack(swapped), axis=1)
        place = pl.ds(pl.multiple_of(at * 8, 8), 8)
        mixed[place, pl.ds(0, LANES)] = summed
        mixed[place, pl.ds(LANES, LANES)] = turned
        return carry

    lax.fori_loop(0, total_rows * 2 * blocks // 8, gather_terms, 0, unroll=4)
    out[...] = dot_split(mixed[...], back[...])


def final_kernel(scaling, spread, inner_cos, inner_sin, outer, out):
    values = spread[...]
    stacked = jnp.concatenate([values * inner_cos[...], values * inner_sin[...]], axis=0)
    high, low = split_parts(stacked)
    joined = jnp.concatenate([high, low, high], axis=0)
    total = jnp.dot(outer[...], joined, preferred_element_type=jnp.float32)
    out[...] = total * scaling


def whole_call(kernel, out_shape, scratch, operands, kept=True):
    return pl.pallas_call(
        kernel,
        out_shape=(pltpu.VMEM if kept else jax.ShapeDtypeStruct)(out_shape, jnp.float32),
        in_specs=[pl.BlockSpec(memory_space=pltpu.VMEM)] * len(operands),
        out_specs=pl.BlockSpec(memory_space=pltpu.VMEM),
        scratch_shapes=[pltpu.VMEM(*shape) for shape in scratch],
        compiler_params=pltpu.CompilerParams(vmem_limit_bytes=VMEM_BYTES),
    )(*[pltpu.with_memory_space_constraint(operand, pltpu.VMEM) for operand in operands])


def row_scratch(blocks, rows, terms):
    return [
        ((4, blocks, rows, terms, LANES), jnp.float32),
        ((2 * blocks * rows * terms, 6 * LANES), jnp.bfloat16),
    ]


def spectra_by_exchange(density, blocks, shared):
    rows_here, width = density.shape
    comps, ranks = lax.axis_size("comp"), lax.axis_size("rank")
    core = lax.rem(lax.axis_index("rank"), 2)
    half = width // 2
    lines = comps // 2
    terms = shared[0].shape[0]
    mine = lax.dynamic_slice_in_dim(density, core * half, half, 1)

    def along(block, step):
        pairs = [(c, ((c // 2 + step) % lines) * 2 + c % 2) for c in range(comps)]
        return lax.ppermute(block, "comp", pairs)

    def across(block):
        return lax.ppermute(block, "comp", [(c, c ^ 1) for c in range(comps)])

    def beside(block):
        return lax.ppermute(block, "rank", [(r, r ^ 1) for r in range(ranks)])

    def spectra(pieces, sources):
        rows = rows_here * len(sources)
        return whole_call(
            lambda *refs: pieces_kernel(blocks, sources, len(pieces), *refs),
            (2 * blocks, 2, rows, terms, LANES),
            row_scratch(blocks, rows, terms),
            (*pieces, *shared),
        )

    lined = [along(mine, step) for step in range(1, lines)]
    flipped_own = across(mine)
    line_near = jnp.stack(lined)
    near = jnp.concatenate([flipped_own[None], line_near])
    far = beside(near)
    flipped_near = across(line_near)
    ready = [(0, None, 0, 0, False), (1, 2, 0, 0, True)]
    ready += [(1, 2, step, step, False) for step in range(1, lines)]
    ahead = comps // 2
    early, late = ready[:ahead], ready[ahead:]
    first = spectra([density, near, far], early)
    flipped_near = after(flipped_near, first)
    flipped_far = beside(flipped_near)
    late = [(near - 1, far - 1, index, *rest) for near, far, index, *rest in late]
    late += [(2, 3, step - 1, step, True) for step in range(1, lines)]
    second = spectra([near, far, flipped_near, flipped_far], late)
    layout = [source[3:] for source in early + late]
    return [first[None], second[None]], layout


def spectra_by_gather(density, blocks, shared):
    rows_here, width = density.shape
    comps, ranks = lax.axis_size("comp"), lax.axis_size("rank")
    terms = shared[0].shape[0]
    total_rows = rows_here * comps
    part = width // ranks
    mine = lax.dynamic_slice_in_dim(density, lax.axis_index("rank") * part, part, 1)
    gathered = lax.all_gather(mine, AXES, axis=0).reshape(comps, ranks, rows_here, part)
    tile_shape = (2 * blocks, 2, 8, terms, LANES)
    spectra = pl.pallas_call(
        lambda *refs: gathered_kernel(blocks, *refs),
        grid=(total_rows // 8,),
        out_shape=jax.ShapeDtypeStruct((total_rows // 8, *tile_shape), jnp.float32),
        in_specs=[pl.BlockSpec((8 // rows_here, ranks, rows_here, part), lambda t: (t, 0, 0, 0))]
        + [pl.BlockSpec(memory_space=pltpu.VMEM)] * 8,
        out_specs=pl.BlockSpec((1, *tile_shape), lambda t: (t, 0, 0, 0, 0, 0)),
        scratch_shapes=[pltpu.VMEM(*shape) for shape in row_scratch(blocks, 8, terms)],
        compiler_params=pltpu.CompilerParams(vmem_limit_bytes=VMEM_BYTES),
    )(gathered, *shared)
    return [spectra], None


def body(density, row_left, col_left, row_right, col_right):
    rows_here, width = density.shape
    comps = lax.axis_size("comp")
    devices = comps * lax.axis_size("rank")
    total_rows = rows_here * comps
    terms = row_left.shape[0]
    groups = min(devices, width // LANES)
    term_groups = devices // groups
    blocks = width // (groups * LANES)
    device_at = lax.axis_index(AXES)
    group_at = lax.rem(device_at, groups)

    cells = lax.broadcasted_iota(jnp.int32, (width // LANES, LANES), 0) * LANES
    cells = cells + lax.broadcasted_iota(jnp.int32, (width // LANES, LANES), 1)
    turns = lax.rem(cells * (4 * group_at + 1), 4 * width)
    angles = turns.astype(jnp.float32) * (2.0 * math.pi / (4 * width))
    if term_groups > 1:
        term_at = lax.broadcasted_iota(jnp.int32, (terms, 1), 0)
        chosen = lax.div(term_at, terms // term_groups) == lax.div(device_at, groups)
        col_left = jnp.where(chosen, col_left, 0.0)
        col_right = jnp.where(chosen, col_right, 0.0)
    shared = (
        col_left,
        col_right,
        jnp.cos(angles),
        -jnp.sin(angles),
        row_left,
        row_right,
        block_twiddles(blocks),
        split_rows(forward_table()),
    )
    if comps <= 8:
        tiles, layout = spectra_by_exchange(density, blocks, shared)
    else:
        tiles, layout = spectra_by_gather(density, blocks, shared)

    out_rows = total_rows * 2 * blocks
    sent = whole_call(
        lambda *refs: convolve_kernel(blocks, rows_here, layout, len(tiles), *refs),
        (out_rows, LANES),
        [
            ((2 * blocks, 3, PAD + total_rows, terms, LANES), jnp.float32),
            ((out_rows, terms, LANES), jnp.float32),
            ((out_rows, 2 * LANES), jnp.float32),
        ],
        (*tiles, split_rows(inverse_table())),
    )
    spread = lax.all_to_all(sent, AXES, split_axis=0, concat_axis=0, tiled=True)
    inner_cos, inner_sin, outer_table = final_tables(devices, groups, blocks, width)
    scaling = 0.5 / (math.sqrt(total_rows * width) * width)
    result = whole_call(
        lambda *refs: final_kernel(scaling, *refs),
        (width // LANES, LANES),
        [],
        (
            spread,
            jnp.asarray(inner_cos, jnp.float32),
            jnp.asarray(inner_sin, jnp.float32),
            split_columns(outer_table),
        ),
        kept=False,
    )
    return result.reshape(1, width)


def solution(mesh):
    return jax.shard_map(
        body,
        mesh=mesh,
        in_specs=(P("comp", None), P(), P(), P(), P()),
        out_specs=P(AXES, None),
        check_vma=False,
    )
```

```python
import math

import jax
import jax.numpy as jnp
import numpy as np
from jax import lax
from jax.experimental import pallas as pl
from jax.experimental.pallas import tpu as pltpu
from jax.sharding import PartitionSpec as P

LANES = 128
VMEM_BYTES = 28 * 1024 * 1024
AXES = ("comp", "rank")
PAD = 4


def split_parts(values):
    high = values.astype(jnp.bfloat16)
    low = (values - high.astype(jnp.float32)).astype(jnp.bfloat16)
    return high, low


def split_rows(table):
    high, low = split_parts(jnp.asarray(table, jnp.float32))
    return jnp.concatenate([high, high, low], axis=0)


def split_columns(table):
    high, low = split_parts(jnp.asarray(table, jnp.float32))
    return jnp.concatenate([high, high, low], axis=1)


def dot_split(rows, table):
    high, low = split_parts(rows)
    joined = jnp.concatenate([high, low, high], axis=1)
    return jnp.dot(joined, table, preferred_element_type=jnp.float32)


def forward_table():
    angles = 2.0 * np.pi * np.outer(np.arange(LANES), np.arange(LANES)) / LANES
    cosine, sine = np.cos(angles), np.sin(angles)
    return np.block([[cosine, -sine], [sine, cosine]])


def inverse_table():
    angles = 2.0 * np.pi * np.outer(np.arange(LANES), np.arange(LANES)) / LANES
    return np.concatenate([np.cos(angles), -np.sin(angles)], axis=0)


def block_twiddles(blocks):
    angles = 2.0 * np.pi * np.outer(np.arange(blocks), np.arange(LANES)) / (blocks * LANES)
    table = np.stack([np.cos(angles), -np.sin(angles)], axis=1)
    return jnp.asarray(
        np.broadcast_to(table[:, :, None, :], (blocks, 2, 8, LANES)), jnp.float32
    )


def final_tables(devices, groups, blocks, width):
    owner = np.arange(devices) % groups
    frequency = (owner[:, None] + groups * np.arange(blocks)[None, :]).astype(np.float64) + 0.25
    frequency = np.broadcast_to(frequency[:, None, :], (devices, 2, blocks))
    inner = 2.0 * np.pi * frequency[..., None] * np.arange(LANES) / width
    rows = devices * 2 * blocks
    inner_cos = np.cos(inner).reshape(rows, LANES)
    inner_sin = np.sin(inner).reshape(rows, LANES)
    outer_count = width // LANES
    outer = 2.0 * np.pi * frequency * LANES / width
    outer = np.arange(outer_count)[:, None] * outer.reshape(1, rows)
    is_real = np.broadcast_to(np.array([True, False])[None, :, None], (devices, 2, blocks))
    is_real = is_real.reshape(1, rows)
    with_cos = np.where(is_real, np.cos(outer), -np.sin(outer))
    with_sin = np.where(is_real, -np.sin(outer), -np.cos(outer))
    return inner_cos, inner_sin, np.concatenate([with_cos, with_sin], axis=1)


def block_fourier(reals, imags):
    count = len(reals)
    if count == 1:
        return reals, imags
    if count == 2:
        return (
            [reals[0] + reals[1], reals[0] - reals[1]],
            [imags[0] + imags[1], imags[0] - imags[1]],
        )
    even_real, odd_real = reals[0] + reals[2], reals[0] - reals[2]
    even_imag, odd_imag = imags[0] + imags[2], imags[0] - imags[2]
    pair_real, gap_real = reals[1] + reals[3], reals[1] - reals[3]
    pair_imag, gap_imag = imags[1] + imags[3], imags[1] - imags[3]
    return (
        [even_real + pair_real, odd_real + gap_imag, even_real - pair_real, odd_real - gap_imag],
        [even_imag + pair_imag, odd_imag - gap_real, even_imag - pair_imag, odd_imag + gap_real],
    )


def reduce_rows(blocks, rows, terms, fetch, factors_at, starts, span, partial):
    inner = blocks * LANES
    outer = span // inner
    unroll = math.gcd(16, outer)

    def reduce_block(block, carry):
        for first in range(0, rows, 8):
            sums = (jnp.zeros((terms, LANES), jnp.float32),) * 32
            for part, start in enumerate(starts):

                def step(at, sums, first=first, part=part, start=start):
                    sums = list(sums)
                    for extra in range(unroll):
                        lane = (at * unroll + extra) * inner + block * LANES
                        factors = factors_at(start + lane, first == 0)
                        for row in range(8):
                            value = fetch(part, first + row, lane)
                            value = jnp.broadcast_to(value, (terms, LANES))
                            for k in range(4):
                                sums[row * 4 + k] += value * factors[k]
                    return tuple(sums)

                sums = lax.fori_loop(0, outer // unroll, step, sums)
            for row in range(8):
                for k in range(4):
                    partial[k, block, first + row] = sums[row * 4 + k]
        return carry

    lax.fori_loop(0, blocks, reduce_block, 0)


def transform_rows(blocks, rows, row_at, row_factors, twiddle, table, out, partial, joined):
    terms, total_rows = row_factors[0].shape
    lanes = lax.broadcasted_iota(jnp.int32, (terms, total_rows), 1)

    def butterfly(row, side):
        picked = jnp.where(lanes == row_at(row), row_factors[side][...], 0.0)
        factor = jnp.sum(picked, axis=1, keepdims=True)
        factor = jnp.broadcast_to(factor, (terms, LANES))
        reals = [partial[2 * side, block, row] * factor for block in range(blocks)]
        imags = [partial[2 * side + 1, block, row] * factor for block in range(blocks)]
        reals, imags = block_fourier(reals, imags)
        for block in range(1, blocks):
            real, imag = reals[block], imags[block]
            cosine, sine = twiddle[block, 0], twiddle[block, 1]
            reals[block] = real * cosine - imag * sine
            imags[block] = real * sine + imag * cosine
        return reals, imags

    def butterfly_pair(pair):
        for side in range(2):
            both = [butterfly(pair * 2 + extra, side) for extra in range(2)]
            for block in range(blocks):
                base = ((block * 2 + side) * rows + pair * 2) * terms
                place = pl.ds(base, 2 * terms)
                for part in range(2):
                    values = jnp.concatenate([both[0][part][block], both[1][part][block]], axis=0)
                    high, low = split_parts(values)
                    for third, piece in enumerate((high, low, high)):
                        joined[place, pl.ds((third * 2 + part) * LANES, LANES)] = piece

    for pair in range(rows // 2):
        butterfly_pair(pair)
    planes = 2 * blocks
    step = planes * rows * terms
    while step > 512:
        step //= 2
    plane_step = step // (rows * terms)

    def transform(at, carry):
        place = pl.ds(pl.multiple_of(at * step, 16), step)
        total = jnp.dot(joined[place, :], table[...], preferred_element_type=jnp.float32)
        total = total.reshape(plane_step, rows, terms, 2 * LANES)
        place = pl.ds(at * plane_step, plane_step)
        out[place, 0] = total[..., :LANES]
        out[place, 1] = total[..., LANES:]
        return carry

    lax.fori_loop(0, planes // plane_step, transform, 0)


def comp_of(step, flipped):
    lines = lax.axis_size("comp") // 2
    comp_at = lax.axis_index("comp")
    line = lax.rem(lax.div(comp_at, 2) + lines - step, lines)
    side = lax.rem(comp_at, 2)
    return line * 2 + (1 - side if flipped else side)


def made_factors(columns, phases, keep=None):
    terms = columns[0].shape[0]

    def factors_at(lane, first):
        place = pl.ds(pl.multiple_of(lane, LANES), LANES)
        if keep is not None and not first:
            return [keep[k, :, place] for k in range(4)]
        turn = pl.ds(lax.div(lane, LANES), 1)
        factors = [
            column[:, place] * jnp.broadcast_to(phase[turn, :], (terms, LANES))
            for column in columns
            for phase in phases
        ]
        if keep is not None:
            for k in range(4):
                keep[k, :, place] = factors[k]
        return factors

    return factors_at


def start_tables(tables, held, arrivals):
    copies = [
        pltpu.make_async_copy(table, place, arrivals.at[k])
        for k, (table, place) in enumerate(zip(tables, held))
    ]
    for copy in copies:
        copy.start()
    return copies


def pieces_kernel(blocks, sources, count, making, *refs):
    pieces, refs = refs[:count], refs[count:]
    if making:
        columns, phases, refs = refs[0:2], refs[2:4], refs[4:]
        row_factors, tables, (out, weights), refs = refs[0:2], refs[2:4], refs[4:6], refs[6:]
    else:
        weights, row_factors, tables, out, refs = refs[0], refs[1:3], refs[3:5], refs[5], refs[6:]
    partial, joined, twiddle, table, arrivals = refs
    copies = start_tables(tables, (twiddle, table), arrivals)
    rows_here = pieces[0].shape[-2]
    terms, width = weights.shape[1:]
    half = width // 2
    core = lax.rem(lax.axis_index("rank"), 2)
    starts = [core * half, (1 - core) * half]
    rows = len(sources) * rows_here

    def fetch(part, row, lane):
        near, far, index, _, _ = sources[row // rows_here]
        row = pl.ds(row % rows_here, 1)
        if far is None:
            return pieces[near][row, pl.ds(pl.multiple_of(starts[part] + lane, LANES), LANES)]
        ref = pieces[far if part else near]
        return ref[index, row, pl.ds(pl.multiple_of(lane, LANES), LANES)]

    bases = [comp_of(step, flipped) * rows_here for _, _, _, step, flipped in sources]

    def row_at(row):
        return bases[row // rows_here] + row % rows_here

    if making:
        factors_at = made_factors(columns, phases, weights)
    else:

        def factors_at(lane, first):
            place = pl.ds(pl.multiple_of(lane, LANES), LANES)
            return [weights[k, :, place] for k in range(4)]

    reduce_rows(blocks, rows, terms, fetch, factors_at, starts, half, partial)
    for copy in copies:
        copy.wait()
    transform_rows(blocks, rows, row_at, row_factors, twiddle, table, out, partial, joined)


def gathered_kernel(blocks, pieces, *refs):
    columns, phases, row_factors, tables = refs[0:2], refs[2:4], refs[4:6], refs[6:8]
    out, partial, joined, twiddle, table, arrivals = refs[8:]
    copies = start_tables(tables, (twiddle, table), arrivals)
    parts, rows_here, span = pieces.shape[1:]

    def fetch(part, row, lane):
        place = pl.ds(pl.multiple_of(lane, LANES), LANES)
        return pieces[row // rows_here, part, pl.ds(row % rows_here, 1), place]

    base = pl.program_id(0) * 8
    starts = [part * span for part in range(parts)]
    terms = columns[0].shape[0]
    reduce_rows(blocks, 8, terms, fetch, made_factors(columns, phases), starts, span, partial)
    for copy in copies:
        copy.wait()
    transform_rows(
        blocks,
        8,
        lambda row: base + row,
        row_factors,
        twiddle,
        table,
        out.at[0],
        partial,
        joined,
    )


def pass_kernel(value, earlier, out):
    del value, earlier, out


def after(value, earlier):
    anywhere = pl.BlockSpec(memory_space=pl.ANY)
    return pl.pallas_call(
        pass_kernel,
        out_shape=jax.ShapeDtypeStruct(value.shape, value.dtype),
        in_specs=[anywhere, anywhere],
        out_specs=anywhere,
        input_output_aliases={0: 0},
    )(*[pltpu.with_memory_space_constraint(array, pltpu.VMEM) for array in (value, earlier)])


def convolve_kernel(blocks, rows_here, layout, tile_count, *refs):
    tiles = refs[:tile_count]
    back, out, spectrum, product, mixed = refs[tile_count:]
    total_rows = spectrum.shape[2] - PAD
    terms = spectrum.shape[3]
    spectrum[:, :, pl.ds(0, PAD)] = jnp.zeros((2 * blocks, 3, PAD, terms, LANES), jnp.float32)
    moves = []
    for number, tile in enumerate(tiles):
        for at in range(tile.shape[0]):
            for first in range(0, tile.shape[3], rows_here):
                moves.append((tile, at, first))
    comps = [comp_of(*layout[k]) if layout else k for k in range(len(moves))]

    def collect(plane, carry):
        for (tile, at, first), comp in zip(moves, comps):
            real = tile[at, plane, 0, pl.ds(first, rows_here)]
            imag = tile[at, plane, 1, pl.ds(first, rows_here)]
            place = pl.ds(PAD + comp * rows_here, rows_here)
            spectrum[plane, 0, place] = real
            spectrum[plane, 1, place] = imag
            spectrum[plane, 2, place] = real + imag
        return carry

    lax.fori_loop(0, 2 * blocks, collect, 0)

    def step(at, sums, block, out_tile, whole):
        sums = list(sums)
        left_base = PAD + 4 * at
        right_base = PAD + 4 * (out_tile - at)
        for part in range(3):
            left = [spectrum[2 * block, part, left_base + k] for k in range(4)]
            right = {
                k: spectrum[2 * block + 1, part, right_base + k]
                for k in range(-3 if whole else 0, 4)
            }
            for row in range(4):
                for k in range(4 if whole else row + 1):
                    sums[row * 3 + part] += left[k] * right[row - k]
        return tuple(sums)

    def finish(sums, block, out_tile):
        for row in range(4):
            both_real, both_imag, crossed = sums[row * 3 : row * 3 + 3]
            base = (out_tile * 4 + row) * 2 * blocks + block
            product[base] = both_real - both_imag
            product[base + blocks] = crossed - both_real - both_imag

    zeros = (jnp.zeros((terms, LANES), jnp.float32),) * 12
    out_tiles = total_rows // 4

    def convolve_block(block, carry):
        for out_tile in range(out_tiles):
            sums = zeros
            for at in range(out_tile + 1):
                sums = step(at, sums, block, out_tile, at < out_tile)
            finish(sums, block, out_tile)
        return carry

    def convolve_tile(index, carry):
        block = lax.rem(index, blocks)
        out_tile = lax.div(index, blocks)
        sums = lax.fori_loop(
            0, out_tile + 1, lambda at, sums: step(at, sums, block, out_tile, True), zeros
        )
        finish(sums, block, out_tile)
        return carry

    if total_rows <= 32:
        lax.fori_loop(0, blocks, convolve_block, 0)
    else:
        lax.fori_loop(0, out_tiles * blocks, convolve_tile, 0)

    def gather_terms(at, carry):
        tiles = [product[at * 8 + k] for k in range(8)]
        summed = jnp.sum(jnp.stack(tiles), axis=1)
        if blocks == 4:
            turned = jnp.concatenate([summed[blocks:], -summed[:blocks]], axis=0)
        else:
            swapped = [
                tiles[k + blocks] if (k // blocks) % 2 == 0 else -tiles[k - blocks]
                for k in range(8)
            ]
            turned = jnp.sum(jnp.stack(swapped), axis=1)
        place = pl.ds(pl.multiple_of(at * 8, 8), 8)
        mixed[place, pl.ds(0, LANES)] = summed
        mixed[place, pl.ds(LANES, LANES)] = turned
        return carry

    lax.fori_loop(0, total_rows * 2 * blocks // 8, gather_terms, 0, unroll=4)
    out[...] = dot_split(mixed[...], back[...])


def final_kernel(scaling, spread, inner_cos, inner_sin, outer, out):
    values = spread[...]
    stacked = jnp.concatenate([values * inner_cos[...], values * inner_sin[...]], axis=0)
    high, low = split_parts(stacked)
    joined = jnp.concatenate([high, low, high], axis=0)
    total = jnp.dot(outer[...], joined, preferred_element_type=jnp.float32)
    out[...] = total * scaling


def whole_call(kernel, out_shapes, scratch, operands, tables=(), kept=True):
    out_type = pltpu.VMEM if kept else jax.ShapeDtypeStruct
    operands = [pltpu.with_memory_space_constraint(operand, pltpu.VMEM) for operand in operands]
    return pl.pallas_call(
        kernel,
        out_shape=[out_type(shape, jnp.float32) for shape in out_shapes],
        in_specs=[pl.BlockSpec(memory_space=pltpu.VMEM)] * len(operands)
        + [pl.BlockSpec(memory_space=pl.ANY)] * len(tables),
        out_specs=[pl.BlockSpec(memory_space=pltpu.VMEM)] * len(out_shapes),
        scratch_shapes=scratch,
        compiler_params=pltpu.CompilerParams(vmem_limit_bytes=VMEM_BYTES),
    )(*operands, *tables)


def row_scratch(blocks, rows, terms, tables):
    return [
        pltpu.VMEM((4, blocks, rows, terms, LANES), jnp.float32),
        pltpu.VMEM((2 * blocks * rows * terms, 6 * LANES), jnp.bfloat16),
        *[pltpu.VMEM(table.shape, table.dtype) for table in tables],
        pltpu.SemaphoreType.DMA((len(tables),)),
    ]


def spectra_by_exchange(density, blocks, weighing, row_factors, tables):
    rows_here, width = density.shape
    comps, ranks = lax.axis_size("comp"), lax.axis_size("rank")
    core = lax.rem(lax.axis_index("rank"), 2)
    half = width // 2
    lines = comps // 2
    terms = row_factors[0].shape[0]
    mine = lax.dynamic_slice_in_dim(density, core * half, half, 1)

    def along(block, step):
        pairs = [(c, ((c // 2 + step) % lines) * 2 + c % 2) for c in range(comps)]
        return lax.ppermute(block, "comp", pairs)

    def across(block):
        return lax.ppermute(block, "comp", [(c, c ^ 1) for c in range(comps)])

    def beside(block):
        return lax.ppermute(block, "rank", [(r, r ^ 1) for r in range(ranks)])

    def spectra(pieces, sources, weights=None):
        rows = rows_here * len(sources)
        making = weights is None
        shapes = [(2 * blocks, 2, rows, terms, LANES)]
        return whole_call(
            lambda *refs: pieces_kernel(blocks, sources, len(pieces), making, *refs),
            shapes + [(4, terms, width)] if making else shapes,
            row_scratch(blocks, rows, terms, tables),
            (*pieces, *(weighing if making else (weights,)), *row_factors),
            tables,
        )

    lined = [along(mine, step) for step in range(1, lines)]
    flipped_own = across(mine)
    line_near = jnp.stack(lined)
    near = jnp.concatenate([flipped_own[None], line_near])
    far = beside(near)
    flipped_near = across(line_near)
    ready = [(0, None, 0, 0, False), (1, 2, 0, 0, True)]
    ready += [(1, 2, step, step, False) for step in range(1, lines)]
    ahead = comps // 2
    early, late = ready[:ahead], ready[ahead:]
    first, weights = spectra([density, near, far], early)
    flipped_near = after(flipped_near, first)
    flipped_far = beside(flipped_near)
    late = [(near - 1, far - 1, index, *rest) for near, far, index, *rest in late]
    late += [(2, 3, step - 1, step, True) for step in range(1, lines)]
    (second,) = spectra([near, far, flipped_near, flipped_far], late, weights)
    layout = [source[3:] for source in early + late]
    return [first[None], second[None]], layout


def spectra_by_gather(density, blocks, weighing, row_factors, tables):
    rows_here, width = density.shape
    comps, ranks = lax.axis_size("comp"), lax.axis_size("rank")
    terms = row_factors[0].shape[0]
    total_rows = rows_here * comps
    part = width // ranks
    mine = lax.dynamic_slice_in_dim(density, lax.axis_index("rank") * part, part, 1)
    gathered = lax.all_gather(mine, AXES, axis=0).reshape(comps, ranks, rows_here, part)
    tile_shape = (2 * blocks, 2, 8, terms, LANES)
    spectra = pl.pallas_call(
        lambda *refs: gathered_kernel(blocks, *refs),
        grid=(total_rows // 8,),
        out_shape=jax.ShapeDtypeStruct((total_rows // 8, *tile_shape), jnp.float32),
        in_specs=[pl.BlockSpec((8 // rows_here, ranks, rows_here, part), lambda t: (t, 0, 0, 0))]
        + [pl.BlockSpec(memory_space=pltpu.VMEM)] * 6
        + [pl.BlockSpec(memory_space=pl.ANY)] * len(tables),
        out_specs=pl.BlockSpec((1, *tile_shape), lambda t: (t, 0, 0, 0, 0, 0)),
        scratch_shapes=row_scratch(blocks, 8, terms, tables),
        compiler_params=pltpu.CompilerParams(vmem_limit_bytes=VMEM_BYTES),
    )(gathered, *weighing, *row_factors, *tables)
    return [spectra], None


def body(density, row_left, col_left, row_right, col_right):
    rows_here, width = density.shape
    comps = lax.axis_size("comp")
    devices = comps * lax.axis_size("rank")
    total_rows = rows_here * comps
    terms = row_left.shape[0]
    groups = min(devices, width // LANES)
    term_groups = devices // groups
    blocks = width // (groups * LANES)
    device_at = lax.axis_index(AXES)
    group_at = lax.rem(device_at, groups)

    cells = lax.broadcasted_iota(jnp.int32, (width // LANES, LANES), 0) * LANES
    cells = cells + lax.broadcasted_iota(jnp.int32, (width // LANES, LANES), 1)
    turns = lax.rem(cells * (4 * group_at + 1), 4 * width)
    angles = turns.astype(jnp.float32) * (2.0 * math.pi / (4 * width))
    if term_groups > 1:
        term_at = lax.broadcasted_iota(jnp.int32, (terms, 1), 0)
        chosen = lax.div(term_at, terms // term_groups) == lax.div(device_at, groups)
        col_left = jnp.where(chosen, col_left, 0.0)
        col_right = jnp.where(chosen, col_right, 0.0)
    weighing = (col_left, col_right, jnp.cos(angles), -jnp.sin(angles))
    row_factors = (row_left, row_right)
    tables = (block_twiddles(blocks), split_rows(forward_table()))
    spectra = spectra_by_exchange if comps <= 8 else spectra_by_gather
    tiles, layout = spectra(density, blocks, weighing, row_factors, tables)

    out_rows = total_rows * 2 * blocks
    (sent,) = whole_call(
        lambda *refs: convolve_kernel(blocks, rows_here, layout, len(tiles), *refs),
        [(out_rows, LANES)],
        [
            pltpu.VMEM((2 * blocks, 3, PAD + total_rows, terms, LANES), jnp.float32),
            pltpu.VMEM((out_rows, terms, LANES), jnp.float32),
            pltpu.VMEM((out_rows, 2 * LANES), jnp.float32),
        ],
        (*tiles, split_rows(inverse_table())),
    )
    spread = lax.all_to_all(sent, AXES, split_axis=0, concat_axis=0, tiled=True)
    inner_cos, inner_sin, outer_table = final_tables(devices, groups, blocks, width)
    scaling = 0.5 / (math.sqrt(total_rows * width) * width)
    (result,) = whole_call(
        lambda *refs: final_kernel(scaling, *refs),
        [(width // LANES, LANES)],
        [],
        (
            spread,
            jnp.asarray(inner_cos, jnp.float32),
            jnp.asarray(inner_sin, jnp.float32),
            split_columns(outer_table),
        ),
        kept=False,
    )
    return result.reshape(1, width)


def solution(mesh):
    return jax.shard_map(
        body,
        mesh=mesh,
        in_specs=(P("comp", None), P(), P(), P(), P()),
        out_specs=P(AXES, None),
        check_vma=False,
    )
```

```python
import math

import jax
import jax.numpy as jnp
import numpy as np
from jax import lax
from jax.experimental import pallas as pl
from jax.experimental.pallas import tpu as pltpu
from jax.sharding import PartitionSpec as P

LANES = 128
VMEM_BYTES = 28 * 1024 * 1024
AXES = ("comp", "rank")
PAD = 4
HELD_PARTS = (0, 2, 1, 3)


def split_parts(values):
    high = values.astype(jnp.bfloat16)
    low = (values - high.astype(jnp.float32)).astype(jnp.bfloat16)
    return high, low


def split_rows(table):
    high, low = split_parts(jnp.asarray(table, jnp.float32))
    return jnp.concatenate([high, high, low], axis=0)


def split_columns(table):
    high, low = split_parts(jnp.asarray(table, jnp.float32))
    return jnp.concatenate([high, high, low], axis=1)


def dot_split(rows, table):
    high, low = split_parts(rows)
    joined = jnp.concatenate([high, low, high], axis=1)
    return jnp.dot(joined, table, preferred_element_type=jnp.float32)


def forward_table():
    angles = 2.0 * np.pi * np.outer(np.arange(LANES), np.arange(LANES)) / LANES
    cosine, sine = np.cos(angles), np.sin(angles)
    return np.block([[cosine, -sine], [sine, cosine]])


def inverse_table():
    angles = 2.0 * np.pi * np.outer(np.arange(LANES), np.arange(LANES)) / LANES
    return np.concatenate([np.cos(angles), -np.sin(angles)], axis=0)


def block_twiddles(blocks):
    angles = 2.0 * np.pi * np.outer(np.arange(blocks), np.arange(LANES)) / (blocks * LANES)
    table = np.stack([np.cos(angles), -np.sin(angles)], axis=1)
    return jnp.asarray(
        np.broadcast_to(table[:, :, None, :], (blocks, 2, 8, LANES)), jnp.float32
    )


def final_tables(devices, groups, blocks, width):
    owner = np.arange(devices) % groups
    frequency = (owner[:, None] + groups * np.arange(blocks)[None, :]).astype(np.float64) + 0.25
    frequency = np.broadcast_to(frequency[:, None, :], (devices, 2, blocks))
    inner = 2.0 * np.pi * frequency[..., None] * np.arange(LANES) / width
    rows = devices * 2 * blocks
    inner_cos = np.cos(inner).reshape(rows, LANES)
    inner_sin = np.sin(inner).reshape(rows, LANES)
    outer_count = width // LANES
    outer = 2.0 * np.pi * frequency * LANES / width
    outer = np.arange(outer_count)[:, None] * outer.reshape(1, rows)
    is_real = np.broadcast_to(np.array([True, False])[None, :, None], (devices, 2, blocks))
    is_real = is_real.reshape(1, rows)
    with_cos = np.where(is_real, np.cos(outer), -np.sin(outer))
    with_sin = np.where(is_real, -np.sin(outer), -np.cos(outer))
    return inner_cos, inner_sin, np.concatenate([with_cos, with_sin], axis=1)


def block_fourier(reals, imags):
    count = len(reals)
    if count == 1:
        return reals, imags
    if count == 2:
        return (
            [reals[0] + reals[1], reals[0] - reals[1]],
            [imags[0] + imags[1], imags[0] - imags[1]],
        )
    even_real, odd_real = reals[0] + reals[2], reals[0] - reals[2]
    even_imag, odd_imag = imags[0] + imags[2], imags[0] - imags[2]
    pair_real, gap_real = reals[1] + reals[3], reals[1] - reals[3]
    pair_imag, gap_imag = imags[1] + imags[3], imags[1] - imags[3]
    return (
        [even_real + pair_real, odd_real + gap_imag, even_real - pair_real, odd_real - gap_imag],
        [even_imag + pair_imag, odd_imag - gap_real, even_imag - pair_imag, odd_imag + gap_real],
    )


def reduce_rows(blocks, rows, terms, fetch, factors_at, starts, span, partial):
    inner = blocks * LANES
    outer = span // inner
    unroll = math.gcd(16, outer)

    def reduce_block(block, carry):
        for first in range(0, rows, 8):
            sums = (jnp.zeros((terms, LANES), jnp.float32),) * 32
            for part, start in enumerate(starts):

                def step(at, sums, first=first, part=part, start=start):
                    sums = list(sums)
                    for extra in range(unroll):
                        lane = (at * unroll + extra) * inner + block * LANES
                        factors = factors_at(start + lane, first == 0)
                        for row in range(8):
                            value = fetch(part, first + row, lane)
                            value = jnp.broadcast_to(value, (terms, LANES))
                            for k in range(4):
                                sums[row * 4 + k] += value * factors[k]
                    return tuple(sums)

                sums = lax.fori_loop(0, outer // unroll, step, sums)
            for row in range(8):
                for k in range(4):
                    partial[k, block, first + row] = sums[row * 4 + k]
        return carry

    lax.fori_loop(0, blocks, reduce_block, 0)


def transform_rows(blocks, rows, row_at, row_factors, twiddle, table, out, partial, joined):
    terms, total_rows = row_factors[0].shape
    lanes = lax.broadcasted_iota(jnp.int32, (terms, total_rows), 1)

    def butterfly(row, side):
        picked = jnp.where(lanes == row_at(row), row_factors[side][...], 0.0)
        factor = jnp.sum(picked, axis=1, keepdims=True)
        factor = jnp.broadcast_to(factor, (terms, LANES))
        reals = [partial[2 * side, block, row] * factor for block in range(blocks)]
        imags = [partial[2 * side + 1, block, row] * factor for block in range(blocks)]
        reals, imags = block_fourier(reals, imags)
        for block in range(1, blocks):
            real, imag = reals[block], imags[block]
            cosine, sine = twiddle[block, 0], twiddle[block, 1]
            reals[block] = real * cosine - imag * sine
            imags[block] = real * sine + imag * cosine
        return reals, imags

    def butterfly_pair(pair):
        for side in range(2):
            both = [butterfly(pair * 2 + extra, side) for extra in range(2)]
            for block in range(blocks):
                base = ((block * 2 + side) * rows + pair * 2) * terms
                place = pl.ds(base, 2 * terms)
                for part in range(2):
                    values = jnp.concatenate([both[0][part][block], both[1][part][block]], axis=0)
                    high, low = split_parts(values)
                    for third, piece in enumerate((high, low, high)):
                        joined[place, pl.ds((third * 2 + part) * LANES, LANES)] = piece

    for pair in range(rows // 2):
        butterfly_pair(pair)
    planes = 2 * blocks
    step = planes * rows * terms
    while step > 512:
        step //= 2
    plane_step = step // (rows * terms)

    def transform(at, carry):
        place = pl.ds(pl.multiple_of(at * step, 16), step)
        total = jnp.dot(joined[place, :], table[...], preferred_element_type=jnp.float32)
        total = total.reshape(plane_step, rows, terms, 2 * LANES)
        place = pl.ds(at * plane_step, plane_step)
        out[place, 0] = total[..., :LANES]
        out[place, 1] = total[..., LANES:]
        return carry

    lax.fori_loop(0, planes // plane_step, transform, 0)


def comp_of(step, flipped):
    lines = lax.axis_size("comp") // 2
    comp_at = lax.axis_index("comp")
    line = lax.rem(lax.div(comp_at, 2) + lines - step, lines)
    side = lax.rem(comp_at, 2)
    return line * 2 + (1 - side if flipped else side)


def make_phases(groups, phases):
    width = phases.shape[1] * LANES
    device_at = lax.axis_index("comp") * lax.axis_size("rank") + lax.axis_index("rank")
    odd = 4 * lax.rem(device_at, groups) + 1
    shape = phases.shape[1:]
    cells = lax.broadcasted_iota(jnp.int32, shape, 0) * LANES
    cells = cells + lax.broadcasted_iota(jnp.int32, shape, 1)
    turns = (cells * odd) & (4 * width - 1)
    turns = jnp.where(turns >= 2 * width, turns - 4 * width, turns)
    angles = turns.astype(jnp.float32) * (2.0 * math.pi / (4 * width))
    phases[0] = jnp.cos(angles)
    phases[1] = -jnp.sin(angles)


def made_factors(columns, phases, kept):
    terms = columns[0].shape[0]

    def factors_at(lane, first):
        place = pl.ds(pl.multiple_of(lane, LANES), LANES)
        if not first:
            return [kept[k, :, place] for k in range(4)]
        turn = pl.ds(lax.div(lane, LANES), 1)
        factors = [
            column[:, place] * jnp.broadcast_to(phases[part, turn, :], (terms, LANES))
            for column in columns
            for part in range(2)
        ]
        for k in range(4):
            kept[k, :, place] = factors[k]
        return factors

    return factors_at


def start_tables(tables, held, arrivals):
    copies = [
        pltpu.make_async_copy(table, place, arrivals.at[k])
        for k, (table, place) in enumerate(zip(tables, held))
    ]
    for copy in copies:
        copy.start()
    return copies


def pieces_kernel(blocks, groups, sources, count, *refs):
    pieces, refs = refs[:count], refs[count:]
    columns, row_factors, tables, refs = refs[0:2], refs[2:4], refs[4:6], refs[6:]
    out, partial, joined, phases, weights, twiddle, table, arrivals = refs
    copies = start_tables(tables, (twiddle, table), arrivals)
    make_phases(groups, phases)
    rows_here = pieces[0].shape[-2]
    terms, width = columns[0].shape
    ranks = lax.axis_size("rank")
    span = width // ranks
    rank_at = lax.axis_index("rank")
    starts = [(rank_at ^ other) * span for other in HELD_PARTS]
    rows = len(sources) * rows_here

    def fetch(part, row, lane):
        quarters, index, _, _ = sources[row // rows_here]
        row = pl.ds(row % rows_here, 1)
        ref = pieces[quarters[part]]
        if index is None:
            return ref[row, pl.ds(pl.multiple_of(starts[part] + lane, LANES), LANES)]
        return ref[index, row, pl.ds(pl.multiple_of(lane, LANES), LANES)]

    bases = [comp_of(step, flipped) * rows_here for _, _, step, flipped in sources]

    def row_at(row):
        return bases[row // rows_here] + row % rows_here

    factors_at = made_factors(columns, phases, weights)
    reduce_rows(blocks, rows, terms, fetch, factors_at, starts, span, partial)
    for copy in copies:
        copy.wait()
    transform_rows(blocks, rows, row_at, row_factors, twiddle, table, out, partial, joined)


def gathered_kernel(blocks, groups, pieces, *refs):
    columns, row_factors, tables, refs = refs[0:2], refs[2:4], refs[4:6], refs[6:]
    out, partial, joined, phases, weights, twiddle, table, arrivals = refs
    copies = start_tables(tables, (twiddle, table), arrivals)
    make_phases(groups, phases)
    parts, rows_here, span = pieces.shape[1:]

    def fetch(part, row, lane):
        place = pl.ds(pl.multiple_of(lane, LANES), LANES)
        return pieces[row // rows_here, part, pl.ds(row % rows_here, 1), place]

    base = pl.program_id(0) * 8
    starts = [part * span for part in range(parts)]
    terms = columns[0].shape[0]
    factors_at = made_factors(columns, phases, weights)
    reduce_rows(blocks, 8, terms, fetch, factors_at, starts, span, partial)
    for copy in copies:
        copy.wait()
    transform_rows(
        blocks,
        8,
        lambda row: base + row,
        row_factors,
        twiddle,
        table,
        out.at[0],
        partial,
        joined,
    )


def pass_kernel(value, earlier, out):
    del value, earlier, out


def after(value, earlier):
    anywhere = pl.BlockSpec(memory_space=pl.ANY)
    return pl.pallas_call(
        pass_kernel,
        out_shape=jax.ShapeDtypeStruct(value.shape, value.dtype),
        in_specs=[anywhere, anywhere],
        out_specs=anywhere,
        input_output_aliases={0: 0},
    )(*[pltpu.with_memory_space_constraint(array, pltpu.VMEM) for array in (value, earlier)])


def convolve_kernel(blocks, rows_here, layout, tile_count, *refs):
    tiles = refs[:tile_count]
    back, out, spectrum, product, mixed = refs[tile_count:]
    total_rows = spectrum.shape[2] - PAD
    terms = spectrum.shape[3]
    spectrum[:, :, pl.ds(0, PAD)] = jnp.zeros((2 * blocks, 3, PAD, terms, LANES), jnp.float32)
    moves = []
    for number, tile in enumerate(tiles):
        for at in range(tile.shape[0]):
            for first in range(0, tile.shape[3], rows_here):
                moves.append((tile, at, first))
    comps = [comp_of(*layout[k]) if layout else k for k in range(len(moves))]

    def collect(plane, carry):
        for (tile, at, first), comp in zip(moves, comps):
            real = tile[at, plane, 0, pl.ds(first, rows_here)]
            imag = tile[at, plane, 1, pl.ds(first, rows_here)]
            place = pl.ds(PAD + comp * rows_here, rows_here)
            spectrum[plane, 0, place] = real
            spectrum[plane, 1, place] = imag
            spectrum[plane, 2, place] = real + imag
        return carry

    lax.fori_loop(0, 2 * blocks, collect, 0)

    def step(at, sums, block, out_tile, whole):
        sums = list(sums)
        left_base = PAD + 4 * at
        right_base = PAD + 4 * (out_tile - at)
        for part in range(3):
            left = [spectrum[2 * block, part, left_base + k] for k in range(4)]
            right = {
                k: spectrum[2 * block + 1, part, right_base + k]
                for k in range(-3 if whole else 0, 4)
            }
            for row in range(4):
                for k in range(4 if whole else row + 1):
                    sums[row * 3 + part] += left[k] * right[row - k]
        return tuple(sums)

    def finish(sums, block, out_tile):
        for row in range(4):
            both_real, both_imag, crossed = sums[row * 3 : row * 3 + 3]
            base = (out_tile * 4 + row) * 2 * blocks + block
            product[base] = both_real - both_imag
            product[base + blocks] = crossed - both_real - both_imag

    zeros = (jnp.zeros((terms, LANES), jnp.float32),) * 12
    out_tiles = total_rows // 4

    def convolve_block(block, carry):
        for out_tile in range(out_tiles):
            sums = zeros
            for at in range(out_tile + 1):
                sums = step(at, sums, block, out_tile, at < out_tile)
            finish(sums, block, out_tile)
        return carry

    def convolve_tile(index, carry):
        block = lax.rem(index, blocks)
        out_tile = lax.div(index, blocks)
        sums = lax.fori_loop(
            0, out_tile + 1, lambda at, sums: step(at, sums, block, out_tile, True), zeros
        )
        finish(sums, block, out_tile)
        return carry

    if total_rows <= 32:
        lax.fori_loop(0, blocks, convolve_block, 0)
    else:
        lax.fori_loop(0, out_tiles * blocks, convolve_tile, 0)

    def gather_terms(at, carry):
        tiles = [product[at * 8 + k] for k in range(8)]
        summed = jnp.sum(jnp.stack(tiles), axis=1)
        if blocks == 4:
            turned = jnp.concatenate([summed[blocks:], -summed[:blocks]], axis=0)
        else:
            swapped = [
                tiles[k + blocks] if (k // blocks) % 2 == 0 else -tiles[k - blocks]
                for k in range(8)
            ]
            turned = jnp.sum(jnp.stack(swapped), axis=1)
        place = pl.ds(pl.multiple_of(at * 8, 8), 8)
        mixed[place, pl.ds(0, LANES)] = summed
        mixed[place, pl.ds(LANES, LANES)] = turned
        return carry

    lax.fori_loop(0, total_rows * 2 * blocks // 8, gather_terms, 0, unroll=4)
    out[...] = dot_split(mixed[...], back[...])


def final_kernel(scaling, spread, inner_cos, inner_sin, outer, out):
    values = spread[...]
    stacked = jnp.concatenate([values * inner_cos[...], values * inner_sin[...]], axis=0)
    high, low = split_parts(stacked)
    joined = jnp.concatenate([high, low, high], axis=0)
    total = jnp.dot(outer[...], joined, preferred_element_type=jnp.float32)
    out[...] = total * scaling


def whole_call(kernel, out_shapes, scratch, operands, tables=(), kept=True):
    out_type = pltpu.VMEM if kept else jax.ShapeDtypeStruct
    operands = [pltpu.with_memory_space_constraint(operand, pltpu.VMEM) for operand in operands]
    return pl.pallas_call(
        kernel,
        out_shape=[out_type(shape, jnp.float32) for shape in out_shapes],
        in_specs=[pl.BlockSpec(memory_space=pltpu.VMEM)] * len(operands)
        + [pl.BlockSpec(memory_space=pl.ANY)] * len(tables),
        out_specs=[pl.BlockSpec(memory_space=pltpu.VMEM)] * len(out_shapes),
        scratch_shapes=scratch,
        compiler_params=pltpu.CompilerParams(vmem_limit_bytes=VMEM_BYTES),
    )(*operands, *tables)


def row_scratch(blocks, rows, terms, width, tables):
    return [
        pltpu.VMEM((4, blocks, rows, terms, LANES), jnp.float32),
        pltpu.VMEM((2 * blocks * rows * terms, 6 * LANES), jnp.bfloat16),
        pltpu.VMEM((2, width // LANES, LANES), jnp.float32),
        pltpu.VMEM((4, terms, width), jnp.float32),
        *[pltpu.VMEM(table.shape, table.dtype) for table in tables],
        pltpu.SemaphoreType.DMA((len(tables),)),
    ]


def spectra_by_exchange(density, blocks, groups, columns, row_factors, tables):
    rows_here, width = density.shape
    comps, ranks = lax.axis_size("comp"), lax.axis_size("rank")
    part = width // ranks
    lines = comps // 2
    terms = row_factors[0].shape[0]
    mine = lax.dynamic_slice_in_dim(density, lax.axis_index("rank") * part, part, 1)

    def along(block, step):
        pairs = [(c, ((c // 2 + step) % lines) * 2 + c % 2) for c in range(comps)]
        return lax.ppermute(block, "comp", pairs)

    def across(block):
        return lax.ppermute(block, "comp", [(c, c ^ 1) for c in range(comps)])

    def swapped(block, other):
        return lax.ppermute(block, "rank", [(r, r ^ other) for r in range(ranks)])

    def spectra(pieces, sources):
        rows = rows_here * len(sources)
        (tile,) = whole_call(
            lambda *refs: pieces_kernel(blocks, groups, sources, len(pieces), *refs),
            [(2 * blocks, 2, rows, terms, LANES)],
            row_scratch(blocks, rows, terms, width, tables),
            (*pieces, *columns, *row_factors),
            tables,
        )
        return tile

    lined = [along(mine, step) for step in range(1, lines)]
    flipped_own = across(mine)
    line_near = jnp.stack(lined)
    near = jnp.concatenate([flipped_own[None], line_near])
    flipped_near = across(line_near)
    near_beyond = swapped(near, 2)
    ready = [near, near_beyond, swapped(near, 1), swapped(near_beyond, 1)]
    flipped_beyond = swapped(flipped_near, 2)
    flipped_beside = swapped(flipped_near, 1)

    quarters = (1, 2, 3, 4)
    early = [((0, 0, 0, 0), None, 0, False), (quarters, 0, 0, True)]
    early += [(quarters, step, step, False) for step in range(1, lines)]
    late = early[comps // 2 :]
    early = early[: comps // 2]
    first = spectra([density, *ready], early)
    flipped_beyond = after(flipped_beyond, first)
    flipped = [flipped_near, flipped_beyond, flipped_beside, swapped(flipped_beyond, 1)]
    late = [((0, 1, 2, 3), *rest) for _, *rest in late]
    late += [((4, 5, 6, 7), step - 1, step, True) for step in range(1, lines)]
    second = spectra([*ready, *flipped], late)
    layout = [source[2:] for source in early + late]
    return [first[None], second[None]], layout


def spectra_by_gather(density, blocks, groups, columns, row_factors, tables):
    rows_here, width = density.shape
    comps, ranks = lax.axis_size("comp"), lax.axis_size("rank")
    terms = row_factors[0].shape[0]
    total_rows = rows_here * comps
    part = width // ranks
    mine = lax.dynamic_slice_in_dim(density, lax.axis_index("rank") * part, part, 1)
    gathered = lax.all_gather(mine, AXES, axis=0).reshape(comps, ranks, rows_here, part)
    tile_shape = (2 * blocks, 2, 8, terms, LANES)
    spectra = pl.pallas_call(
        lambda *refs: gathered_kernel(blocks, groups, *refs),
        grid=(total_rows // 8,),
        out_shape=jax.ShapeDtypeStruct((total_rows // 8, *tile_shape), jnp.float32),
        in_specs=[pl.BlockSpec((8 // rows_here, ranks, rows_here, part), lambda t: (t, 0, 0, 0))]
        + [pl.BlockSpec(memory_space=pltpu.VMEM)] * 4
        + [pl.BlockSpec(memory_space=pl.ANY)] * len(tables),
        out_specs=pl.BlockSpec((1, *tile_shape), lambda t: (t, 0, 0, 0, 0, 0)),
        scratch_shapes=row_scratch(blocks, 8, terms, width, tables),
        compiler_params=pltpu.CompilerParams(vmem_limit_bytes=VMEM_BYTES),
    )(gathered, *columns, *row_factors, *tables)
    return [spectra], None


def body(density, row_left, col_left, row_right, col_right):
    rows_here, width = density.shape
    comps = lax.axis_size("comp")
    devices = comps * lax.axis_size("rank")
    total_rows = rows_here * comps
    terms = row_left.shape[0]
    groups = min(devices, width // LANES)
    term_groups = devices // groups
    blocks = width // (groups * LANES)
    device_at = lax.axis_index(AXES)
    if term_groups > 1:
        term_at = lax.broadcasted_iota(jnp.int32, (terms, 1), 0)
        chosen = lax.div(term_at, terms // term_groups) == lax.div(device_at, groups)
        col_left = jnp.where(chosen, col_left, 0.0)
        col_right = jnp.where(chosen, col_right, 0.0)
    columns = (col_left, col_right)
    row_factors = (row_left, row_right)
    tables = (block_twiddles(blocks), split_rows(forward_table()))
    spectra = spectra_by_exchange if comps <= 8 else spectra_by_gather
    tiles, layout = spectra(density, blocks, groups, columns, row_factors, tables)

    out_rows = total_rows * 2 * blocks
    (sent,) = whole_call(
        lambda *refs: convolve_kernel(blocks, rows_here, layout, len(tiles), *refs),
        [(out_rows, LANES)],
        [
            pltpu.VMEM((2 * blocks, 3, PAD + total_rows, terms, LANES), jnp.float32),
            pltpu.VMEM((out_rows, terms, LANES), jnp.float32),
            pltpu.VMEM((out_rows, 2 * LANES), jnp.float32),
        ],
        (*tiles, split_rows(inverse_table())),
    )
    spread = lax.all_to_all(sent, AXES, split_axis=0, concat_axis=0, tiled=True)
    inner_cos, inner_sin, outer_table = final_tables(devices, groups, blocks, width)
    scaling = 0.5 / (math.sqrt(total_rows * width) * width)
    (result,) = whole_call(
        lambda *refs: final_kernel(scaling, *refs),
        [(width // LANES, LANES)],
        [],
        (
            spread,
            jnp.asarray(inner_cos, jnp.float32),
            jnp.asarray(inner_sin, jnp.float32),
            split_columns(outer_table),
        ),
        kept=False,
    )
    return result.reshape(1, width)


def solution(mesh):
    return jax.shard_map(
        body,
        mesh=mesh,
        in_specs=(P("comp", None), P(), P(), P(), P()),
        out_specs=P(AXES, None),
        check_vma=False,
    )
```

```python
import math

import jax
import jax.numpy as jnp
import numpy as np
from jax import lax
from jax.experimental import pallas as pl
from jax.experimental.pallas import tpu as pltpu
from jax.sharding import PartitionSpec as P

LANES = 128
VMEM_BYTES = 16 * 1024 * 1024
AXES = ("comp", "rank")
PAD = 4
HELD_PARTS = (0, 2, 1, 3)


def split_parts(values):
    high = values.astype(jnp.bfloat16)
    low = (values - high.astype(jnp.float32)).astype(jnp.bfloat16)
    return high, low


def split_rows(table):
    high, low = split_parts(jnp.asarray(table, jnp.float32))
    return jnp.concatenate([high, high, low], axis=0)


def split_columns(table):
    high, low = split_parts(jnp.asarray(table, jnp.float32))
    return jnp.concatenate([high, high, low], axis=1)


def dot_split(rows, table):
    high, low = split_parts(rows)
    joined = jnp.concatenate([high, low, high], axis=1)
    return jnp.dot(joined, table, preferred_element_type=jnp.float32)


def forward_table():
    angles = 2.0 * np.pi * np.outer(np.arange(LANES), np.arange(LANES)) / LANES
    cosine, sine = np.cos(angles), np.sin(angles)
    return np.block([[cosine, -sine], [sine, cosine]])


def inverse_table():
    angles = 2.0 * np.pi * np.outer(np.arange(LANES), np.arange(LANES)) / LANES
    return np.concatenate([np.cos(angles), -np.sin(angles)], axis=0)


def block_twiddles(blocks):
    angles = 2.0 * np.pi * np.outer(np.arange(blocks), np.arange(LANES)) / (blocks * LANES)
    table = np.stack([np.cos(angles), -np.sin(angles)], axis=1)
    return jnp.asarray(
        np.broadcast_to(table[:, :, None, :], (blocks, 2, 8, LANES)), jnp.float32
    )


def final_tables(devices, groups, blocks, width):
    owner = np.arange(devices) % groups
    frequency = (owner[:, None] + groups * np.arange(blocks)[None, :]).astype(np.float64) + 0.25
    frequency = np.broadcast_to(frequency[:, None, :], (devices, 2, blocks))
    inner = 2.0 * np.pi * frequency[..., None] * np.arange(LANES) / width
    rows = devices * 2 * blocks
    inner_cos = np.cos(inner).reshape(rows, LANES)
    inner_sin = np.sin(inner).reshape(rows, LANES)
    outer_count = width // LANES
    outer = 2.0 * np.pi * frequency * LANES / width
    outer = np.arange(outer_count)[:, None] * outer.reshape(1, rows)
    is_real = np.broadcast_to(np.array([True, False])[None, :, None], (devices, 2, blocks))
    is_real = is_real.reshape(1, rows)
    with_cos = np.where(is_real, np.cos(outer), -np.sin(outer))
    with_sin = np.where(is_real, -np.sin(outer), -np.cos(outer))
    return inner_cos, inner_sin, np.concatenate([with_cos, with_sin], axis=1)


def block_fourier(reals, imags):
    count = len(reals)
    if count == 1:
        return reals, imags
    if count == 2:
        return (
            [reals[0] + reals[1], reals[0] - reals[1]],
            [imags[0] + imags[1], imags[0] - imags[1]],
        )
    even_real, odd_real = reals[0] + reals[2], reals[0] - reals[2]
    even_imag, odd_imag = imags[0] + imags[2], imags[0] - imags[2]
    pair_real, gap_real = reals[1] + reals[3], reals[1] - reals[3]
    pair_imag, gap_imag = imags[1] + imags[3], imags[1] - imags[3]
    return (
        [even_real + pair_real, odd_real + gap_imag, even_real - pair_real, odd_real - gap_imag],
        [even_imag + pair_imag, odd_imag - gap_real, even_imag - pair_imag, odd_imag + gap_real],
    )


def reduce_rows(blocks, rows, terms, fetch, factors_at, starts, span, partial):
    inner = blocks * LANES
    outer = span // inner
    unroll = math.gcd(16, outer)

    def reduce_block(block, first, count):
        sums = (jnp.zeros((terms, LANES), jnp.float32),) * (4 * count)
        for part, start in enumerate(starts):

            def step(at, sums, part=part, start=start):
                sums = list(sums)
                for extra in range(unroll):
                    lane = (at * unroll + extra) * inner + block * LANES
                    factors = factors_at(start + lane, first == 0)
                    for row in range(count):
                        value = fetch(part, first + row, lane)
                        value = jnp.broadcast_to(value, (terms, LANES))
                        for k in range(4):
                            sums[row * 4 + k] += value * factors[k]
                return tuple(sums)

            sums = lax.fori_loop(0, outer // unroll, step, sums)
        for row in range(count):
            for k in range(4):
                partial[k, block, first + row] = sums[row * 4 + k]

    for first in range(0, rows, 8):

        def reduce_tile(block, carry, first=first):
            reduce_block(block, first, min(8, rows - first))
            return carry

        lax.fori_loop(0, blocks, reduce_tile, 0)


def transform_rows(blocks, rows, row_at, row_factors, twiddle, table, out, partial, joined):
    terms, total_rows = row_factors[0].shape
    lanes = lax.broadcasted_iota(jnp.int32, (terms, total_rows), 1)

    def butterfly(row, side):
        picked = jnp.where(lanes == row_at(row), row_factors[side][...], 0.0)
        factor = jnp.sum(picked, axis=1, keepdims=True)
        factor = jnp.broadcast_to(factor, (terms, LANES))
        reals = [partial[2 * side, block, row] * factor for block in range(blocks)]
        imags = [partial[2 * side + 1, block, row] * factor for block in range(blocks)]
        reals, imags = block_fourier(reals, imags)
        for block in range(1, blocks):
            real, imag = reals[block], imags[block]
            cosine, sine = twiddle[block, 0], twiddle[block, 1]
            reals[block] = real * cosine - imag * sine
            imags[block] = real * sine + imag * cosine
        return reals, imags

    def butterfly_pair(pair):
        for side in range(2):
            both = [butterfly(pair * 2 + extra, side) for extra in range(2)]
            for block in range(blocks):
                base = ((block * 2 + side) * rows + pair * 2) * terms
                place = pl.ds(base, 2 * terms)
                for part in range(2):
                    values = jnp.concatenate([both[0][part][block], both[1][part][block]], axis=0)
                    high, low = split_parts(values)
                    for third, piece in enumerate((high, low, high)):
                        joined[place, pl.ds((third * 2 + part) * LANES, LANES)] = piece

    for pair in range(rows // 2):
        butterfly_pair(pair)
    planes = 2 * blocks
    step = planes * rows * terms
    while step > 512:
        step //= 2
    plane_step = step // (rows * terms)

    def transform(at, carry):
        place = pl.ds(pl.multiple_of(at * step, 16), step)
        total = jnp.dot(joined[place, :], table[...], preferred_element_type=jnp.float32)
        total = total.reshape(plane_step, rows, terms, 2 * LANES)
        place = pl.ds(at * plane_step, plane_step)
        out[place, 0] = total[..., :LANES]
        out[place, 1] = total[..., LANES:]
        return carry

    lax.fori_loop(0, planes // plane_step, transform, 0)


def comp_of(step, flipped):
    lines = lax.axis_size("comp") // 2
    comp_at = lax.axis_index("comp")
    line = lax.rem(lax.div(comp_at, 2) + lines - step, lines)
    side = lax.rem(comp_at, 2)
    return line * 2 + (1 - side if flipped else side)


def make_phases(groups, phases):
    width = phases.shape[1] * LANES
    device_at = lax.axis_index("comp") * lax.axis_size("rank") + lax.axis_index("rank")
    odd = 4 * lax.rem(device_at, groups) + 1
    shape = phases.shape[1:]
    cells = lax.broadcasted_iota(jnp.int32, shape, 0) * LANES
    cells = cells + lax.broadcasted_iota(jnp.int32, shape, 1)
    turns = (cells * odd) & (4 * width - 1)
    turns = jnp.where(turns >= 2 * width, turns - 4 * width, turns)
    angles = turns.astype(jnp.float32) * (2.0 * math.pi / (4 * width))
    phases[0] = jnp.cos(angles)
    phases[1] = -jnp.sin(angles)


def made_factors(columns, phases, kept):
    terms = columns[0].shape[0]

    def factors_at(lane, first):
        place = pl.ds(pl.multiple_of(lane, LANES), LANES)
        if not first:
            return [kept[k, :, place] for k in range(4)]
        turn = pl.ds(lax.div(lane, LANES), 1)
        factors = [
            column[:, place] * jnp.broadcast_to(phases[part, turn, :], (terms, LANES))
            for column in columns
            for part in range(2)
        ]
        for k in range(4):
            kept[k, :, place] = factors[k]
        return factors

    return factors_at


def start_tables(tables, held, arrivals):
    copies = [
        pltpu.make_async_copy(table, place, arrivals.at[k])
        for k, (table, place) in enumerate(zip(tables, held))
    ]
    for copy in copies:
        copy.start()
    return copies


def pieces_kernel(blocks, groups, sources, count, *refs):
    pieces, refs = refs[:count], refs[count:]
    columns, row_factors, tables, refs = refs[0:2], refs[2:4], refs[4:6], refs[6:]
    out, partial, joined, phases, weights, twiddle, table, arrivals = refs
    copies = start_tables(tables, (twiddle, table), arrivals)
    make_phases(groups, phases)
    rows_here = pieces[0].shape[-2]
    terms, width = columns[0].shape
    ranks = lax.axis_size("rank")
    span = width // ranks
    rank_at = lax.axis_index("rank")
    starts = [(rank_at ^ other) * span for other in HELD_PARTS]
    rows = len(sources) * rows_here

    def fetch(part, row, lane):
        quarters, index, _, _ = sources[row // rows_here]
        row = pl.ds(row % rows_here, 1)
        ref = pieces[quarters[part]]
        if index is None:
            return ref[row, pl.ds(pl.multiple_of(starts[part] + lane, LANES), LANES)]
        return ref[index, row, pl.ds(pl.multiple_of(lane, LANES), LANES)]

    bases = [comp_of(step, flipped) * rows_here for _, _, step, flipped in sources]

    def row_at(row):
        return bases[row // rows_here] + row % rows_here

    factors_at = made_factors(columns, phases, weights)
    reduce_rows(blocks, rows, terms, fetch, factors_at, starts, span, partial)
    for copy in copies:
        copy.wait()
    transform_rows(blocks, rows, row_at, row_factors, twiddle, table, out, partial, joined)


def gathered_kernel(blocks, groups, pieces, *refs):
    columns, row_factors, tables, refs = refs[0:2], refs[2:4], refs[4:6], refs[6:]
    out, partial, joined, phases, weights, twiddle, table, arrivals = refs
    copies = start_tables(tables, (twiddle, table), arrivals)
    make_phases(groups, phases)
    parts, rows_here, span = pieces.shape[1:]

    def fetch(part, row, lane):
        place = pl.ds(pl.multiple_of(lane, LANES), LANES)
        return pieces[row // rows_here, part, pl.ds(row % rows_here, 1), place]

    base = pl.program_id(0) * 8
    starts = [part * span for part in range(parts)]
    terms = columns[0].shape[0]
    factors_at = made_factors(columns, phases, weights)
    reduce_rows(blocks, 8, terms, fetch, factors_at, starts, span, partial)
    for copy in copies:
        copy.wait()
    transform_rows(
        blocks,
        8,
        lambda row: base + row,
        row_factors,
        twiddle,
        table,
        out.at[0],
        partial,
        joined,
    )


def pass_kernel(value, earlier, out):
    del value, earlier, out


def after(value, earlier):
    anywhere = pl.BlockSpec(memory_space=pl.ANY)
    return pl.pallas_call(
        pass_kernel,
        out_shape=jax.ShapeDtypeStruct(value.shape, value.dtype),
        in_specs=[anywhere, anywhere],
        out_specs=anywhere,
        input_output_aliases={0: 0},
    )(*[pltpu.with_memory_space_constraint(array, pltpu.VMEM) for array in (value, earlier)])


def convolve_kernel(blocks, rows_here, layout, by_rank, tile_count, *refs):
    tiles = refs[:tile_count]
    back, out, spectrum, product, mixed = refs[tile_count:]
    total_rows = spectrum.shape[2] - PAD
    terms = spectrum.shape[3]
    spectrum[:, :, pl.ds(0, PAD)] = jnp.zeros((2 * blocks, 3, PAD, terms, LANES), jnp.float32)
    moves = []
    for number, tile in enumerate(tiles):
        for at in range(tile.shape[0]):
            for first in range(0, tile.shape[3], rows_here):
                moves.append((tile, at, first))
    comps = [comp_of(*layout[k]) if layout else k for k in range(len(moves))]

    def collect(plane, carry):
        for (tile, at, first), comp in zip(moves, comps):
            real = tile[at, plane, 0, pl.ds(first, rows_here)]
            imag = tile[at, plane, 1, pl.ds(first, rows_here)]
            place = pl.ds(PAD + comp * rows_here, rows_here)
            spectrum[plane, 0, place] = real
            spectrum[plane, 1, place] = imag
            spectrum[plane, 2, place] = real + imag
        return carry

    lax.fori_loop(0, 2 * blocks, collect, 0)

    def step(at, sums, block, out_tile, whole):
        sums = list(sums)
        left_base = PAD + 4 * at
        right_base = PAD + 4 * (out_tile - at)
        for part in range(3):
            left = [spectrum[2 * block, part, left_base + k] for k in range(4)]
            right = {
                k: spectrum[2 * block + 1, part, right_base + k]
                for k in range(-3 if whole else 0, 4)
            }
            for row in range(4):
                for k in range(4 if whole else row + 1):
                    sums[row * 3 + part] += left[k] * right[row - k]
        return tuple(sums)

    def finish(sums, block, out_tile):
        for row in range(4):
            both_real, both_imag, crossed = sums[row * 3 : row * 3 + 3]
            base = (out_tile * 4 + row) * 2 * blocks + block
            product[base] = both_real - both_imag
            product[base + blocks] = crossed - both_real - both_imag

    zeros = (jnp.zeros((terms, LANES), jnp.float32),) * 12
    out_tiles = total_rows // 4

    def convolve_block(block, carry):
        for out_tile in range(out_tiles):
            sums = zeros
            for at in range(out_tile + 1):
                sums = step(at, sums, block, out_tile, at < out_tile)
            finish(sums, block, out_tile)
        return carry

    def convolve_tile(index, carry):
        block = lax.rem(index, blocks)
        out_tile = lax.div(index, blocks)
        sums = lax.fori_loop(
            0, out_tile + 1, lambda at, sums: step(at, sums, block, out_tile, True), zeros
        )
        finish(sums, block, out_tile)
        return carry

    if total_rows <= 32:
        lax.fori_loop(0, blocks, convolve_block, 0)
    else:
        lax.fori_loop(0, out_tiles * blocks, convolve_tile, 0)

    def gather_terms(at, carry):
        tiles = [product[at * 8 + k] for k in range(8)]
        summed = jnp.sum(jnp.stack(tiles), axis=1)
        if blocks == 4:
            turned = jnp.concatenate([summed[blocks:], -summed[:blocks]], axis=0)
        else:
            swapped = [
                tiles[k + blocks] if (k // blocks) % 2 == 0 else -tiles[k - blocks]
                for k in range(8)
            ]
            turned = jnp.sum(jnp.stack(swapped), axis=1)
        if by_rank:
            ranks = lax.axis_size("rank")
            at = lax.rem(at, ranks) * (total_rows // ranks) + lax.div(at, ranks)
        place = pl.ds(pl.multiple_of(at * 8, 8), 8)
        mixed[place, pl.ds(0, LANES)] = summed
        mixed[place, pl.ds(LANES, LANES)] = turned
        return carry

    lax.fori_loop(0, total_rows * 2 * blocks // 8, gather_terms, 0, unroll=4)
    out[...] = dot_split(mixed[...], back[...])


def final_kernel(scaling, spread, inner_cos, inner_sin, outer, out):
    values = spread[...]
    stacked = jnp.concatenate([values * inner_cos[...], values * inner_sin[...]], axis=0)
    high, low = split_parts(stacked)
    joined = jnp.concatenate([high, low, high], axis=0)
    total = jnp.dot(outer[...], joined, preferred_element_type=jnp.float32)
    out[...] = total * scaling


def in_hbm(array):
    return pltpu.with_memory_space_constraint(array, pltpu.HBM)


def whole_call(kernel, out_shapes, scratch, operands, tables=(), kept=True):
    out_type = pltpu.VMEM if kept else jax.ShapeDtypeStruct
    operands = [pltpu.with_memory_space_constraint(operand, pltpu.VMEM) for operand in operands]
    return pl.pallas_call(
        kernel,
        out_shape=[out_type(shape, jnp.float32) for shape in out_shapes],
        in_specs=[pl.BlockSpec(memory_space=pltpu.VMEM)] * len(operands)
        + [pl.BlockSpec(memory_space=pltpu.HBM)] * len(tables),
        out_specs=[pl.BlockSpec(memory_space=pltpu.VMEM)] * len(out_shapes),
        scratch_shapes=scratch,
        compiler_params=pltpu.CompilerParams(vmem_limit_bytes=VMEM_BYTES),
    )(*operands, *[in_hbm(table) for table in tables])


def row_scratch(blocks, rows, terms, width, tables):
    return [
        pltpu.VMEM((4, blocks, rows, terms, LANES), jnp.float32),
        pltpu.VMEM((2 * blocks * rows * terms, 6 * LANES), jnp.bfloat16),
        pltpu.VMEM((2, width // LANES, LANES), jnp.float32),
        pltpu.VMEM((4, terms, width), jnp.float32),
        *[pltpu.VMEM(table.shape, table.dtype) for table in tables],
        pltpu.SemaphoreType.DMA((len(tables),)),
    ]


def spectra_by_exchange(density, blocks, groups, columns, row_factors, tables):
    rows_here, width = density.shape
    comps, ranks = lax.axis_size("comp"), lax.axis_size("rank")
    part = width // ranks
    lines = comps // 2
    terms = row_factors[0].shape[0]
    mine = lax.dynamic_slice_in_dim(density, lax.axis_index("rank") * part, part, 1)

    def along(block, step):
        pairs = [(c, ((c // 2 + step) % lines) * 2 + c % 2) for c in range(comps)]
        return lax.ppermute(block, "comp", pairs)

    def across(block):
        return lax.ppermute(block, "comp", [(c, c ^ 1) for c in range(comps)])

    def swapped(block, other):
        return lax.ppermute(block, "rank", [(r, r ^ other) for r in range(ranks)])

    def spectra(pieces, sources):
        rows = rows_here * len(sources)
        (tile,) = whole_call(
            lambda *refs: pieces_kernel(blocks, groups, sources, len(pieces), *refs),
            [(2 * blocks, 2, rows, terms, LANES)],
            row_scratch(blocks, rows, terms, width, tables),
            (*pieces, *columns, *row_factors),
            tables,
        )
        return tile

    lined = [along(mine, step) for step in range(1, lines)]
    own_source = ((0, 0, 0, 0), None, 0, False)
    own = spectra([density], [own_source])
    flipped_own = after(across(mine), own)
    line_near = jnp.stack(lined)
    near = jnp.concatenate([flipped_own[None], line_near])
    flipped_near = across(line_near)
    near_beyond = swapped(near, 2)
    ready = [near, near_beyond, swapped(near, 1), swapped(near_beyond, 1)]
    flipped_beyond = swapped(flipped_near, 2)
    flipped_beside = swapped(flipped_near, 1)

    quarters = (0, 1, 2, 3)
    early = [(quarters, 0, 0, True)]
    early += [(quarters, step, step, False) for step in range(1, lines)]
    late = [(quarters, step - 1, step, True) for step in range(1, lines)]
    first = spectra(ready, early)
    flipped_beyond = after(flipped_beyond, first)
    flipped = [flipped_near, flipped_beyond, flipped_beside, swapped(flipped_beyond, 1)]
    second = spectra(flipped, late)
    layout = [source[2:] for source in [own_source] + early + late]
    return [own[None], first[None], second[None]], layout


def spectra_by_gather(density, blocks, groups, columns, row_factors, tables):
    rows_here, width = density.shape
    comps, ranks = lax.axis_size("comp"), lax.axis_size("rank")
    terms = row_factors[0].shape[0]
    total_rows = rows_here * comps
    part = width // ranks
    mine = lax.dynamic_slice_in_dim(density, lax.axis_index("rank") * part, part, 1)
    gathered = lax.all_gather(mine, AXES, axis=0).reshape(comps, ranks, rows_here, part)
    tile_shape = (2 * blocks, 2, 8, terms, LANES)
    spectra = pl.pallas_call(
        lambda *refs: gathered_kernel(blocks, groups, *refs),
        grid=(total_rows // 8,),
        out_shape=jax.ShapeDtypeStruct((total_rows // 8, *tile_shape), jnp.float32),
        in_specs=[pl.BlockSpec((8 // rows_here, ranks, rows_here, part), lambda t: (t, 0, 0, 0))]
        + [pl.BlockSpec(memory_space=pltpu.VMEM)] * 4
        + [pl.BlockSpec(memory_space=pltpu.HBM)] * len(tables),
        out_specs=pl.BlockSpec((1, *tile_shape), lambda t: (t, 0, 0, 0, 0, 0)),
        scratch_shapes=row_scratch(blocks, 8, terms, width, tables),
        compiler_params=pltpu.CompilerParams(vmem_limit_bytes=VMEM_BYTES),
    )(gathered, *columns, *row_factors, *[in_hbm(table) for table in tables])
    return [spectra], None


def body(density, row_left, col_left, row_right, col_right):
    rows_here, width = density.shape
    comps = lax.axis_size("comp")
    devices = comps * lax.axis_size("rank")
    total_rows = rows_here * comps
    terms = row_left.shape[0]
    groups = min(devices, width // LANES)
    term_groups = devices // groups
    blocks = width // (groups * LANES)
    device_at = lax.axis_index(AXES)
    if term_groups > 1:
        term_at = lax.broadcasted_iota(jnp.int32, (terms, 1), 0)
        chosen = lax.div(term_at, terms // term_groups) == lax.div(device_at, groups)
        col_left = jnp.where(chosen, col_left, 0.0)
        col_right = jnp.where(chosen, col_right, 0.0)
    columns = (col_left, col_right)
    row_factors = (row_left, row_right)
    tables = (block_twiddles(blocks), split_rows(forward_table()))
    spectra = spectra_by_exchange if comps <= 8 else spectra_by_gather
    tiles, layout = spectra(density, blocks, groups, columns, row_factors, tables)

    out_rows = total_rows * 2 * blocks
    by_rank = total_rows == devices and 2 * blocks == 8
    (sent,) = whole_call(
        lambda *refs: convolve_kernel(blocks, rows_here, layout, by_rank, len(tiles), *refs),
        [(out_rows, LANES)],
        [
            pltpu.VMEM((2 * blocks, 3, PAD + total_rows, terms, LANES), jnp.float32),
            pltpu.VMEM((out_rows, terms, LANES), jnp.float32),
            pltpu.VMEM((out_rows, 2 * LANES), jnp.float32),
        ],
        (*tiles, split_rows(inverse_table())),
    )
    if by_rank:
        ranks = devices // comps
        spread = lax.all_to_all(sent, "rank", split_axis=0, concat_axis=0, tiled=True)
        spread = spread.reshape(ranks, comps, 8, LANES).swapaxes(0, 1).reshape(out_rows, LANES)
        spread = lax.all_to_all(spread, "comp", split_axis=0, concat_axis=0, tiled=True)
    else:
        spread = lax.all_to_all(sent, AXES, split_axis=0, concat_axis=0, tiled=True)
    inner_cos, inner_sin, outer_table = final_tables(devices, groups, blocks, width)
    scaling = 0.5 / (math.sqrt(total_rows * width) * width)
    (result,) = whole_call(
        lambda *refs: final_kernel(scaling, *refs),
        [(width // LANES, LANES)],
        [],
        (
            spread,
            jnp.asarray(inner_cos, jnp.float32),
            jnp.asarray(inner_sin, jnp.float32),
            split_columns(outer_table),
        ),
        kept=False,
    )
    return result.reshape(1, width)


def solution(mesh):
    return jax.shard_map(
        body,
        mesh=mesh,
        in_specs=(P("comp", None), P(), P(), P(), P()),
        out_specs=P(AXES, None),
        check_vma=False,
    )
```

```python
import math

import jax
import jax.numpy as jnp
import numpy as np
from jax import lax
from jax.experimental import pallas as pl
from jax.experimental.pallas import tpu as pltpu
from jax.sharding import PartitionSpec as P

LANES = 128
VMEM_BYTES = 16 * 1024 * 1024
AXES = ("comp", "rank")
PAD = 4
HELD_PARTS = (0, 2, 1, 3)


def split_parts(values):
    high = values.astype(jnp.bfloat16)
    low = (values - high.astype(jnp.float32)).astype(jnp.bfloat16)
    return high, low


def split_rows(table):
    high, low = split_parts(jnp.asarray(table, jnp.float32))
    return jnp.concatenate([high, high, low], axis=0)


def split_columns(table):
    high, low = split_parts(jnp.asarray(table, jnp.float32))
    return jnp.concatenate([high, high, low], axis=1)


def dot_split(rows, table):
    high, low = split_parts(rows)
    joined = jnp.concatenate([high, low, high], axis=1)
    return jnp.dot(joined, table, preferred_element_type=jnp.float32)


def forward_table():
    angles = 2.0 * np.pi * np.outer(np.arange(LANES), np.arange(LANES)) / LANES
    cosine, sine = np.cos(angles), np.sin(angles)
    return np.block([[cosine, -sine], [sine, cosine]])


def inverse_table():
    angles = 2.0 * np.pi * np.outer(np.arange(LANES), np.arange(LANES)) / LANES
    return np.concatenate([np.cos(angles), -np.sin(angles)], axis=0)


def block_twiddles(blocks):
    angles = 2.0 * np.pi * np.outer(np.arange(blocks), np.arange(LANES)) / (blocks * LANES)
    table = np.stack([np.cos(angles), -np.sin(angles)], axis=1)
    return jnp.asarray(
        np.broadcast_to(table[:, :, None, :], (blocks, 2, 8, LANES)), jnp.float32
    )


def final_tables(devices, groups, blocks, width):
    owner = np.arange(devices) % groups
    frequency = (owner[:, None] + groups * np.arange(blocks)[None, :]).astype(np.float64) + 0.25
    frequency = np.broadcast_to(frequency[:, None, :], (devices, 2, blocks))
    inner = 2.0 * np.pi * frequency[..., None] * np.arange(LANES) / width
    rows = devices * 2 * blocks
    inner_cos = np.cos(inner).reshape(rows, LANES)
    inner_sin = np.sin(inner).reshape(rows, LANES)
    outer_count = width // LANES
    outer = 2.0 * np.pi * frequency * LANES / width
    outer = np.arange(outer_count)[:, None] * outer.reshape(1, rows)
    is_real = np.broadcast_to(np.array([True, False])[None, :, None], (devices, 2, blocks))
    is_real = is_real.reshape(1, rows)
    with_cos = np.where(is_real, np.cos(outer), -np.sin(outer))
    with_sin = np.where(is_real, -np.sin(outer), -np.cos(outer))
    return inner_cos, inner_sin, np.concatenate([with_cos, with_sin], axis=1)


def block_fourier(reals, imags):
    count = len(reals)
    if count == 1:
        return reals, imags
    if count == 2:
        return (
            [reals[0] + reals[1], reals[0] - reals[1]],
            [imags[0] + imags[1], imags[0] - imags[1]],
        )
    even_real, odd_real = reals[0] + reals[2], reals[0] - reals[2]
    even_imag, odd_imag = imags[0] + imags[2], imags[0] - imags[2]
    pair_real, gap_real = reals[1] + reals[3], reals[1] - reals[3]
    pair_imag, gap_imag = imags[1] + imags[3], imags[1] - imags[3]
    return (
        [even_real + pair_real, odd_real + gap_imag, even_real - pair_real, odd_real - gap_imag],
        [even_imag + pair_imag, odd_imag - gap_real, even_imag - pair_imag, odd_imag + gap_real],
    )


def reduce_rows(blocks, rows, terms, fetch, factors_at, starts, span, partial):
    inner = blocks * LANES
    outer = span // inner
    unroll = math.gcd(16, outer)

    def reduce_block(block, first, count):
        sums = (jnp.zeros((terms, LANES), jnp.float32),) * (4 * count)
        for part, start in enumerate(starts):

            def step(at, sums, part=part, start=start):
                sums = list(sums)
                for extra in range(unroll):
                    lane = (at * unroll + extra) * inner + block * LANES
                    factors = factors_at(start + lane, first == 0)
                    for row in range(count):
                        value = fetch(part, first + row, lane)
                        value = jnp.broadcast_to(value, (terms, LANES))
                        for k in range(4):
                            sums[row * 4 + k] += value * factors[k]
                return tuple(sums)

            sums = lax.fori_loop(0, outer // unroll, step, sums)
        for row in range(count):
            for k in range(4):
                partial[k, block, first + row] = sums[row * 4 + k]

    def reduce_tiles(block, carry):
        for first in range(0, rows, 8):
            reduce_block(block, first, min(8, rows - first))
        return carry

    lax.fori_loop(0, blocks, reduce_tiles, 0)


def transform_rows(blocks, rows, row_at, row_factors, twiddle, table, out, partial, joined):
    terms, total_rows = row_factors[0].shape
    lanes = lax.broadcasted_iota(jnp.int32, (terms, total_rows), 1)

    def butterfly(row, side):
        picked = jnp.where(lanes == row_at(row), row_factors[side][...], 0.0)
        factor = jnp.sum(picked, axis=1, keepdims=True)
        factor = jnp.broadcast_to(factor, (terms, LANES))
        reals = [partial[2 * side, block, row] * factor for block in range(blocks)]
        imags = [partial[2 * side + 1, block, row] * factor for block in range(blocks)]
        reals, imags = block_fourier(reals, imags)
        for block in range(1, blocks):
            real, imag = reals[block], imags[block]
            cosine, sine = twiddle[block, 0], twiddle[block, 1]
            reals[block] = real * cosine - imag * sine
            imags[block] = real * sine + imag * cosine
        return reals, imags

    def butterfly_pair(pair):
        for side in range(2):
            both = [butterfly(pair * 2 + extra, side) for extra in range(2)]
            for block in range(blocks):
                base = ((block * 2 + side) * rows + pair * 2) * terms
                place = pl.ds(base, 2 * terms)
                for part in range(2):
                    values = jnp.concatenate([both[0][part][block], both[1][part][block]], axis=0)
                    high, low = split_parts(values)
                    for third, piece in enumerate((high, low, high)):
                        joined[place, pl.ds((third * 2 + part) * LANES, LANES)] = piece

    for pair in range(rows // 2):
        butterfly_pair(pair)
    planes = 2 * blocks
    step = planes * rows * terms
    while step > 512:
        step //= 2
    plane_step = step // (rows * terms)

    def transform(at, carry):
        place = pl.ds(pl.multiple_of(at * step, 16), step)
        total = jnp.dot(joined[place, :], table[...], preferred_element_type=jnp.float32)
        total = total.reshape(plane_step, rows, terms, 2 * LANES)
        place = pl.ds(at * plane_step, plane_step)
        out[place, 0] = total[..., :LANES]
        out[place, 1] = total[..., LANES:]
        return carry

    lax.fori_loop(0, planes // plane_step, transform, 0)


def comp_of(step, flipped):
    lines = lax.axis_size("comp") // 2
    comp_at = lax.axis_index("comp")
    line = lax.rem(lax.div(comp_at, 2) + lines - step, lines)
    side = lax.rem(comp_at, 2)
    return line * 2 + (1 - side if flipped else side)


def make_phases(groups, phases):
    width = phases.shape[1] * LANES
    device_at = lax.axis_index("comp") * lax.axis_size("rank") + lax.axis_index("rank")
    odd = 4 * lax.rem(device_at, groups) + 1
    shape = phases.shape[1:]
    cells = lax.broadcasted_iota(jnp.int32, shape, 0) * LANES
    cells = cells + lax.broadcasted_iota(jnp.int32, shape, 1)
    turns = (cells * odd) & (4 * width - 1)
    turns = jnp.where(turns >= 2 * width, turns - 4 * width, turns)
    angles = turns.astype(jnp.float32) * (2.0 * math.pi / (4 * width))
    phases[0] = jnp.cos(angles)
    phases[1] = -jnp.sin(angles)


def made_factors(columns, phases, kept):
    terms = columns[0].shape[0]

    def factors_at(lane, first):
        place = pl.ds(pl.multiple_of(lane, LANES), LANES)
        if not first:
            return [kept[k, :, place] for k in range(4)]
        turn = pl.ds(lax.div(lane, LANES), 1)
        factors = [
            column[:, place] * jnp.broadcast_to(phases[part, turn, :], (terms, LANES))
            for column in columns
            for part in range(2)
        ]
        for k in range(4):
            kept[k, :, place] = factors[k]
        return factors

    return factors_at


def start_tables(tables, held, arrivals):
    copies = [
        pltpu.make_async_copy(table, place, arrivals.at[k])
        for k, (table, place) in enumerate(zip(tables, held))
    ]
    for copy in copies:
        copy.start()
    return copies


def pieces_kernel(blocks, groups, sources, count, *refs):
    pieces, refs = refs[:count], refs[count:]
    columns, row_factors, tables, refs = refs[0:2], refs[2:4], refs[4:6], refs[6:]
    out, partial, joined, phases, weights, twiddle, table, arrivals = refs
    copies = start_tables(tables, (twiddle, table), arrivals)
    make_phases(groups, phases)
    rows_here = pieces[0].shape[-2]
    terms, width = columns[0].shape
    ranks = lax.axis_size("rank")
    span = width // ranks
    rank_at = lax.axis_index("rank")
    starts = [(rank_at ^ other) * span for other in HELD_PARTS]
    rows = len(sources) * rows_here

    def fetch(part, row, lane):
        quarters, index, _, _ = sources[row // rows_here]
        row = pl.ds(row % rows_here, 1)
        ref = pieces[quarters[part]]
        if index is None:
            return ref[row, pl.ds(pl.multiple_of(starts[part] + lane, LANES), LANES)]
        return ref[index, row, pl.ds(pl.multiple_of(lane, LANES), LANES)]

    bases = [comp_of(step, flipped) * rows_here for _, _, step, flipped in sources]

    def row_at(row):
        return bases[row // rows_here] + row % rows_here

    factors_at = made_factors(columns, phases, weights)
    reduce_rows(blocks, rows, terms, fetch, factors_at, starts, span, partial)
    for copy in copies:
        copy.wait()
    transform_rows(blocks, rows, row_at, row_factors, twiddle, table, out, partial, joined)


def gathered_kernel(blocks, groups, pieces, *refs):
    columns, row_factors, tables, refs = refs[0:2], refs[2:4], refs[4:6], refs[6:]
    out, partial, joined, phases, weights, twiddle, table, arrivals = refs
    copies = start_tables(tables, (twiddle, table), arrivals)
    make_phases(groups, phases)
    parts, rows_here, span = pieces.shape[1:]

    def fetch(part, row, lane):
        place = pl.ds(pl.multiple_of(lane, LANES), LANES)
        return pieces[row // rows_here, part, pl.ds(row % rows_here, 1), place]

    base = pl.program_id(0) * 8
    starts = [part * span for part in range(parts)]
    terms = columns[0].shape[0]
    factors_at = made_factors(columns, phases, weights)
    reduce_rows(blocks, 8, terms, fetch, factors_at, starts, span, partial)
    for copy in copies:
        copy.wait()
    transform_rows(
        blocks,
        8,
        lambda row: base + row,
        row_factors,
        twiddle,
        table,
        out.at[0],
        partial,
        joined,
    )


def pass_kernel(value, earlier, out):
    del value, earlier, out


def after(value, earlier):
    anywhere = pl.BlockSpec(memory_space=pl.ANY)
    return pl.pallas_call(
        pass_kernel,
        out_shape=jax.ShapeDtypeStruct(value.shape, value.dtype),
        in_specs=[anywhere, anywhere],
        out_specs=anywhere,
        input_output_aliases={0: 0},
    )(*[pltpu.with_memory_space_constraint(array, pltpu.VMEM) for array in (value, earlier)])


def convolve_kernel(blocks, rows_here, layout, tile_count, *refs):
    tiles = refs[:tile_count]
    back, out, spectrum, product, mixed = refs[tile_count:]
    total_rows = spectrum.shape[2] - PAD
    terms = spectrum.shape[3]
    spectrum[:, :, pl.ds(0, PAD)] = jnp.zeros((2 * blocks, 3, PAD, terms, LANES), jnp.float32)
    moves = []
    for number, tile in enumerate(tiles):
        for at in range(tile.shape[0]):
            for first in range(0, tile.shape[3], rows_here):
                moves.append((tile, at, first))
    comps = [comp_of(*layout[k]) if layout else k for k in range(len(moves))]

    def collect(plane, carry):
        for (tile, at, first), comp in zip(moves, comps):
            real = tile[at, plane, 0, pl.ds(first, rows_here)]
            imag = tile[at, plane, 1, pl.ds(first, rows_here)]
            place = pl.ds(PAD + comp * rows_here, rows_here)
            spectrum[plane, 0, place] = real
            spectrum[plane, 1, place] = imag
            spectrum[plane, 2, place] = real + imag
        return carry

    lax.fori_loop(0, 2 * blocks, collect, 0)

    def step(at, sums, block, out_tile, whole):
        sums = list(sums)
        left_base = PAD + 4 * at
        right_base = PAD + 4 * (out_tile - at)
        for part in range(3):
            left = [spectrum[2 * block, part, left_base + k] for k in range(4)]
            right = {
                k: spectrum[2 * block + 1, part, right_base + k]
                for k in range(-3 if whole else 0, 4)
            }
            for row in range(4):
                for k in range(4 if whole else row + 1):
                    sums[row * 3 + part] += left[k] * right[row - k]
        return tuple(sums)

    def finish(sums, block, out_tile):
        for row in range(4):
            both_real, both_imag, crossed = sums[row * 3 : row * 3 + 3]
            base = (out_tile * 4 + row) * 2 * blocks + block
            product[base] = both_real - both_imag
            product[base + blocks] = crossed - both_real - both_imag

    zeros = (jnp.zeros((terms, LANES), jnp.float32),) * 12
    out_tiles = total_rows // 4

    def convolve_block(block, carry):
        for out_tile in range(out_tiles):
            sums = zeros
            for at in range(out_tile + 1):
                sums = step(at, sums, block, out_tile, at < out_tile)
            finish(sums, block, out_tile)
        return carry

    def convolve_tile(index, carry):
        block = lax.rem(index, blocks)
        out_tile = lax.div(index, blocks)
        sums = lax.fori_loop(
            0, out_tile + 1, lambda at, sums: step(at, sums, block, out_tile, True), zeros
        )
        finish(sums, block, out_tile)
        return carry

    if total_rows <= 32:
        lax.fori_loop(0, blocks, convolve_block, 0)
    else:
        lax.fori_loop(0, out_tiles * blocks, convolve_tile, 0)

    def gather_terms(at, carry):
        tiles = [product[at * 8 + k] for k in range(8)]
        summed = jnp.sum(jnp.stack(tiles), axis=1)
        if blocks == 4:
            turned = jnp.concatenate([summed[blocks:], -summed[:blocks]], axis=0)
        else:
            swapped = [
                tiles[k + blocks] if (k // blocks) % 2 == 0 else -tiles[k - blocks]
                for k in range(8)
            ]
            turned = jnp.sum(jnp.stack(swapped), axis=1)
        place = pl.ds(pl.multiple_of(at * 8, 8), 8)
        mixed[place, pl.ds(0, LANES)] = summed
        mixed[place, pl.ds(LANES, LANES)] = turned
        return carry

    lax.fori_loop(0, total_rows * 2 * blocks // 8, gather_terms, 0, unroll=4)
    out[...] = dot_split(mixed[...], back[...])


def final_kernel(scaling, spread, inner_cos, inner_sin, outer, out):
    values = spread[...]
    stacked = jnp.concatenate([values * inner_cos[...], values * inner_sin[...]], axis=0)
    high, low = split_parts(stacked)
    joined = jnp.concatenate([high, low, high], axis=0)
    total = jnp.dot(outer[...], joined, preferred_element_type=jnp.float32)
    out[...] = total * scaling


def in_hbm(array):
    return pltpu.with_memory_space_constraint(array, pltpu.HBM)


def whole_call(kernel, out_shapes, scratch, operands, tables=(), kept=True):
    out_type = pltpu.VMEM if kept else jax.ShapeDtypeStruct
    operands = [pltpu.with_memory_space_constraint(operand, pltpu.VMEM) for operand in operands]
    return pl.pallas_call(
        kernel,
        out_shape=[out_type(shape, jnp.float32) for shape in out_shapes],
        in_specs=[pl.BlockSpec(memory_space=pltpu.VMEM)] * len(operands)
        + [pl.BlockSpec(memory_space=pltpu.HBM)] * len(tables),
        out_specs=[pl.BlockSpec(memory_space=pltpu.VMEM)] * len(out_shapes),
        scratch_shapes=scratch,
        compiler_params=pltpu.CompilerParams(vmem_limit_bytes=VMEM_BYTES),
    )(*operands, *[in_hbm(table) for table in tables])


def row_scratch(blocks, rows, terms, width, tables):
    return [
        pltpu.VMEM((4, blocks, rows, terms, LANES), jnp.float32),
        pltpu.VMEM((2 * blocks * rows * terms, 6 * LANES), jnp.bfloat16),
        pltpu.VMEM((2, width // LANES, LANES), jnp.float32),
        pltpu.VMEM((4, terms, width), jnp.float32),
        *[pltpu.VMEM(table.shape, table.dtype) for table in tables],
        pltpu.SemaphoreType.DMA((len(tables),)),
    ]


def spectra_by_exchange(density, blocks, groups, columns, row_factors, tables):
    rows_here, width = density.shape
    comps, ranks = lax.axis_size("comp"), lax.axis_size("rank")
    part = width // ranks
    lines = comps // 2
    terms = row_factors[0].shape[0]
    mine = lax.dynamic_slice_in_dim(density, lax.axis_index("rank") * part, part, 1)

    def along(block, step):
        pairs = [(c, ((c // 2 + step) % lines) * 2 + c % 2) for c in range(comps)]
        return lax.ppermute(block, "comp", pairs)

    def across(block):
        return lax.ppermute(block, "comp", [(c, c ^ 1) for c in range(comps)])

    def swapped(block, other):
        return lax.ppermute(block, "rank", [(r, r ^ other) for r in range(ranks)])

    def spectra(pieces, sources):
        rows = rows_here * len(sources)
        (tile,) = whole_call(
            lambda *refs: pieces_kernel(blocks, groups, sources, len(pieces), *refs),
            [(2 * blocks, 2, rows, terms, LANES)],
            row_scratch(blocks, rows, terms, width, tables),
            (*pieces, *columns, *row_factors),
            tables,
        )
        return tile

    lined = [along(mine, step) for step in range(1, lines)]
    own_source = ((0, 0, 0, 0), None, 0, False)
    own = spectra([density], [own_source])
    flipped_own = after(across(mine), own)
    line_near = jnp.stack(lined)
    near = jnp.concatenate([flipped_own[None], line_near])
    flipped_near = across(line_near)
    near_beyond = swapped(near, 2)
    ready = [near, near_beyond, swapped(near, 1), swapped(near_beyond, 1)]
    flipped_beyond = swapped(flipped_near, 2)
    flipped_beside = swapped(flipped_near, 1)

    quarters = (0, 1, 2, 3)
    early = [(quarters, 0, 0, True)]
    early += [(quarters, step, step, False) for step in range(1, lines)]
    late = [(quarters, step - 1, step, True) for step in range(1, lines)]
    first = spectra(ready, early)
    flipped_beyond = after(flipped_beyond, first)
    flipped = [flipped_near, flipped_beyond, flipped_beside, swapped(flipped_beyond, 1)]
    second = spectra(flipped, late)
    layout = [source[2:] for source in [own_source] + early + late]
    return [own[None], first[None], second[None]], layout


def spectra_by_gather(density, blocks, groups, columns, row_factors, tables):
    rows_here, width = density.shape
    comps, ranks = lax.axis_size("comp"), lax.axis_size("rank")
    terms = row_factors[0].shape[0]
    total_rows = rows_here * comps
    part = width // ranks
    mine = lax.dynamic_slice_in_dim(density, lax.axis_index("rank") * part, part, 1)
    gathered = lax.all_gather(mine, AXES, axis=0).reshape(comps, ranks, rows_here, part)
    tile_shape = (2 * blocks, 2, 8, terms, LANES)
    spectra = pl.pallas_call(
        lambda *refs: gathered_kernel(blocks, groups, *refs),
        grid=(total_rows // 8,),
        out_shape=jax.ShapeDtypeStruct((total_rows // 8, *tile_shape), jnp.float32),
        in_specs=[pl.BlockSpec((8 // rows_here, ranks, rows_here, part), lambda t: (t, 0, 0, 0))]
        + [pl.BlockSpec(memory_space=pltpu.VMEM)] * 4
        + [pl.BlockSpec(memory_space=pltpu.HBM)] * len(tables),
        out_specs=pl.BlockSpec((1, *tile_shape), lambda t: (t, 0, 0, 0, 0, 0)),
        scratch_shapes=row_scratch(blocks, 8, terms, width, tables),
        compiler_params=pltpu.CompilerParams(vmem_limit_bytes=VMEM_BYTES),
    )(gathered, *columns, *row_factors, *[in_hbm(table) for table in tables])
    return [spectra], None


def body(density, row_left, col_left, row_right, col_right):
    rows_here, width = density.shape
    comps = lax.axis_size("comp")
    devices = comps * lax.axis_size("rank")
    total_rows = rows_here * comps
    terms = row_left.shape[0]
    groups = min(devices, width // LANES)
    term_groups = devices // groups
    blocks = width // (groups * LANES)
    device_at = lax.axis_index(AXES)
    if term_groups > 1:
        term_at = lax.broadcasted_iota(jnp.int32, (terms, 1), 0)
        chosen = lax.div(term_at, terms // term_groups) == lax.div(device_at, groups)
        col_left = jnp.where(chosen, col_left, 0.0)
        col_right = jnp.where(chosen, col_right, 0.0)
    columns = (col_left, col_right)
    row_factors = (row_left, row_right)
    tables = (block_twiddles(blocks), split_rows(forward_table()))
    spectra = spectra_by_exchange if comps <= 8 else spectra_by_gather
    tiles, layout = spectra(density, blocks, groups, columns, row_factors, tables)

    out_rows = total_rows * 2 * blocks
    (sent,) = whole_call(
        lambda *refs: convolve_kernel(blocks, rows_here, layout, len(tiles), *refs),
        [(out_rows, LANES)],
        [
            pltpu.VMEM((2 * blocks, 3, PAD + total_rows, terms, LANES), jnp.float32),
            pltpu.VMEM((out_rows, terms, LANES), jnp.float32),
            pltpu.VMEM((out_rows, 2 * LANES), jnp.float32),
        ],
        (*tiles, split_rows(inverse_table())),
    )
    spread = lax.all_to_all(sent, AXES, split_axis=0, concat_axis=0, tiled=True)
    inner_cos, inner_sin, outer_table = final_tables(devices, groups, blocks, width)
    scaling = 0.5 / (math.sqrt(total_rows * width) * width)
    (result,) = whole_call(
        lambda *refs: final_kernel(scaling, *refs),
        [(width // LANES, LANES)],
        [],
        (
            spread,
            jnp.asarray(inner_cos, jnp.float32),
            jnp.asarray(inner_sin, jnp.float32),
            split_columns(outer_table),
        ),
        kept=False,
    )
    return result.reshape(1, width)


def solution(mesh):
    return jax.shard_map(
        body,
        mesh=mesh,
        in_specs=(P("comp", None), P(), P(), P(), P()),
        out_specs=P(AXES, None),
        check_vma=False,
    )
```

```python
import math

import jax
import jax.numpy as jnp
import numpy as np
from jax import lax
from jax.experimental import pallas as pl
from jax.experimental.pallas import tpu as pltpu
from jax.sharding import PartitionSpec as P

LANES = 128
VMEM_BYTES = 16 * 1024 * 1024
AXES = ("comp", "rank")
PAD = 4


def split_parts(values):
    high = values.astype(jnp.bfloat16)
    low = (values - high.astype(jnp.float32)).astype(jnp.bfloat16)
    return high, low


def split_rows(table):
    high, low = split_parts(jnp.asarray(table, jnp.float32))
    return jnp.concatenate([high, high, low], axis=0)


def split_columns(table):
    high, low = split_parts(jnp.asarray(table, jnp.float32))
    return jnp.concatenate([high, high, low], axis=1)


def dot_split(rows, table):
    high, low = split_parts(rows)
    joined = jnp.concatenate([high, low, high], axis=1)
    return jnp.dot(joined, table, preferred_element_type=jnp.float32)


def forward_table():
    angles = 2.0 * np.pi * np.outer(np.arange(LANES), np.arange(LANES)) / LANES
    cosine, sine = np.cos(angles), np.sin(angles)
    return np.block([[cosine, -sine], [sine, cosine]])


def inverse_table():
    angles = 2.0 * np.pi * np.outer(np.arange(LANES), np.arange(LANES)) / LANES
    return np.concatenate([np.cos(angles), -np.sin(angles)], axis=0)


def block_twiddles(blocks):
    angles = 2.0 * np.pi * np.outer(np.arange(blocks), np.arange(LANES)) / (blocks * LANES)
    table = np.stack([np.cos(angles), -np.sin(angles)], axis=1)
    return jnp.asarray(
        np.broadcast_to(table[:, :, None, :], (blocks, 2, 8, LANES)), jnp.float32
    )


def final_tables(devices, groups, blocks, width):
    owner = np.arange(devices) % groups
    frequency = (owner[:, None] + groups * np.arange(blocks)[None, :]).astype(np.float64) + 0.25
    frequency = np.broadcast_to(frequency[:, None, :], (devices, 2, blocks))
    inner = 2.0 * np.pi * frequency[..., None] * np.arange(LANES) / width
    rows = devices * 2 * blocks
    inner_cos = np.cos(inner).reshape(rows, LANES)
    inner_sin = np.sin(inner).reshape(rows, LANES)
    outer_count = width // LANES
    outer = 2.0 * np.pi * frequency * LANES / width
    outer = np.arange(outer_count)[:, None] * outer.reshape(1, rows)
    is_real = np.broadcast_to(np.array([True, False])[None, :, None], (devices, 2, blocks))
    is_real = is_real.reshape(1, rows)
    with_cos = np.where(is_real, np.cos(outer), -np.sin(outer))
    with_sin = np.where(is_real, -np.sin(outer), -np.cos(outer))
    return inner_cos, inner_sin, np.concatenate([with_cos, with_sin], axis=1)


def block_fourier(reals, imags):
    count = len(reals)
    if count == 1:
        return reals, imags
    if count == 2:
        return (
            [reals[0] + reals[1], reals[0] - reals[1]],
            [imags[0] + imags[1], imags[0] - imags[1]],
        )
    even_real, odd_real = reals[0] + reals[2], reals[0] - reals[2]
    even_imag, odd_imag = imags[0] + imags[2], imags[0] - imags[2]
    pair_real, gap_real = reals[1] + reals[3], reals[1] - reals[3]
    pair_imag, gap_imag = imags[1] + imags[3], imags[1] - imags[3]
    return (
        [even_real + pair_real, odd_real + gap_imag, even_real - pair_real, odd_real - gap_imag],
        [even_imag + pair_imag, odd_imag - gap_real, even_imag - pair_imag, odd_imag + gap_real],
    )


def reduce_rows(blocks, rows, terms, fetch, factors_at, starts, span, partial):
    inner = blocks * LANES
    outer = span // inner
    unroll = math.gcd(16, outer)

    def reduce_block(block, first, count):
        sums = (jnp.zeros((terms, LANES), jnp.float32),) * (4 * count)
        for part, start in enumerate(starts):

            def step(at, sums, part=part, start=start):
                sums = list(sums)
                for extra in range(unroll):
                    lane = (at * unroll + extra) * inner + block * LANES
                    factors = factors_at(start + lane, first == 0)
                    for row in range(count):
                        value = fetch(part, first + row, lane)
                        value = jnp.broadcast_to(value, (terms, LANES))
                        for k in range(4):
                            sums[row * 4 + k] += value * factors[k]
                return tuple(sums)

            sums = lax.fori_loop(0, outer // unroll, step, sums)
        for row in range(count):
            for k in range(4):
                partial[k, block, first + row] = sums[row * 4 + k]

    def reduce_tiles(block, carry):
        for first in range(0, rows, 8):
            reduce_block(block, first, min(8, rows - first))
        return carry

    lax.fori_loop(0, blocks, reduce_tiles, 0)


def transform_rows(blocks, rows, row_at, row_factors, twiddle, table, out, partial, joined):
    terms, total_rows = row_factors[0].shape
    lanes = lax.broadcasted_iota(jnp.int32, (terms, total_rows), 1)

    def butterfly(row, side):
        picked = jnp.where(lanes == row_at(row), row_factors[side][...], 0.0)
        factor = jnp.sum(picked, axis=1, keepdims=True)
        factor = jnp.broadcast_to(factor, (terms, LANES))
        reals = [partial[2 * side, block, row] * factor for block in range(blocks)]
        imags = [partial[2 * side + 1, block, row] * factor for block in range(blocks)]
        reals, imags = block_fourier(reals, imags)
        for block in range(1, blocks):
            real, imag = reals[block], imags[block]
            cosine, sine = twiddle[block, 0], twiddle[block, 1]
            reals[block] = real * cosine - imag * sine
            imags[block] = real * sine + imag * cosine
        return reals, imags

    def butterfly_pair(pair):
        for side in range(2):
            both = [butterfly(pair * 2 + extra, side) for extra in range(2)]
            for block in range(blocks):
                base = ((block * 2 + side) * rows + pair * 2) * terms
                place = pl.ds(base, 2 * terms)
                for part in range(2):
                    values = jnp.concatenate([both[0][part][block], both[1][part][block]], axis=0)
                    high, low = split_parts(values)
                    for third, piece in enumerate((high, low, high)):
                        joined[place, pl.ds((third * 2 + part) * LANES, LANES)] = piece

    for pair in range(rows // 2):
        butterfly_pair(pair)
    planes = 2 * blocks
    step = planes * rows * terms
    while step > 512:
        step //= 2
    plane_step = step // (rows * terms)

    def transform(at, carry):
        place = pl.ds(pl.multiple_of(at * step, 16), step)
        total = jnp.dot(joined[place, :], table[...], preferred_element_type=jnp.float32)
        total = total.reshape(plane_step, rows, terms, 2 * LANES)
        place = pl.ds(at * plane_step, plane_step)
        out[place, 0] = total[..., :LANES]
        out[place, 1] = total[..., LANES:]
        return carry

    lax.fori_loop(0, planes // plane_step, transform, 0)


def comp_of(step, flipped):
    lines = lax.axis_size("comp") // 2
    comp_at = lax.axis_index("comp")
    line = lax.rem(lax.div(comp_at, 2) + lines - step, lines)
    side = lax.rem(comp_at, 2)
    return line * 2 + (1 - side if flipped else side)


def make_phases(groups, phases):
    width = phases.shape[1] * LANES
    device_at = lax.axis_index("comp") * lax.axis_size("rank") + lax.axis_index("rank")
    odd = 4 * lax.rem(device_at, groups) + 1
    shape = phases.shape[1:]
    cells = lax.broadcasted_iota(jnp.int32, shape, 0) * LANES
    cells = cells + lax.broadcasted_iota(jnp.int32, shape, 1)
    turns = (cells * odd) & (4 * width - 1)
    turns = jnp.where(turns >= 2 * width, turns - 4 * width, turns)
    angles = turns.astype(jnp.float32) * (2.0 * math.pi / (4 * width))
    phases[0] = jnp.cos(angles)
    phases[1] = -jnp.sin(angles)


def made_factors(columns, phases, kept):
    terms = columns[0].shape[0]

    def factors_at(lane, first):
        place = pl.ds(pl.multiple_of(lane, LANES), LANES)
        if not first:
            return [kept[k, :, place] for k in range(4)]
        turn = pl.ds(lax.div(lane, LANES), 1)
        factors = [
            column[:, place] * jnp.broadcast_to(phases[part, turn, :], (terms, LANES))
            for column in columns
            for part in range(2)
        ]
        for k in range(4):
            kept[k, :, place] = factors[k]
        return factors

    return factors_at


def start_tables(tables, held, arrivals):
    copies = [
        pltpu.make_async_copy(table, place, arrivals.at[k])
        for k, (table, place) in enumerate(zip(tables, held))
    ]
    for copy in copies:
        copy.start()
    return copies


def pieces_kernel(blocks, groups, sources, count, *refs):
    pieces, refs = refs[:count], refs[count:]
    columns, row_factors, tables, refs = refs[0:2], refs[2:4], refs[4:6], refs[6:]
    out, partial, joined, phases, weights, twiddle, table, arrivals = refs
    copies = start_tables(tables, (twiddle, table), arrivals)
    make_phases(groups, phases)
    reduce_pieces(blocks, sources, pieces, columns, phases, weights, partial)
    finish_pieces(
        blocks, sources, copies, row_factors, twiddle, table, out, partial, joined
    )


def own_kernel(blocks, groups, sources, *refs):
    row_factors, sent, refs = refs[0:2], refs[2:7], refs[7:]
    out, partial, joined, phases, weights = refs[:5]
    held, arrivals = refs[5:10], refs[10]
    copies = start_tables(sent, held, arrivals)
    make_phases(groups, phases)
    for copy in copies[2:]:
        copy.wait()
    twiddle, table, own, *columns = held
    reduce_pieces(blocks, sources, [own], columns, phases, weights, partial)
    finish_pieces(
        blocks, sources, copies[:2], row_factors, twiddle, table, out, partial, joined
    )


def reduce_pieces(blocks, sources, pieces, columns, phases, weights, partial):
    rows_here = pieces[0].shape[-2]
    terms, width = columns[0].shape
    span = width // 2
    core = lax.rem(lax.axis_index("rank"), 2)
    starts = [core * span, (1 - core) * span]

    def fetch(part, row, lane):
        halves, index, _, _ = sources[row // rows_here]
        row = pl.ds(row % rows_here, 1)
        ref = pieces[halves[part]]
        if index is None:
            return ref[row, pl.ds(pl.multiple_of(starts[part] + lane, LANES), LANES)]
        return ref[index, row, pl.ds(pl.multiple_of(lane, LANES), LANES)]

    factors_at = made_factors(columns, phases, weights)
    rows = len(sources) * rows_here
    reduce_rows(blocks, rows, terms, fetch, factors_at, starts, span, partial)


def finish_pieces(blocks, sources, copies, row_factors, twiddle, table, out, partial, joined):
    rows = partial.shape[2]
    rows_here = rows // len(sources)
    bases = [comp_of(step, flipped) * rows_here for _, _, step, flipped in sources]

    def row_at(row):
        return bases[row // rows_here] + row % rows_here

    for copy in copies:
        copy.wait()
    transform_rows(blocks, rows, row_at, row_factors, twiddle, table, out, partial, joined)


def gathered_kernel(blocks, groups, pieces, *refs):
    columns, row_factors, tables, refs = refs[0:2], refs[2:4], refs[4:6], refs[6:]
    out, partial, joined, phases, weights, twiddle, table, arrivals = refs
    copies = start_tables(tables, (twiddle, table), arrivals)
    make_phases(groups, phases)
    parts, rows_here, span = pieces.shape[1:]

    def fetch(part, row, lane):
        place = pl.ds(pl.multiple_of(lane, LANES), LANES)
        return pieces[row // rows_here, part, pl.ds(row % rows_here, 1), place]

    base = pl.program_id(0) * 8
    starts = [part * span for part in range(parts)]
    terms = columns[0].shape[0]
    factors_at = made_factors(columns, phases, weights)
    reduce_rows(blocks, 8, terms, fetch, factors_at, starts, span, partial)
    for copy in copies:
        copy.wait()
    transform_rows(
        blocks,
        8,
        lambda row: base + row,
        row_factors,
        twiddle,
        table,
        out.at[0],
        partial,
        joined,
    )


def pass_kernel(*refs):
    del refs


def after(values, earlier):
    anywhere = pl.BlockSpec(memory_space=pl.ANY)
    operands = [pltpu.with_memory_space_constraint(x, pltpu.VMEM) for x in (*values, earlier)]
    return pl.pallas_call(
        pass_kernel,
        out_shape=[jax.ShapeDtypeStruct(value.shape, value.dtype) for value in values],
        in_specs=[anywhere] * len(operands),
        out_specs=[anywhere] * len(values),
        input_output_aliases={k: k for k in range(len(values))},
    )(*operands)


def convolve_kernel(blocks, rows_here, layout, tile_count, *refs):
    tiles = refs[:tile_count]
    back, out, spectrum, product, mixed = refs[tile_count:]
    total_rows = spectrum.shape[2] - PAD
    terms = spectrum.shape[3]
    spectrum[:, :, pl.ds(0, PAD)] = jnp.zeros((2 * blocks, 3, PAD, terms, LANES), jnp.float32)
    moves = []
    for number, tile in enumerate(tiles):
        for at in range(tile.shape[0]):
            for first in range(0, tile.shape[3], rows_here):
                moves.append((tile, at, first))
    comps = [comp_of(*layout[k]) if layout else k for k in range(len(moves))]

    def collect(plane, carry):
        for (tile, at, first), comp in zip(moves, comps):
            real = tile[at, plane, 0, pl.ds(first, rows_here)]
            imag = tile[at, plane, 1, pl.ds(first, rows_here)]
            place = pl.ds(PAD + comp * rows_here, rows_here)
            spectrum[plane, 0, place] = real
            spectrum[plane, 1, place] = imag
            spectrum[plane, 2, place] = real + imag
        return carry

    lax.fori_loop(0, 2 * blocks, collect, 0)

    def step(at, sums, block, out_tile, whole):
        sums = list(sums)
        left_base = PAD + 4 * at
        right_base = PAD + 4 * (out_tile - at)
        for part in range(3):
            left = [spectrum[2 * block, part, left_base + k] for k in range(4)]
            right = {
                k: spectrum[2 * block + 1, part, right_base + k]
                for k in range(-3 if whole else 0, 4)
            }
            for row in range(4):
                for k in range(4 if whole else row + 1):
                    sums[row * 3 + part] += left[k] * right[row - k]
        return tuple(sums)

    def finish(sums, block, out_tile):
        for row in range(4):
            both_real, both_imag, crossed = sums[row * 3 : row * 3 + 3]
            base = (out_tile * 4 + row) * 2 * blocks + block
            product[base] = both_real - both_imag
            product[base + blocks] = crossed - both_real - both_imag

    zeros = (jnp.zeros((terms, LANES), jnp.float32),) * 12
    out_tiles = total_rows // 4

    def convolve_block(block, carry):
        for out_tile in range(out_tiles):
            sums = zeros
            for at in range(out_tile + 1):
                sums = step(at, sums, block, out_tile, at < out_tile)
            finish(sums, block, out_tile)
        return carry

    def convolve_tile(index, carry):
        block = lax.rem(index, blocks)
        out_tile = lax.div(index, blocks)
        sums = lax.fori_loop(
            0, out_tile + 1, lambda at, sums: step(at, sums, block, out_tile, True), zeros
        )
        finish(sums, block, out_tile)
        return carry

    if total_rows <= 32:
        lax.fori_loop(0, blocks, convolve_block, 0)
    else:
        lax.fori_loop(0, out_tiles * blocks, convolve_tile, 0)

    def gather_terms(at, carry):
        tiles = [product[at * 8 + k] for k in range(8)]
        summed = jnp.sum(jnp.stack(tiles), axis=1)
        if blocks == 4:
            turned = jnp.concatenate([summed[blocks:], -summed[:blocks]], axis=0)
        else:
            swapped = [
                tiles[k + blocks] if (k // blocks) % 2 == 0 else -tiles[k - blocks]
                for k in range(8)
            ]
            turned = jnp.sum(jnp.stack(swapped), axis=1)
        place = pl.ds(pl.multiple_of(at * 8, 8), 8)
        mixed[place, pl.ds(0, LANES)] = summed
        mixed[place, pl.ds(LANES, LANES)] = turned
        return carry

    lax.fori_loop(0, total_rows * 2 * blocks // 8, gather_terms, 0, unroll=4)
    out[...] = dot_split(mixed[...], back[...])


def final_kernel(scaling, spread, inner_cos, inner_sin, outer, out):
    values = spread[...]
    stacked = jnp.concatenate([values * inner_cos[...], values * inner_sin[...]], axis=0)
    high, low = split_parts(stacked)
    joined = jnp.concatenate([high, low, high], axis=0)
    total = jnp.dot(outer[...], joined, preferred_element_type=jnp.float32)
    out[...] = total * scaling


def in_hbm(array):
    return pltpu.with_memory_space_constraint(array, pltpu.HBM)


def whole_call(kernel, out_shapes, scratch, operands, tables=(), kept=True):
    out_type = pltpu.VMEM if kept else jax.ShapeDtypeStruct
    operands = [pltpu.with_memory_space_constraint(operand, pltpu.VMEM) for operand in operands]
    return pl.pallas_call(
        kernel,
        out_shape=[out_type(shape, jnp.float32) for shape in out_shapes],
        in_specs=[pl.BlockSpec(memory_space=pltpu.VMEM)] * len(operands)
        + [pl.BlockSpec(memory_space=pltpu.HBM)] * len(tables),
        out_specs=[pl.BlockSpec(memory_space=pltpu.VMEM)] * len(out_shapes),
        scratch_shapes=scratch,
        compiler_params=pltpu.CompilerParams(vmem_limit_bytes=VMEM_BYTES),
    )(*operands, *[in_hbm(table) for table in tables])


def row_scratch(blocks, rows, terms, width, tables):
    return [
        pltpu.VMEM((4, blocks, rows, terms, LANES), jnp.float32),
        pltpu.VMEM((2 * blocks * rows * terms, 6 * LANES), jnp.bfloat16),
        pltpu.VMEM((2, width // LANES, LANES), jnp.float32),
        pltpu.VMEM((4, terms, width), jnp.float32),
        *[pltpu.VMEM(table.shape, table.dtype) for table in tables],
        pltpu.SemaphoreType.DMA((len(tables),)),
    ]


def spectra_by_exchange(density, blocks, groups, columns, row_factors, tables):
    rows_here, width = density.shape
    comps, ranks = lax.axis_size("comp"), lax.axis_size("rank")
    half = width // 2
    lines = comps // 2
    terms = row_factors[0].shape[0]
    core = lax.rem(lax.axis_index("rank"), 2)
    mine = lax.dynamic_slice_in_dim(density, core * half, half, 1)

    def along(block, step):
        pairs = [(c, ((c // 2 + step) % lines) * 2 + c % 2) for c in range(comps)]
        return lax.ppermute(block, "comp", pairs)

    def across(block):
        return lax.ppermute(block, "comp", [(c, c ^ 1) for c in range(comps)])

    def beside(block):
        return lax.ppermute(block, "rank", [(r, r ^ 1) for r in range(ranks)])

    def spectra(kernel, sources, operands, fetched):
        rows = rows_here * len(sources)
        (tile,) = whole_call(
            lambda *refs: kernel(blocks, groups, sources, *refs),
            [(2 * blocks, 2, rows, terms, LANES)],
            row_scratch(blocks, rows, terms, width, fetched),
            (*operands, *row_factors),
            fetched,
        )
        return tile

    def joined_spectra(pieces, sources):
        def kernel(blocks, groups, sources, *refs):
            pieces_kernel(blocks, groups, sources, len(pieces), *refs)

        return spectra(kernel, sources, (*pieces, *columns), tables)

    halves = (0, 1)
    own_source = ((0, 0), None, 0, False)
    early = [(halves, 0, 0, True)]
    early += [(halves, step, step, False) for step in range(1, lines)]
    late = [(halves, step - 1, step, True) for step in range(1, lines)]

    lined = [along(mine, step) for step in range(1, lines)]
    flipped_own = across(mine)
    own = spectra(own_kernel, [own_source], (), (*tables, density, *columns))
    (lined[lines // 2 - 1],) = after([lined[lines // 2 - 1]], own)
    flipped = [across(block) for block in lined]
    near = jnp.stack([flipped_own, *lined])
    first = joined_spectra([near, beside(near)], early)
    flipped_near = jnp.stack(after(flipped, first))
    second = joined_spectra([flipped_near, beside(flipped_near)], late)
    layout = [source[2:] for source in [own_source] + early + late]
    return [own[None], first[None], second[None]], layout


def spectra_by_gather(density, blocks, groups, columns, row_factors, tables):
    rows_here, width = density.shape
    comps, ranks = lax.axis_size("comp"), lax.axis_size("rank")
    terms = row_factors[0].shape[0]
    total_rows = rows_here * comps
    part = width // ranks
    mine = lax.dynamic_slice_in_dim(density, lax.axis_index("rank") * part, part, 1)
    gathered = lax.all_gather(mine, AXES, axis=0).reshape(comps, ranks, rows_here, part)
    tile_shape = (2 * blocks, 2, 8, terms, LANES)
    spectra = pl.pallas_call(
        lambda *refs: gathered_kernel(blocks, groups, *refs),
        grid=(total_rows // 8,),
        out_shape=jax.ShapeDtypeStruct((total_rows // 8, *tile_shape), jnp.float32),
        in_specs=[pl.BlockSpec((8 // rows_here, ranks, rows_here, part), lambda t: (t, 0, 0, 0))]
        + [pl.BlockSpec(memory_space=pltpu.VMEM)] * 4
        + [pl.BlockSpec(memory_space=pltpu.HBM)] * len(tables),
        out_specs=pl.BlockSpec((1, *tile_shape), lambda t: (t, 0, 0, 0, 0, 0)),
        scratch_shapes=row_scratch(blocks, 8, terms, width, tables),
        compiler_params=pltpu.CompilerParams(vmem_limit_bytes=VMEM_BYTES),
    )(gathered, *columns, *row_factors, *[in_hbm(table) for table in tables])
    return [spectra], None


def body(density, row_left, col_left, row_right, col_right):
    rows_here, width = density.shape
    comps = lax.axis_size("comp")
    devices = comps * lax.axis_size("rank")
    total_rows = rows_here * comps
    terms = row_left.shape[0]
    groups = min(devices, width // LANES)
    term_groups = devices // groups
    blocks = width // (groups * LANES)
    device_at = lax.axis_index(AXES)
    if term_groups > 1:
        term_at = lax.broadcasted_iota(jnp.int32, (terms, 1), 0)
        chosen = lax.div(term_at, terms // term_groups) == lax.div(device_at, groups)
        col_left = jnp.where(chosen, col_left, 0.0)
        col_right = jnp.where(chosen, col_right, 0.0)
    columns = (col_left, col_right)
    row_factors = (row_left, row_right)
    tables = (block_twiddles(blocks), split_rows(forward_table()))
    spectra = spectra_by_exchange if comps <= 8 else spectra_by_gather
    tiles, layout = spectra(density, blocks, groups, columns, row_factors, tables)

    out_rows = total_rows * 2 * blocks
    (sent,) = whole_call(
        lambda *refs: convolve_kernel(blocks, rows_here, layout, len(tiles), *refs),
        [(out_rows, LANES)],
        [
            pltpu.VMEM((2 * blocks, 3, PAD + total_rows, terms, LANES), jnp.float32),
            pltpu.VMEM((out_rows, terms, LANES), jnp.float32),
            pltpu.VMEM((out_rows, 2 * LANES), jnp.float32),
        ],
        (*tiles, split_rows(inverse_table())),
    )
    spread = lax.all_to_all(sent, AXES, split_axis=0, concat_axis=0, tiled=True)
    inner_cos, inner_sin, outer_table = final_tables(devices, groups, blocks, width)
    scaling = 0.5 / (math.sqrt(total_rows * width) * width)
    (result,) = whole_call(
        lambda *refs: final_kernel(scaling, *refs),
        [(width // LANES, LANES)],
        [],
        (
            spread,
            jnp.asarray(inner_cos, jnp.float32),
            jnp.asarray(inner_sin, jnp.float32),
            split_columns(outer_table),
        ),
        kept=False,
    )
    return result.reshape(1, width)


def solution(mesh):
    return jax.shard_map(
        body,
        mesh=mesh,
        in_specs=(P("comp", None), P(), P(), P(), P()),
        out_specs=P(AXES, None),
        check_vma=False,
    )
```

```python
import math

import jax
import jax.numpy as jnp
import numpy as np
from jax import lax
from jax.experimental import pallas as pl
from jax.experimental.pallas import tpu as pltpu
from jax.sharding import PartitionSpec as P

LANES = 128
VMEM_BYTES = 16 * 1024 * 1024
AXES = ("comp", "rank")
PAD = 4
HELD_PARTS = (0, 2, 1, 3)


def split_parts(values):
    high = values.astype(jnp.bfloat16)
    low = (values - high.astype(jnp.float32)).astype(jnp.bfloat16)
    return high, low


def split_rows(table):
    high, low = split_parts(jnp.asarray(table, jnp.float32))
    return jnp.concatenate([high, high, low], axis=0)


def split_columns(table):
    high, low = split_parts(jnp.asarray(table, jnp.float32))
    return jnp.concatenate([high, high, low], axis=1)


def dot_split(rows, table):
    high, low = split_parts(rows)
    joined = jnp.concatenate([high, low, high], axis=1)
    return jnp.dot(joined, table, preferred_element_type=jnp.float32)


def forward_table():
    angles = 2.0 * np.pi * np.outer(np.arange(LANES), np.arange(LANES)) / LANES
    cosine, sine = np.cos(angles), np.sin(angles)
    return np.block([[cosine, -sine], [sine, cosine]])


def inverse_table():
    angles = 2.0 * np.pi * np.outer(np.arange(LANES), np.arange(LANES)) / LANES
    return np.concatenate([np.cos(angles), -np.sin(angles)], axis=0)


def block_twiddles(blocks):
    angles = 2.0 * np.pi * np.outer(np.arange(blocks), np.arange(LANES)) / (blocks * LANES)
    table = np.stack([np.cos(angles), -np.sin(angles)], axis=1)
    return jnp.asarray(
        np.broadcast_to(table[:, :, None, :], (blocks, 2, 8, LANES)), jnp.float32
    )


def final_tables(devices, groups, blocks, width):
    owner = np.arange(devices) % groups
    frequency = (owner[:, None] + groups * np.arange(blocks)[None, :]).astype(np.float64) + 0.25
    frequency = np.broadcast_to(frequency[:, None, :], (devices, 2, blocks))
    inner = 2.0 * np.pi * frequency[..., None] * np.arange(LANES) / width
    rows = devices * 2 * blocks
    inner_cos = np.cos(inner).reshape(rows, LANES)
    inner_sin = np.sin(inner).reshape(rows, LANES)
    outer_count = width // LANES
    outer = 2.0 * np.pi * frequency * LANES / width
    outer = np.arange(outer_count)[:, None] * outer.reshape(1, rows)
    is_real = np.broadcast_to(np.array([True, False])[None, :, None], (devices, 2, blocks))
    is_real = is_real.reshape(1, rows)
    with_cos = np.where(is_real, np.cos(outer), -np.sin(outer))
    with_sin = np.where(is_real, -np.sin(outer), -np.cos(outer))
    return inner_cos, inner_sin, np.concatenate([with_cos, with_sin], axis=1)


def block_fourier(reals, imags):
    count = len(reals)
    if count == 1:
        return reals, imags
    if count == 2:
        return (
            [reals[0] + reals[1], reals[0] - reals[1]],
            [imags[0] + imags[1], imags[0] - imags[1]],
        )
    even_real, odd_real = reals[0] + reals[2], reals[0] - reals[2]
    even_imag, odd_imag = imags[0] + imags[2], imags[0] - imags[2]
    pair_real, gap_real = reals[1] + reals[3], reals[1] - reals[3]
    pair_imag, gap_imag = imags[1] + imags[3], imags[1] - imags[3]
    return (
        [even_real + pair_real, odd_real + gap_imag, even_real - pair_real, odd_real - gap_imag],
        [even_imag + pair_imag, odd_imag - gap_real, even_imag - pair_imag, odd_imag + gap_real],
    )


def reduce_rows(blocks, rows, terms, fetch, factors_at, starts, span, partial):
    inner = blocks * LANES
    outer = span // inner
    unroll = math.gcd(16, outer)

    def reduce_block(block, first, count):
        sums = (jnp.zeros((terms, LANES), jnp.float32),) * (4 * count)
        for part, start in enumerate(starts):

            def step(at, sums, part=part, start=start):
                sums = list(sums)
                for extra in range(unroll):
                    lane = (at * unroll + extra) * inner + block * LANES
                    factors = factors_at(start + lane, first == 0)
                    for row in range(count):
                        value = fetch(part, first + row, lane)
                        value = jnp.broadcast_to(value, (terms, LANES))
                        for k in range(4):
                            sums[row * 4 + k] += value * factors[k]
                return tuple(sums)

            sums = lax.fori_loop(0, outer // unroll, step, sums)
        for row in range(count):
            for k in range(4):
                partial[k, block, first + row] = sums[row * 4 + k]

    def reduce_tiles(block, carry):
        for first in range(0, rows, 8):
            reduce_block(block, first, min(8, rows - first))
        return carry

    lax.fori_loop(0, blocks, reduce_tiles, 0)


def transform_rows(blocks, rows, row_at, row_factors, twiddle, table, out, partial, joined):
    terms, total_rows = row_factors[0].shape
    lanes = lax.broadcasted_iota(jnp.int32, (terms, total_rows), 1)

    def butterfly(row, side):
        picked = jnp.where(lanes == row_at(row), row_factors[side][...], 0.0)
        factor = jnp.sum(picked, axis=1, keepdims=True)
        factor = jnp.broadcast_to(factor, (terms, LANES))
        reals = [partial[2 * side, block, row] * factor for block in range(blocks)]
        imags = [partial[2 * side + 1, block, row] * factor for block in range(blocks)]
        reals, imags = block_fourier(reals, imags)
        for block in range(1, blocks):
            real, imag = reals[block], imags[block]
            cosine, sine = twiddle[block, 0], twiddle[block, 1]
            reals[block] = real * cosine - imag * sine
            imags[block] = real * sine + imag * cosine
        return reals, imags

    def butterfly_pair(pair):
        for side in range(2):
            both = [butterfly(pair * 2 + extra, side) for extra in range(2)]
            for block in range(blocks):
                base = ((block * 2 + side) * rows + pair * 2) * terms
                place = pl.ds(base, 2 * terms)
                for part in range(2):
                    values = jnp.concatenate([both[0][part][block], both[1][part][block]], axis=0)
                    high, low = split_parts(values)
                    for third, piece in enumerate((high, low, high)):
                        joined[place, pl.ds((third * 2 + part) * LANES, LANES)] = piece

    for pair in range(rows // 2):
        butterfly_pair(pair)
    planes = 2 * blocks
    step = planes * rows * terms
    while step > 512:
        step //= 2
    plane_step = step // (rows * terms)

    def transform(at, carry):
        place = pl.ds(pl.multiple_of(at * step, 16), step)
        total = jnp.dot(joined[place, :], table[...], preferred_element_type=jnp.float32)
        total = total.reshape(plane_step, rows, terms, 2 * LANES)
        place = pl.ds(at * plane_step, plane_step)
        out[place, 0] = total[..., :LANES]
        out[place, 1] = total[..., LANES:]
        return carry

    lax.fori_loop(0, planes // plane_step, transform, 0)


def comp_of(step, flipped):
    lines = lax.axis_size("comp") // 2
    comp_at = lax.axis_index("comp")
    line = lax.rem(lax.div(comp_at, 2) + lines - step, lines)
    side = lax.rem(comp_at, 2)
    return line * 2 + (1 - side if flipped else side)


def make_phases(groups, phases):
    width = phases.shape[1] * LANES
    device_at = lax.axis_index("comp") * lax.axis_size("rank") + lax.axis_index("rank")
    odd = 4 * lax.rem(device_at, groups) + 1
    shape = phases.shape[1:]
    cells = lax.broadcasted_iota(jnp.int32, shape, 0) * LANES
    cells = cells + lax.broadcasted_iota(jnp.int32, shape, 1)
    turns = (cells * odd) & (4 * width - 1)
    turns = jnp.where(turns >= 2 * width, turns - 4 * width, turns)
    angles = turns.astype(jnp.float32) * (2.0 * math.pi / (4 * width))
    phases[0] = jnp.cos(angles)
    phases[1] = -jnp.sin(angles)


def made_factors(columns, phases, kept):
    terms = columns[0].shape[0]

    def factors_at(lane, first):
        place = pl.ds(pl.multiple_of(lane, LANES), LANES)
        if not first:
            return [kept[k, :, place] for k in range(4)]
        turn = pl.ds(lax.div(lane, LANES), 1)
        factors = [
            column[:, place] * jnp.broadcast_to(phases[part, turn, :], (terms, LANES))
            for column in columns
            for part in range(2)
        ]
        for k in range(4):
            kept[k, :, place] = factors[k]
        return factors

    return factors_at


def start_tables(tables, held, arrivals):
    copies = [
        pltpu.make_async_copy(table, place, arrivals.at[k])
        for k, (table, place) in enumerate(zip(tables, held))
    ]
    for copy in copies:
        copy.start()
    return copies


def pieces_kernel(blocks, groups, sources, count, *refs):
    pieces, refs = refs[:count], refs[count:]
    columns, row_factors, tables, refs = refs[0:2], refs[2:4], refs[4:6], refs[6:]
    out, partial, joined, phases, weights, twiddle, table, arrivals = refs
    copies = start_tables(tables, (twiddle, table), arrivals)
    make_phases(groups, phases)
    reduce_pieces(blocks, sources, pieces, columns, phases, weights, partial)
    finish_pieces(
        blocks, sources, copies, row_factors, twiddle, table, out, partial, joined
    )


def own_kernel(blocks, groups, sources, *refs):
    row_factors, sent, refs = refs[1:3], refs[3:8], refs[8:]
    out, partial, joined, phases, weights = refs[:5]
    held, arrivals = refs[5:10], refs[10]
    copies = start_tables(sent, held, arrivals)
    make_phases(groups, phases)
    for copy in copies[2:]:
        copy.wait()
    twiddle, table, own, *columns = held
    reduce_pieces(blocks, sources, [own], columns, phases, weights, partial)
    finish_pieces(
        blocks, sources, copies[:2], row_factors, twiddle, table, out, partial, joined
    )


def reduce_pieces(blocks, sources, pieces, columns, phases, weights, partial):
    rows_here = pieces[0].shape[-2]
    terms, width = columns[0].shape
    ranks = lax.axis_size("rank")
    span = width // ranks
    rank_at = lax.axis_index("rank")
    starts = [(rank_at ^ other) * span for other in HELD_PARTS]

    def fetch(part, row, lane):
        quarters, _, _ = sources[row // rows_here]
        row = pl.ds(row % rows_here, 1)
        if quarters is None:
            return pieces[0][row, pl.ds(pl.multiple_of(starts[part] + lane, LANES), LANES)]
        number, index = quarters[part]
        return pieces[number][index, row, pl.ds(pl.multiple_of(lane, LANES), LANES)]

    factors_at = made_factors(columns, phases, weights)
    rows = len(sources) * rows_here
    reduce_rows(blocks, rows, terms, fetch, factors_at, starts, span, partial)


def finish_pieces(blocks, sources, copies, row_factors, twiddle, table, out, partial, joined):
    rows = partial.shape[2]
    rows_here = rows // len(sources)
    bases = [comp_of(step, flipped) * rows_here for _, step, flipped in sources]

    def row_at(row):
        return bases[row // rows_here] + row % rows_here

    for copy in copies:
        copy.wait()
    transform_rows(blocks, rows, row_at, row_factors, twiddle, table, out, partial, joined)


def gathered_kernel(blocks, groups, pieces, *refs):
    columns, row_factors, tables, refs = refs[0:2], refs[2:4], refs[4:6], refs[6:]
    out, partial, joined, phases, weights, twiddle, table, arrivals = refs
    copies = start_tables(tables, (twiddle, table), arrivals)
    make_phases(groups, phases)
    parts, rows_here, span = pieces.shape[1:]

    def fetch(part, row, lane):
        place = pl.ds(pl.multiple_of(lane, LANES), LANES)
        return pieces[row // rows_here, part, pl.ds(row % rows_here, 1), place]

    base = pl.program_id(0) * 8
    starts = [part * span for part in range(parts)]
    terms = columns[0].shape[0]
    factors_at = made_factors(columns, phases, weights)
    reduce_rows(blocks, 8, terms, fetch, factors_at, starts, span, partial)
    for copy in copies:
        copy.wait()
    transform_rows(
        blocks,
        8,
        lambda row: base + row,
        row_factors,
        twiddle,
        table,
        out.at[0],
        partial,
        joined,
    )


def pass_kernel(*refs):
    del refs


def after(values, earlier):
    anywhere = pl.BlockSpec(memory_space=pl.ANY)
    operands = [pltpu.with_memory_space_constraint(x, pltpu.VMEM) for x in (*values, earlier)]
    return pl.pallas_call(
        pass_kernel,
        out_shape=[jax.ShapeDtypeStruct(value.shape, value.dtype) for value in values],
        in_specs=[anywhere] * len(operands),
        out_specs=[anywhere] * len(values),
        input_output_aliases={k: k for k in range(len(values))},
    )(*operands)


def convolve_kernel(blocks, rows_here, layout, tile_count, *refs):
    tiles = refs[:tile_count]
    back, out, spectrum, product, mixed = refs[tile_count:]
    total_rows = spectrum.shape[2] - PAD
    terms = spectrum.shape[3]
    spectrum[:, :, pl.ds(0, PAD)] = jnp.zeros((2 * blocks, 3, PAD, terms, LANES), jnp.float32)
    moves = []
    for number, tile in enumerate(tiles):
        for at in range(tile.shape[0]):
            for first in range(0, tile.shape[3], rows_here):
                moves.append((tile, at, first))
    comps = [comp_of(*layout[k]) if layout else k for k in range(len(moves))]

    def collect(plane, carry):
        for (tile, at, first), comp in zip(moves, comps):
            real = tile[at, plane, 0, pl.ds(first, rows_here)]
            imag = tile[at, plane, 1, pl.ds(first, rows_here)]
            place = pl.ds(PAD + comp * rows_here, rows_here)
            spectrum[plane, 0, place] = real
            spectrum[plane, 1, place] = imag
            spectrum[plane, 2, place] = real + imag
        return carry

    lax.fori_loop(0, 2 * blocks, collect, 0)

    def step(at, sums, block, out_tile, whole):
        sums = list(sums)
        left_base = PAD + 4 * at
        right_base = PAD + 4 * (out_tile - at)
        for part in range(3):
            left = [spectrum[2 * block, part, left_base + k] for k in range(4)]
            right = {
                k: spectrum[2 * block + 1, part, right_base + k]
                for k in range(-3 if whole else 0, 4)
            }
            for row in range(4):
                for k in range(4 if whole else row + 1):
                    sums[row * 3 + part] += left[k] * right[row - k]
        return tuple(sums)

    def finish(sums, block, out_tile):
        for row in range(4):
            both_real, both_imag, crossed = sums[row * 3 : row * 3 + 3]
            base = (out_tile * 4 + row) * 2 * blocks + block
            product[base] = both_real - both_imag
            product[base + blocks] = crossed - both_real - both_imag

    zeros = (jnp.zeros((terms, LANES), jnp.float32),) * 12
    out_tiles = total_rows // 4

    def convolve_block(block, carry):
        for out_tile in range(out_tiles):
            sums = zeros
            for at in range(out_tile + 1):
                sums = step(at, sums, block, out_tile, at < out_tile)
            finish(sums, block, out_tile)
        return carry

    def convolve_tile(index, carry):
        block = lax.rem(index, blocks)
        out_tile = lax.div(index, blocks)
        sums = lax.fori_loop(
            0, out_tile + 1, lambda at, sums: step(at, sums, block, out_tile, True), zeros
        )
        finish(sums, block, out_tile)
        return carry

    if total_rows <= 32:
        lax.fori_loop(0, blocks, convolve_block, 0)
    else:
        lax.fori_loop(0, out_tiles * blocks, convolve_tile, 0)

    def gather_terms(at, carry):
        tiles = [product[at * 8 + k] for k in range(8)]
        summed = jnp.sum(jnp.stack(tiles), axis=1)
        if blocks == 4:
            turned = jnp.concatenate([summed[blocks:], -summed[:blocks]], axis=0)
        else:
            swapped = [
                tiles[k + blocks] if (k // blocks) % 2 == 0 else -tiles[k - blocks]
                for k in range(8)
            ]
            turned = jnp.sum(jnp.stack(swapped), axis=1)
        place = pl.ds(pl.multiple_of(at * 8, 8), 8)
        mixed[place, pl.ds(0, LANES)] = summed
        mixed[place, pl.ds(LANES, LANES)] = turned
        return carry

    lax.fori_loop(0, total_rows * 2 * blocks // 8, gather_terms, 0, unroll=4)
    out[...] = dot_split(mixed[...], back[...])


def final_kernel(scaling, spread, inner_cos, inner_sin, outer, out):
    values = spread[...]
    stacked = jnp.concatenate([values * inner_cos[...], values * inner_sin[...]], axis=0)
    high, low = split_parts(stacked)
    joined = jnp.concatenate([high, low, high], axis=0)
    total = jnp.dot(outer[...], joined, preferred_element_type=jnp.float32)
    out[...] = total * scaling


def in_hbm(array):
    return pltpu.with_memory_space_constraint(array, pltpu.HBM)


def whole_call(kernel, out_shapes, scratch, operands, tables=(), kept=True):
    out_type = pltpu.VMEM if kept else jax.ShapeDtypeStruct
    operands = [pltpu.with_memory_space_constraint(operand, pltpu.VMEM) for operand in operands]
    return pl.pallas_call(
        kernel,
        out_shape=[out_type(shape, jnp.float32) for shape in out_shapes],
        in_specs=[pl.BlockSpec(memory_space=pltpu.VMEM)] * len(operands)
        + [pl.BlockSpec(memory_space=pltpu.HBM)] * len(tables),
        out_specs=[pl.BlockSpec(memory_space=pltpu.VMEM)] * len(out_shapes),
        scratch_shapes=scratch,
        compiler_params=pltpu.CompilerParams(vmem_limit_bytes=VMEM_BYTES),
    )(*operands, *[in_hbm(table) for table in tables])


def row_scratch(blocks, rows, terms, width, tables):
    return [
        pltpu.VMEM((4, blocks, rows, terms, LANES), jnp.float32),
        pltpu.VMEM((2 * blocks * rows * terms, 6 * LANES), jnp.bfloat16),
        pltpu.VMEM((2, width // LANES, LANES), jnp.float32),
        pltpu.VMEM((4, terms, width), jnp.float32),
        *[pltpu.VMEM(table.shape, table.dtype) for table in tables],
        pltpu.SemaphoreType.DMA((len(tables),)),
    ]


def spectra_by_exchange(density, blocks, groups, columns, row_factors, tables):
    rows_here, width = density.shape
    comps, ranks = lax.axis_size("comp"), lax.axis_size("rank")
    part = width // ranks
    lines = comps // 2
    terms = row_factors[0].shape[0]
    mine = lax.dynamic_slice_in_dim(density, lax.axis_index("rank") * part, part, 1)

    def direct(step, flipped):
        pairs = [(c, ((c // 2 + step) % lines) * 2 + (c % 2) ^ flipped) for c in range(comps)]
        return lax.ppermute(mine, "comp", pairs)

    def swapped(block, other):
        return lax.ppermute(block, "rank", [(r, r ^ other) for r in range(ranks)])

    def spectra(kernel, sources, operands, fetched):
        rows = rows_here * len(sources)
        (tile,) = whole_call(
            lambda *refs: kernel(blocks, groups, sources, *refs),
            [(2 * blocks, 2, rows, terms, LANES)],
            row_scratch(blocks, rows, terms, width, fetched),
            (*operands, *row_factors),
            fetched,
        )
        return tile

    def joined_spectra(pieces, sources):
        def kernel(blocks, groups, sources, *refs):
            pieces_kernel(blocks, groups, sources, len(pieces), *refs)

        return spectra(kernel, sources, (*pieces, *columns), tables)

    own_source = (None, 0, False)
    early = [(0, True)] + [(step, False) for step in range(1, lines)]
    late = [(step, True) for step in range(1, lines)]

    near = jnp.stack([direct(*place) for place in early])
    flipped = jnp.stack([direct(*place) for place in late])
    beyond = swapped(near, 2)
    flipped_beyond = swapped(flipped, 2)
    flipped_beside = swapped(flipped, 1)
    own = spectra(own_kernel, [own_source], (near,), (*tables, density, *columns))
    both = jnp.concatenate([near, *after([beyond], own)])
    count = len(early)
    early = [
        (((0, k), (0, count + k), (1, k), (1, count + k)), *place)
        for k, place in enumerate(early)
    ]
    first = joined_spectra([both, swapped(both, 1)], early)
    (flipped_beyond,) = after([flipped_beyond], first)
    late = [(((0, k), (1, k), (2, k), (3, k)), *place) for k, place in enumerate(late)]
    second = joined_spectra(
        [flipped, flipped_beyond, flipped_beside, swapped(flipped_beyond, 1)], late
    )
    layout = [source[1:] for source in [own_source] + early + late]
    return [own[None], first[None], second[None]], layout


def spectra_by_gather(density, blocks, groups, columns, row_factors, tables):
    rows_here, width = density.shape
    comps, ranks = lax.axis_size("comp"), lax.axis_size("rank")
    terms = row_factors[0].shape[0]
    total_rows = rows_here * comps
    part = width // ranks
    mine = lax.dynamic_slice_in_dim(density, lax.axis_index("rank") * part, part, 1)
    gathered = lax.all_gather(mine, AXES, axis=0).reshape(comps, ranks, rows_here, part)
    tile_shape = (2 * blocks, 2, 8, terms, LANES)
    spectra = pl.pallas_call(
        lambda *refs: gathered_kernel(blocks, groups, *refs),
        grid=(total_rows // 8,),
        out_shape=jax.ShapeDtypeStruct((total_rows // 8, *tile_shape), jnp.float32),
        in_specs=[pl.BlockSpec((8 // rows_here, ranks, rows_here, part), lambda t: (t, 0, 0, 0))]
        + [pl.BlockSpec(memory_space=pltpu.VMEM)] * 4
        + [pl.BlockSpec(memory_space=pltpu.HBM)] * len(tables),
        out_specs=pl.BlockSpec((1, *tile_shape), lambda t: (t, 0, 0, 0, 0, 0)),
        scratch_shapes=row_scratch(blocks, 8, terms, width, tables),
        compiler_params=pltpu.CompilerParams(vmem_limit_bytes=VMEM_BYTES),
    )(gathered, *columns, *row_factors, *[in_hbm(table) for table in tables])
    return [spectra], None


def body(density, row_left, col_left, row_right, col_right):
    rows_here, width = density.shape
    comps = lax.axis_size("comp")
    devices = comps * lax.axis_size("rank")
    total_rows = rows_here * comps
    terms = row_left.shape[0]
    groups = min(devices, width // LANES)
    term_groups = devices // groups
    blocks = width // (groups * LANES)
    device_at = lax.axis_index(AXES)
    if term_groups > 1:
        term_at = lax.broadcasted_iota(jnp.int32, (terms, 1), 0)
        chosen = lax.div(term_at, terms // term_groups) == lax.div(device_at, groups)
        col_left = jnp.where(chosen, col_left, 0.0)
        col_right = jnp.where(chosen, col_right, 0.0)
    columns = (col_left, col_right)
    row_factors = (row_left, row_right)
    tables = (block_twiddles(blocks), split_rows(forward_table()))
    spectra = spectra_by_exchange if comps <= 8 else spectra_by_gather
    tiles, layout = spectra(density, blocks, groups, columns, row_factors, tables)

    out_rows = total_rows * 2 * blocks
    (sent,) = whole_call(
        lambda *refs: convolve_kernel(blocks, rows_here, layout, len(tiles), *refs),
        [(out_rows, LANES)],
        [
            pltpu.VMEM((2 * blocks, 3, PAD + total_rows, terms, LANES), jnp.float32),
            pltpu.VMEM((out_rows, terms, LANES), jnp.float32),
            pltpu.VMEM((out_rows, 2 * LANES), jnp.float32),
        ],
        (*tiles, split_rows(inverse_table())),
    )
    spread = lax.all_to_all(sent, AXES, split_axis=0, concat_axis=0, tiled=True)
    inner_cos, inner_sin, outer_table = final_tables(devices, groups, blocks, width)
    scaling = 0.5 / (math.sqrt(total_rows * width) * width)
    (result,) = whole_call(
        lambda *refs: final_kernel(scaling, *refs),
        [(width // LANES, LANES)],
        [],
        (
            spread,
            jnp.asarray(inner_cos, jnp.float32),
            jnp.asarray(inner_sin, jnp.float32),
            split_columns(outer_table),
        ),
        kept=False,
    )
    return result.reshape(1, width)


def solution(mesh):
    return jax.shard_map(
        body,
        mesh=mesh,
        in_specs=(P("comp", None), P(), P(), P(), P()),
        out_specs=P(AXES, None),
        check_vma=False,
    )
```

```python
import math

import jax
import jax.numpy as jnp
import numpy as np
from jax import lax
from jax.experimental import pallas as pl
from jax.experimental.pallas import tpu as pltpu
from jax.sharding import PartitionSpec as P

LANES = 128
VMEM_BYTES = 16 * 1024 * 1024
AXES = ("comp", "rank")
PAD = 4
HELD_PARTS = (0, 2, 1, 3)


def split_parts(values):
    high = values.astype(jnp.bfloat16)
    low = (values - high.astype(jnp.float32)).astype(jnp.bfloat16)
    return high, low


def split_rows(table):
    high, low = split_parts(jnp.asarray(table, jnp.float32))
    return jnp.concatenate([high, high, low], axis=0)


def split_columns(table):
    high, low = split_parts(jnp.asarray(table, jnp.float32))
    return jnp.concatenate([high, high, low], axis=1)


def dot_split(rows, table):
    high, low = split_parts(rows)
    joined = jnp.concatenate([high, low, high], axis=1)
    return jnp.dot(joined, table, preferred_element_type=jnp.float32)


def forward_table():
    angles = 2.0 * np.pi * np.outer(np.arange(LANES), np.arange(LANES)) / LANES
    cosine, sine = np.cos(angles), np.sin(angles)
    return np.block([[cosine, -sine], [sine, cosine]])


def inverse_table():
    angles = 2.0 * np.pi * np.outer(np.arange(LANES), np.arange(LANES)) / LANES
    return np.concatenate([np.cos(angles), -np.sin(angles)], axis=0)


def block_twiddles(blocks):
    angles = 2.0 * np.pi * np.outer(np.arange(blocks), np.arange(LANES)) / (blocks * LANES)
    table = np.stack([np.cos(angles), -np.sin(angles)], axis=1)
    return jnp.asarray(
        np.broadcast_to(table[:, :, None, :], (blocks, 2, 8, LANES)), jnp.float32
    )


def final_tables(devices, groups, blocks, width):
    owner = np.arange(devices) % groups
    frequency = (owner[:, None] + groups * np.arange(blocks)[None, :]).astype(np.float64) + 0.25
    frequency = np.broadcast_to(frequency[:, None, :], (devices, 2, blocks))
    inner = 2.0 * np.pi * frequency[..., None] * np.arange(LANES) / width
    rows = devices * 2 * blocks
    inner_cos = np.cos(inner).reshape(rows, LANES)
    inner_sin = np.sin(inner).reshape(rows, LANES)
    outer_count = width // LANES
    outer = 2.0 * np.pi * frequency * LANES / width
    outer = np.arange(outer_count)[:, None] * outer.reshape(1, rows)
    is_real = np.broadcast_to(np.array([True, False])[None, :, None], (devices, 2, blocks))
    is_real = is_real.reshape(1, rows)
    with_cos = np.where(is_real, np.cos(outer), -np.sin(outer))
    with_sin = np.where(is_real, -np.sin(outer), -np.cos(outer))
    return inner_cos, inner_sin, np.concatenate([with_cos, with_sin], axis=1)


def block_fourier(reals, imags):
    count = len(reals)
    if count == 1:
        return reals, imags
    if count == 2:
        return (
            [reals[0] + reals[1], reals[0] - reals[1]],
            [imags[0] + imags[1], imags[0] - imags[1]],
        )
    even_real, odd_real = reals[0] + reals[2], reals[0] - reals[2]
    even_imag, odd_imag = imags[0] + imags[2], imags[0] - imags[2]
    pair_real, gap_real = reals[1] + reals[3], reals[1] - reals[3]
    pair_imag, gap_imag = imags[1] + imags[3], imags[1] - imags[3]
    return (
        [even_real + pair_real, odd_real + gap_imag, even_real - pair_real, odd_real - gap_imag],
        [even_imag + pair_imag, odd_imag - gap_real, even_imag - pair_imag, odd_imag + gap_real],
    )


def reduce_rows(blocks, rows, terms, fetch, factors_at, starts, span, partial):
    inner = blocks * LANES
    outer = span // inner
    unroll = math.gcd(16, outer)

    def reduce_block(block, first, count):
        sums = (jnp.zeros((terms, LANES), jnp.float32),) * (4 * count)
        for part, start in enumerate(starts):

            def step(at, sums, part=part, start=start):
                sums = list(sums)
                for extra in range(unroll):
                    lane = (at * unroll + extra) * inner + block * LANES
                    factors = factors_at(start + lane, first == 0)
                    for row in range(count):
                        value = fetch(part, first + row, lane)
                        value = jnp.broadcast_to(value, (terms, LANES))
                        for k in range(4):
                            sums[row * 4 + k] += value * factors[k]
                return tuple(sums)

            sums = lax.fori_loop(0, outer // unroll, step, sums)
        for row in range(count):
            for k in range(4):
                partial[k, block, first + row] = sums[row * 4 + k]

    def reduce_tiles(block, carry):
        for first in range(0, rows, 8):
            reduce_block(block, first, min(8, rows - first))
        return carry

    lax.fori_loop(0, blocks, reduce_tiles, 0)


def transform_rows(blocks, rows, row_at, row_factors, twiddle, table, out, partial, joined):
    terms, total_rows = row_factors[0].shape
    lanes = lax.broadcasted_iota(jnp.int32, (terms, total_rows), 1)

    def butterfly(row, side):
        picked = jnp.where(lanes == row_at(row), row_factors[side][...], 0.0)
        factor = jnp.sum(picked, axis=1, keepdims=True)
        factor = jnp.broadcast_to(factor, (terms, LANES))
        reals = [partial[2 * side, block, row] * factor for block in range(blocks)]
        imags = [partial[2 * side + 1, block, row] * factor for block in range(blocks)]
        reals, imags = block_fourier(reals, imags)
        for block in range(1, blocks):
            real, imag = reals[block], imags[block]
            cosine, sine = twiddle[block, 0], twiddle[block, 1]
            reals[block] = real * cosine - imag * sine
            imags[block] = real * sine + imag * cosine
        return reals, imags

    def butterfly_pair(pair):
        for side in range(2):
            both = [butterfly(pair * 2 + extra, side) for extra in range(2)]
            for block in range(blocks):
                base = ((block * 2 + side) * rows + pair * 2) * terms
                place = pl.ds(base, 2 * terms)
                for part in range(2):
                    values = jnp.concatenate([both[0][part][block], both[1][part][block]], axis=0)
                    high, low = split_parts(values)
                    for third, piece in enumerate((high, low, high)):
                        joined[place, pl.ds((third * 2 + part) * LANES, LANES)] = piece

    for pair in range(rows // 2):
        butterfly_pair(pair)
    planes = 2 * blocks
    step = planes * rows * terms
    while step > 512:
        step //= 2
    plane_step = step // (rows * terms)

    def transform(at, carry):
        place = pl.ds(pl.multiple_of(at * step, 16), step)
        total = jnp.dot(joined[place, :], table[...], preferred_element_type=jnp.float32)
        total = total.reshape(plane_step, rows, terms, 2 * LANES)
        place = pl.ds(at * plane_step, plane_step)
        out[place, 0] = total[..., :LANES]
        out[place, 1] = total[..., LANES:]
        return carry

    lax.fori_loop(0, planes // plane_step, transform, 0)


def comp_of(step, flipped):
    lines = lax.axis_size("comp") // 2
    comp_at = lax.axis_index("comp")
    line = lax.rem(lax.div(comp_at, 2) + lines - step, lines)
    side = lax.rem(comp_at, 2)
    return line * 2 + (1 - side if flipped else side)


def make_phases(groups, phases):
    width = phases.shape[1] * LANES
    device_at = lax.axis_index("comp") * lax.axis_size("rank") + lax.axis_index("rank")
    odd = 4 * lax.rem(device_at, groups) + 1
    shape = phases.shape[1:]
    cells = lax.broadcasted_iota(jnp.int32, shape, 0) * LANES
    cells = cells + lax.broadcasted_iota(jnp.int32, shape, 1)
    turns = (cells * odd) & (4 * width - 1)
    turns = jnp.where(turns >= 2 * width, turns - 4 * width, turns)
    angles = turns.astype(jnp.float32) * (2.0 * math.pi / (4 * width))
    phases[0] = jnp.cos(angles)
    phases[1] = -jnp.sin(angles)


def made_factors(columns, phases, kept):
    terms = columns[0].shape[0]

    def factors_at(lane, first):
        place = pl.ds(pl.multiple_of(lane, LANES), LANES)
        if not first:
            return [kept[k, :, place] for k in range(4)]
        turn = pl.ds(lax.div(lane, LANES), 1)
        factors = [
            column[:, place] * jnp.broadcast_to(phases[part, turn, :], (terms, LANES))
            for column in columns
            for part in range(2)
        ]
        for k in range(4):
            kept[k, :, place] = factors[k]
        return factors

    return factors_at


def start_tables(tables, held, arrivals):
    copies = [
        pltpu.make_async_copy(table, place, arrivals.at[k])
        for k, (table, place) in enumerate(zip(tables, held))
    ]
    for copy in copies:
        copy.start()
    return copies


def pieces_kernel(blocks, groups, sources, count, *refs):
    pieces, refs = refs[:count], refs[count:]
    columns, row_factors, tables, refs = refs[0:2], refs[2:4], refs[4:6], refs[6:]
    out, partial, joined, phases, weights, twiddle, table, arrivals = refs
    copies = start_tables(tables, (twiddle, table), arrivals)
    make_phases(groups, phases)
    reduce_pieces(blocks, sources, pieces, columns, phases, weights, partial)
    finish_pieces(
        blocks, sources, copies, row_factors, twiddle, table, out, partial, joined
    )


def own_kernel(blocks, groups, sources, *refs):
    row_factors, sent, refs = refs[0:2], refs[2:7], refs[7:]
    out, partial, joined, phases, weights = refs[:5]
    held, arrivals = refs[5:10], refs[10]
    copies = start_tables(sent, held, arrivals)
    make_phases(groups, phases)
    for copy in copies[2:]:
        copy.wait()
    twiddle, table, own, *columns = held
    reduce_pieces(blocks, sources, [own], columns, phases, weights, partial)
    finish_pieces(
        blocks, sources, copies[:2], row_factors, twiddle, table, out, partial, joined
    )


def reduce_pieces(blocks, sources, pieces, columns, phases, weights, partial):
    rows_here = pieces[0].shape[-2]
    terms, width = columns[0].shape
    ranks = lax.axis_size("rank")
    span = width // ranks
    rank_at = lax.axis_index("rank")
    starts = [(rank_at ^ other) * span for other in HELD_PARTS]

    def fetch(part, row, lane):
        quarters, _, _ = sources[row // rows_here]
        row = pl.ds(row % rows_here, 1)
        if quarters is None:
            return pieces[0][row, pl.ds(pl.multiple_of(starts[part] + lane, LANES), LANES)]
        number, index = quarters[part]
        return pieces[number][index, row, pl.ds(pl.multiple_of(lane, LANES), LANES)]

    factors_at = made_factors(columns, phases, weights)
    rows = len(sources) * rows_here
    reduce_rows(blocks, rows, terms, fetch, factors_at, starts, span, partial)


def finish_pieces(blocks, sources, copies, row_factors, twiddle, table, out, partial, joined):
    rows = partial.shape[2]
    rows_here = rows // len(sources)
    bases = [comp_of(step, flipped) * rows_here for _, step, flipped in sources]

    def row_at(row):
        return bases[row // rows_here] + row % rows_here

    for copy in copies:
        copy.wait()
    transform_rows(blocks, rows, row_at, row_factors, twiddle, table, out, partial, joined)


def gathered_kernel(blocks, groups, pieces, *refs):
    columns, row_factors, tables, refs = refs[0:2], refs[2:4], refs[4:6], refs[6:]
    out, partial, joined, phases, weights, twiddle, table, arrivals = refs
    copies = start_tables(tables, (twiddle, table), arrivals)
    make_phases(groups, phases)
    parts, rows_here, span = pieces.shape[1:]

    def fetch(part, row, lane):
        place = pl.ds(pl.multiple_of(lane, LANES), LANES)
        return pieces[row // rows_here, part, pl.ds(row % rows_here, 1), place]

    base = pl.program_id(0) * 8
    starts = [part * span for part in range(parts)]
    terms = columns[0].shape[0]
    factors_at = made_factors(columns, phases, weights)
    reduce_rows(blocks, 8, terms, fetch, factors_at, starts, span, partial)
    for copy in copies:
        copy.wait()
    transform_rows(
        blocks,
        8,
        lambda row: base + row,
        row_factors,
        twiddle,
        table,
        out.at[0],
        partial,
        joined,
    )


def pass_kernel(*refs):
    del refs


def after(values, earlier):
    anywhere = pl.BlockSpec(memory_space=pl.ANY)
    operands = [pltpu.with_memory_space_constraint(x, pltpu.VMEM) for x in (*values, earlier)]
    return pl.pallas_call(
        pass_kernel,
        out_shape=[jax.ShapeDtypeStruct(value.shape, value.dtype) for value in values],
        in_specs=[anywhere] * len(operands),
        out_specs=[anywhere] * len(values),
        input_output_aliases={k: k for k in range(len(values))},
    )(*operands)


def convolve_kernel(blocks, rows_here, layout, tile_count, *refs):
    tiles = refs[:tile_count]
    back, out, spectrum, product, mixed = refs[tile_count:]
    total_rows = spectrum.shape[2] - PAD
    terms = spectrum.shape[3]
    spectrum[:, :, pl.ds(0, PAD)] = jnp.zeros((2 * blocks, 3, PAD, terms, LANES), jnp.float32)
    moves = []
    for number, tile in enumerate(tiles):
        for at in range(tile.shape[0]):
            for first in range(0, tile.shape[3], rows_here):
                moves.append((tile, at, first))
    comps = [comp_of(*layout[k]) if layout else k for k in range(len(moves))]

    def collect(plane, carry):
        for (tile, at, first), comp in zip(moves, comps):
            real = tile[at, plane, 0, pl.ds(first, rows_here)]
            imag = tile[at, plane, 1, pl.ds(first, rows_here)]
            place = pl.ds(PAD + comp * rows_here, rows_here)
            spectrum[plane, 0, place] = real
            spectrum[plane, 1, place] = imag
            spectrum[plane, 2, place] = real + imag
        return carry

    lax.fori_loop(0, 2 * blocks, collect, 0)

    def step(at, sums, block, out_tile, whole):
        sums = list(sums)
        left_base = PAD + 4 * at
        right_base = PAD + 4 * (out_tile - at)
        for part in range(3):
            left = [spectrum[2 * block, part, left_base + k] for k in range(4)]
            right = {
                k: spectrum[2 * block + 1, part, right_base + k]
                for k in range(-3 if whole else 0, 4)
            }
            for row in range(4):
                for k in range(4 if whole else row + 1):
                    sums[row * 3 + part] += left[k] * right[row - k]
        return tuple(sums)

    def finish(sums, block, out_tile):
        for row in range(4):
            both_real, both_imag, crossed = sums[row * 3 : row * 3 + 3]
            base = (out_tile * 4 + row) * 2 * blocks + block
            product[base] = both_real - both_imag
            product[base + blocks] = crossed - both_real - both_imag

    zeros = (jnp.zeros((terms, LANES), jnp.float32),) * 12
    out_tiles = total_rows // 4

    def convolve_block(block, carry):
        for out_tile in range(out_tiles):
            sums = zeros
            for at in range(out_tile + 1):
                sums = step(at, sums, block, out_tile, at < out_tile)
            finish(sums, block, out_tile)
        return carry

    def convolve_tile(index, carry):
        block = lax.rem(index, blocks)
        out_tile = lax.div(index, blocks)
        sums = lax.fori_loop(
            0, out_tile + 1, lambda at, sums: step(at, sums, block, out_tile, True), zeros
        )
        finish(sums, block, out_tile)
        return carry

    if total_rows <= 32:
        lax.fori_loop(0, blocks, convolve_block, 0)
    else:
        lax.fori_loop(0, out_tiles * blocks, convolve_tile, 0)

    def gather_terms(at, carry):
        tiles = [product[at * 8 + k] for k in range(8)]
        summed = jnp.sum(jnp.stack(tiles), axis=1)
        if blocks == 4:
            turned = jnp.concatenate([summed[blocks:], -summed[:blocks]], axis=0)
        else:
            swapped = [
                tiles[k + blocks] if (k // blocks) % 2 == 0 else -tiles[k - blocks]
                for k in range(8)
            ]
            turned = jnp.sum(jnp.stack(swapped), axis=1)
        place = pl.ds(pl.multiple_of(at * 8, 8), 8)
        mixed[place, pl.ds(0, LANES)] = summed
        mixed[place, pl.ds(LANES, LANES)] = turned
        return carry

    lax.fori_loop(0, total_rows * 2 * blocks // 8, gather_terms, 0, unroll=4)
    out[...] = dot_split(mixed[...], back[...])


def final_kernel(scaling, spread, inner_cos, inner_sin, outer, out):
    values = spread[...]
    stacked = jnp.concatenate([values * inner_cos[...], values * inner_sin[...]], axis=0)
    high, low = split_parts(stacked)
    joined = jnp.concatenate([high, low, high], axis=0)
    total = jnp.dot(outer[...], joined, preferred_element_type=jnp.float32)
    out[...] = total * scaling


def in_hbm(array):
    return pltpu.with_memory_space_constraint(array, pltpu.HBM)


def whole_call(kernel, out_shapes, scratch, operands, tables=(), kept=True):
    out_type = pltpu.VMEM if kept else jax.ShapeDtypeStruct
    operands = [pltpu.with_memory_space_constraint(operand, pltpu.VMEM) for operand in operands]
    return pl.pallas_call(
        kernel,
        out_shape=[out_type(shape, jnp.float32) for shape in out_shapes],
        in_specs=[pl.BlockSpec(memory_space=pltpu.VMEM)] * len(operands)
        + [pl.BlockSpec(memory_space=pltpu.HBM)] * len(tables),
        out_specs=[pl.BlockSpec(memory_space=pltpu.VMEM)] * len(out_shapes),
        scratch_shapes=scratch,
        compiler_params=pltpu.CompilerParams(vmem_limit_bytes=VMEM_BYTES),
    )(*operands, *[in_hbm(table) for table in tables])


def row_scratch(blocks, rows, terms, width, tables):
    return [
        pltpu.VMEM((4, blocks, rows, terms, LANES), jnp.float32),
        pltpu.VMEM((2 * blocks * rows * terms, 6 * LANES), jnp.bfloat16),
        pltpu.VMEM((2, width // LANES, LANES), jnp.float32),
        pltpu.VMEM((4, terms, width), jnp.float32),
        *[pltpu.VMEM(table.shape, table.dtype) for table in tables],
        pltpu.SemaphoreType.DMA((len(tables),)),
    ]


def spectra_by_exchange(density, blocks, groups, columns, row_factors, tables):
    rows_here, width = density.shape
    comps, ranks = lax.axis_size("comp"), lax.axis_size("rank")
    part = width // ranks
    lines = comps // 2
    terms = row_factors[0].shape[0]
    mine = lax.dynamic_slice_in_dim(density, lax.axis_index("rank") * part, part, 1)

    def along(block, step):
        pairs = [(c, ((c // 2 + step) % lines) * 2 + c % 2) for c in range(comps)]
        return lax.ppermute(block, "comp", pairs)

    def across(block):
        return lax.ppermute(block, "comp", [(c, c ^ 1) for c in range(comps)])

    def swapped(block, other):
        return lax.ppermute(block, "rank", [(r, r ^ other) for r in range(ranks)])

    def spectra(kernel, sources, operands, fetched):
        rows = rows_here * len(sources)
        (tile,) = whole_call(
            lambda *refs: kernel(blocks, groups, sources, *refs),
            [(2 * blocks, 2, rows, terms, LANES)],
            row_scratch(blocks, rows, terms, width, fetched),
            (*operands, *row_factors),
            fetched,
        )
        return tile

    def joined_spectra(pieces, sources):
        def kernel(blocks, groups, sources, *refs):
            pieces_kernel(blocks, groups, sources, len(pieces), *refs)

        return spectra(kernel, sources, (*pieces, *columns), tables)

    own_source = (None, 0, False)
    early = [(0, True)] + [(step, False) for step in range(1, lines)]
    late = [(step, True) for step in range(1, lines)]

    def quartered(places):
        return [(tuple((q, k) for q in range(4)), *place) for k, place in enumerate(places)]

    lined = [along(mine, step) for step in range(1, lines)]
    flipped_own = across(mine)
    own = spectra(own_kernel, [own_source], (), (*tables, density, *columns))
    (lined[lines // 2 - 1],) = after([lined[lines // 2 - 1]], own)
    near = jnp.stack([flipped_own, *lined])
    flipped = across(jnp.stack(lined))
    beyond = swapped(near, 2)
    ready = [near, beyond, swapped(near, 1), swapped(beyond, 1)]
    flipped_beyond = swapped(flipped, 2)
    flipped_beside = swapped(flipped, 1)
    first = joined_spectra(ready, quartered(early))
    (flipped_beyond,) = after([flipped_beyond], first)
    second = joined_spectra(
        [flipped, flipped_beyond, flipped_beside, swapped(flipped_beyond, 1)], quartered(late)
    )
    layout = [own_source[1:]] + early + late
    return [own[None], first[None], second[None]], layout


def spectra_by_gather(density, blocks, groups, columns, row_factors, tables):
    rows_here, width = density.shape
    comps, ranks = lax.axis_size("comp"), lax.axis_size("rank")
    terms = row_factors[0].shape[0]
    total_rows = rows_here * comps
    part = width // ranks
    mine = lax.dynamic_slice_in_dim(density, lax.axis_index("rank") * part, part, 1)
    gathered = lax.all_gather(mine, AXES, axis=0).reshape(comps, ranks, rows_here, part)
    tile_shape = (2 * blocks, 2, 8, terms, LANES)
    spectra = pl.pallas_call(
        lambda *refs: gathered_kernel(blocks, groups, *refs),
        grid=(total_rows // 8,),
        out_shape=jax.ShapeDtypeStruct((total_rows // 8, *tile_shape), jnp.float32),
        in_specs=[pl.BlockSpec((8 // rows_here, ranks, rows_here, part), lambda t: (t, 0, 0, 0))]
        + [pl.BlockSpec(memory_space=pltpu.VMEM)] * 4
        + [pl.BlockSpec(memory_space=pltpu.HBM)] * len(tables),
        out_specs=pl.BlockSpec((1, *tile_shape), lambda t: (t, 0, 0, 0, 0, 0)),
        scratch_shapes=row_scratch(blocks, 8, terms, width, tables),
        compiler_params=pltpu.CompilerParams(vmem_limit_bytes=VMEM_BYTES),
    )(gathered, *columns, *row_factors, *[in_hbm(table) for table in tables])
    return [spectra], None


def body(density, row_left, col_left, row_right, col_right):
    rows_here, width = density.shape
    comps = lax.axis_size("comp")
    devices = comps * lax.axis_size("rank")
    total_rows = rows_here * comps
    terms = row_left.shape[0]
    groups = min(devices, width // LANES)
    term_groups = devices // groups
    blocks = width // (groups * LANES)
    device_at = lax.axis_index(AXES)
    if term_groups > 1:
        term_at = lax.broadcasted_iota(jnp.int32, (terms, 1), 0)
        chosen = lax.div(term_at, terms // term_groups) == lax.div(device_at, groups)
        col_left = jnp.where(chosen, col_left, 0.0)
        col_right = jnp.where(chosen, col_right, 0.0)
    columns = (col_left, col_right)
    row_factors = (row_left, row_right)
    tables = (block_twiddles(blocks), split_rows(forward_table()))
    spectra = spectra_by_exchange if comps <= 8 else spectra_by_gather
    tiles, layout = spectra(density, blocks, groups, columns, row_factors, tables)

    out_rows = total_rows * 2 * blocks
    (sent,) = whole_call(
        lambda *refs: convolve_kernel(blocks, rows_here, layout, len(tiles), *refs),
        [(out_rows, LANES)],
        [
            pltpu.VMEM((2 * blocks, 3, PAD + total_rows, terms, LANES), jnp.float32),
            pltpu.VMEM((out_rows, terms, LANES), jnp.float32),
            pltpu.VMEM((out_rows, 2 * LANES), jnp.float32),
        ],
        (*tiles, split_rows(inverse_table())),
    )
    spread = lax.all_to_all(sent, AXES, split_axis=0, concat_axis=0, tiled=True)
    inner_cos, inner_sin, outer_table = final_tables(devices, groups, blocks, width)
    scaling = 0.5 / (math.sqrt(total_rows * width) * width)
    (result,) = whole_call(
        lambda *refs: final_kernel(scaling, *refs),
        [(width // LANES, LANES)],
        [],
        (
            spread,
            jnp.asarray(inner_cos, jnp.float32),
            jnp.asarray(inner_sin, jnp.float32),
            split_columns(outer_table),
        ),
        kept=False,
    )
    return result.reshape(1, width)


def solution(mesh):
    return jax.shard_map(
        body,
        mesh=mesh,
        in_specs=(P("comp", None), P(), P(), P(), P()),
        out_specs=P(AXES, None),
        check_vma=False,
    )
```

```python
import math

import jax
import jax.numpy as jnp
import numpy as np
from jax import lax
from jax.experimental import pallas as pl
from jax.experimental.pallas import tpu as pltpu
from jax.sharding import PartitionSpec as P

LANES = 128
VMEM_BYTES = 16 * 1024 * 1024
AXES = ("comp", "rank")
PAD = 4
HELD_PARTS = (0, 2, 1, 3)


def split_parts(values):
    high = values.astype(jnp.bfloat16)
    low = (values - high.astype(jnp.float32)).astype(jnp.bfloat16)
    return high, low


def split_rows(table):
    high, low = split_parts(jnp.asarray(table, jnp.float32))
    return jnp.concatenate([high, high, low], axis=0)


def split_columns(table):
    high, low = split_parts(jnp.asarray(table, jnp.float32))
    return jnp.concatenate([high, high, low], axis=1)


def dot_split(rows, table):
    high, low = split_parts(rows)
    joined = jnp.concatenate([high, low, high], axis=1)
    return jnp.dot(joined, table, preferred_element_type=jnp.float32)


def forward_table():
    angles = 2.0 * np.pi * np.outer(np.arange(LANES), np.arange(LANES)) / LANES
    cosine, sine = np.cos(angles), np.sin(angles)
    return np.block([[cosine, -sine], [sine, cosine]])


def inverse_table():
    angles = 2.0 * np.pi * np.outer(np.arange(LANES), np.arange(LANES)) / LANES
    return np.concatenate([np.cos(angles), -np.sin(angles)], axis=0)


def block_twiddles(blocks):
    angles = 2.0 * np.pi * np.outer(np.arange(blocks), np.arange(LANES)) / (blocks * LANES)
    table = np.stack([np.cos(angles), -np.sin(angles)], axis=1)
    return jnp.asarray(
        np.broadcast_to(table[:, :, None, :], (blocks, 2, 8, LANES)), jnp.float32
    )


def final_tables(devices, groups, blocks, width):
    owner = np.arange(devices) % groups
    frequency = (owner[:, None] + groups * np.arange(blocks)[None, :]).astype(np.float64) + 0.25
    frequency = np.broadcast_to(frequency[:, None, :], (devices, 2, blocks))
    inner = 2.0 * np.pi * frequency[..., None] * np.arange(LANES) / width
    rows = devices * 2 * blocks
    inner_cos = np.cos(inner).reshape(rows, LANES)
    inner_sin = np.sin(inner).reshape(rows, LANES)
    outer_count = width // LANES
    outer = 2.0 * np.pi * frequency * LANES / width
    outer = np.arange(outer_count)[:, None] * outer.reshape(1, rows)
    is_real = np.broadcast_to(np.array([True, False])[None, :, None], (devices, 2, blocks))
    is_real = is_real.reshape(1, rows)
    with_cos = np.where(is_real, np.cos(outer), -np.sin(outer))
    with_sin = np.where(is_real, -np.sin(outer), -np.cos(outer))
    return inner_cos, inner_sin, np.concatenate([with_cos, with_sin], axis=1)


def block_fourier(reals, imags):
    count = len(reals)
    if count == 1:
        return reals, imags
    if count == 2:
        return (
            [reals[0] + reals[1], reals[0] - reals[1]],
            [imags[0] + imags[1], imags[0] - imags[1]],
        )
    even_real, odd_real = reals[0] + reals[2], reals[0] - reals[2]
    even_imag, odd_imag = imags[0] + imags[2], imags[0] - imags[2]
    pair_real, gap_real = reals[1] + reals[3], reals[1] - reals[3]
    pair_imag, gap_imag = imags[1] + imags[3], imags[1] - imags[3]
    return (
        [even_real + pair_real, odd_real + gap_imag, even_real - pair_real, odd_real - gap_imag],
        [even_imag + pair_imag, odd_imag - gap_real, even_imag - pair_imag, odd_imag + gap_real],
    )


def reduce_rows(blocks, rows, terms, fetch, factors_at, starts, span, partial, before=None):
    inner = blocks * LANES
    outer = span // inner
    unroll = math.gcd(16, outer)

    def reduce_block(block, first, count):
        sums = (jnp.zeros((terms, LANES), jnp.float32),) * (4 * count)
        if before is not None:
            sums = tuple(
                before[k, block, first + row] for row in range(count) for k in range(4)
            )
        for part, start in enumerate(starts):

            def step(at, sums, part=part, start=start):
                sums = list(sums)
                for extra in range(unroll):
                    lane = (at * unroll + extra) * inner + block * LANES
                    factors = factors_at(start + lane, first == 0)
                    for row in range(count):
                        value = fetch(part, first + row, lane)
                        value = jnp.broadcast_to(value, (terms, LANES))
                        for k in range(4):
                            sums[row * 4 + k] += value * factors[k]
                return tuple(sums)

            sums = lax.fori_loop(0, outer // unroll, step, sums)
        for row in range(count):
            for k in range(4):
                partial[k, block, first + row] = sums[row * 4 + k]

    def reduce_tiles(block, carry):
        for first in range(0, rows, 8):
            reduce_block(block, first, min(8, rows - first))
        return carry

    lax.fori_loop(0, blocks, reduce_tiles, 0)


def transform_rows(blocks, rows, row_at, row_factors, twiddle, table, out, partial, joined):
    terms, total_rows = row_factors[0].shape
    lanes = lax.broadcasted_iota(jnp.int32, (terms, total_rows), 1)

    def butterfly(row, side):
        picked = jnp.where(lanes == row_at(row), row_factors[side][...], 0.0)
        factor = jnp.sum(picked, axis=1, keepdims=True)
        factor = jnp.broadcast_to(factor, (terms, LANES))
        reals = [partial[2 * side, block, row] * factor for block in range(blocks)]
        imags = [partial[2 * side + 1, block, row] * factor for block in range(blocks)]
        reals, imags = block_fourier(reals, imags)
        for block in range(1, blocks):
            real, imag = reals[block], imags[block]
            cosine, sine = twiddle[block, 0], twiddle[block, 1]
            reals[block] = real * cosine - imag * sine
            imags[block] = real * sine + imag * cosine
        return reals, imags

    def butterfly_pair(pair):
        for side in range(2):
            both = [butterfly(pair * 2 + extra, side) for extra in range(2)]
            for block in range(blocks):
                base = ((block * 2 + side) * rows + pair * 2) * terms
                place = pl.ds(base, 2 * terms)
                for part in range(2):
                    values = jnp.concatenate([both[0][part][block], both[1][part][block]], axis=0)
                    high, low = split_parts(values)
                    for third, piece in enumerate((high, low, high)):
                        joined[place, pl.ds((third * 2 + part) * LANES, LANES)] = piece

    for pair in range(rows // 2):
        butterfly_pair(pair)
    planes = 2 * blocks
    step = planes * rows * terms
    while step > 512:
        step //= 2
    plane_step = step // (rows * terms)

    def transform(at, carry):
        place = pl.ds(pl.multiple_of(at * step, 16), step)
        total = jnp.dot(joined[place, :], table[...], preferred_element_type=jnp.float32)
        total = total.reshape(plane_step, rows, terms, 2 * LANES)
        place = pl.ds(at * plane_step, plane_step)
        out[place, 0] = total[..., :LANES]
        out[place, 1] = total[..., LANES:]
        return carry

    lax.fori_loop(0, planes // plane_step, transform, 0)


def comp_of(step, flipped):
    lines = lax.axis_size("comp") // 2
    comp_at = lax.axis_index("comp")
    line = lax.rem(lax.div(comp_at, 2) + lines - step, lines)
    side = lax.rem(comp_at, 2)
    return line * 2 + (1 - side if flipped else side)


def make_phases(groups, phases):
    width = phases.shape[1] * LANES
    device_at = lax.axis_index("comp") * lax.axis_size("rank") + lax.axis_index("rank")
    odd = 4 * lax.rem(device_at, groups) + 1
    shape = phases.shape[1:]
    cells = lax.broadcasted_iota(jnp.int32, shape, 0) * LANES
    cells = cells + lax.broadcasted_iota(jnp.int32, shape, 1)
    turns = (cells * odd) & (4 * width - 1)
    turns = jnp.where(turns >= 2 * width, turns - 4 * width, turns)
    angles = turns.astype(jnp.float32) * (2.0 * math.pi / (4 * width))
    phases[0] = jnp.cos(angles)
    phases[1] = -jnp.sin(angles)


def made_factors(columns, phases, kept):
    terms = columns[0].shape[0]

    def factors_at(lane, first):
        place = pl.ds(pl.multiple_of(lane, LANES), LANES)
        if not first:
            return [kept[k, :, place] for k in range(4)]
        turn = pl.ds(lax.div(lane, LANES), 1)
        factors = [
            column[:, place] * jnp.broadcast_to(phases[part, turn, :], (terms, LANES))
            for column in columns
            for part in range(2)
        ]
        for k in range(4):
            kept[k, :, place] = factors[k]
        return factors

    return factors_at


def start_tables(tables, held, arrivals):
    copies = [
        pltpu.make_async_copy(table, place, arrivals.at[k])
        for k, (table, place) in enumerate(zip(tables, held))
    ]
    for copy in copies:
        copy.start()
    return copies


def pieces_kernel(blocks, groups, sources, count, *refs):
    pieces, refs = refs[:count], refs[count:]
    columns, row_factors, tables, refs = refs[0:2], refs[2:4], refs[4:6], refs[6:]
    out, partial, joined, phases, weights, twiddle, table, arrivals = refs
    copies = start_tables(tables, (twiddle, table), arrivals)
    make_phases(groups, phases)
    reduce_pieces(blocks, sources, pieces, columns, phases, weights, partial)
    finish_pieces(
        blocks, sources, copies, row_factors, twiddle, table, out, partial, joined
    )


def own_kernel(blocks, groups, sources, *refs):
    row_factors, sent, refs = refs[1:3], refs[3:8], refs[8:]
    out, partial, joined, phases, weights = refs[:5]
    held, arrivals = refs[5:10], refs[10]
    copies = start_tables(sent, held, arrivals)
    make_phases(groups, phases)
    for copy in copies[2:]:
        copy.wait()
    twiddle, table, own, *columns = held
    reduce_pieces(blocks, sources, [own], columns, phases, weights, partial)
    finish_pieces(
        blocks, sources, copies[:2], row_factors, twiddle, table, out, partial, joined
    )


def reduce_pieces(
    blocks, sources, pieces, columns, phases, weights, partial, parts=(0, 1, 2, 3)
):
    rows_here = pieces[0].shape[-2]
    terms, width = columns[0].shape
    ranks = lax.axis_size("rank")
    span = width // ranks
    rank_at = lax.axis_index("rank")
    starts = [(rank_at ^ HELD_PARTS[part]) * span for part in parts]

    def fetch(part, row, lane):
        quarters, _, _ = sources[row // rows_here]
        row = pl.ds(row % rows_here, 1)
        if quarters is None:
            return pieces[0][row, pl.ds(pl.multiple_of(starts[part] + lane, LANES), LANES)]
        number, index = quarters[parts[part]]
        return pieces[number][index, row, pl.ds(pl.multiple_of(lane, LANES), LANES)]

    factors_at = made_factors(columns, phases, weights)
    rows = len(sources) * rows_here
    reduce_rows(blocks, rows, terms, fetch, factors_at, starts, span, partial)


def ahead_kernel(blocks, groups, sources, *refs):
    pieces, columns, (partial, quarter, phases, weights) = refs[0:3], refs[3:5], refs[5:]
    make_phases(groups, phases)
    reduce_pieces(
        blocks, sources, pieces, columns, phases, weights, partial, parts=(0, 1, 2)
    )
    factors_at = made_factors(columns, phases, weights)
    span = quarter.shape[2]
    start = (lax.axis_index("rank") ^ HELD_PARTS[3]) * span

    def weigh(at, carry):
        lane = at * LANES
        for k, factor in enumerate(factors_at(start + lane, True)):
            quarter[k, :, pl.ds(pl.multiple_of(lane, LANES), LANES)] = factor
        return carry

    lax.fori_loop(0, span // LANES, weigh, 0, unroll=4)


def last_kernel(blocks, groups, sources, *refs):
    del groups
    piece, before, quarter = refs[0:3]
    row_factors, tables, refs = refs[3:5], refs[5:7], refs[7:]
    out, partial, joined, _, _, twiddle, table, arrivals = refs
    copies = start_tables(tables, (twiddle, table), arrivals)
    rows_here = piece.shape[-2]
    terms, span = quarter.shape[1:]

    def fetch(part, row, lane):
        _, index = sources[row // rows_here][0][3]
        place = pl.ds(pl.multiple_of(lane, LANES), LANES)
        return piece[index, pl.ds(row % rows_here, 1), place]

    def factors_at(lane, first):
        place = pl.ds(pl.multiple_of(lane, LANES), LANES)
        return [quarter[k, :, place] for k in range(4)]

    rows = len(sources) * rows_here
    reduce_rows(blocks, rows, terms, fetch, factors_at, [0], span, partial, before)
    finish_pieces(
        blocks, sources, copies, row_factors, twiddle, table, out, partial, joined
    )


def finish_pieces(blocks, sources, copies, row_factors, twiddle, table, out, partial, joined):
    rows = partial.shape[2]
    rows_here = rows // len(sources)
    bases = [comp_of(step, flipped) * rows_here for _, step, flipped in sources]

    def row_at(row):
        return bases[row // rows_here] + row % rows_here

    for copy in copies:
        copy.wait()
    transform_rows(blocks, rows, row_at, row_factors, twiddle, table, out, partial, joined)


def gathered_kernel(blocks, groups, pieces, *refs):
    columns, row_factors, tables, refs = refs[0:2], refs[2:4], refs[4:6], refs[6:]
    out, partial, joined, phases, weights, twiddle, table, arrivals = refs
    copies = start_tables(tables, (twiddle, table), arrivals)
    make_phases(groups, phases)
    parts, rows_here, span = pieces.shape[1:]

    def fetch(part, row, lane):
        place = pl.ds(pl.multiple_of(lane, LANES), LANES)
        return pieces[row // rows_here, part, pl.ds(row % rows_here, 1), place]

    base = pl.program_id(0) * 8
    starts = [part * span for part in range(parts)]
    terms = columns[0].shape[0]
    factors_at = made_factors(columns, phases, weights)
    reduce_rows(blocks, 8, terms, fetch, factors_at, starts, span, partial)
    for copy in copies:
        copy.wait()
    transform_rows(
        blocks,
        8,
        lambda row: base + row,
        row_factors,
        twiddle,
        table,
        out.at[0],
        partial,
        joined,
    )


def pass_kernel(*refs):
    del refs


def after(values, earlier):
    anywhere = pl.BlockSpec(memory_space=pl.ANY)
    operands = [pltpu.with_memory_space_constraint(x, pltpu.VMEM) for x in (*values, earlier)]
    return pl.pallas_call(
        pass_kernel,
        out_shape=[jax.ShapeDtypeStruct(value.shape, value.dtype) for value in values],
        in_specs=[anywhere] * len(operands),
        out_specs=[anywhere] * len(values),
        input_output_aliases={k: k for k in range(len(values))},
    )(*operands)


def convolve_kernel(blocks, rows_here, layout, tile_count, *refs):
    tiles = refs[:tile_count]
    back, out, spectrum, product, mixed = refs[tile_count:]
    total_rows = spectrum.shape[2] - PAD
    terms = spectrum.shape[3]
    spectrum[:, :, pl.ds(0, PAD)] = jnp.zeros((2 * blocks, 3, PAD, terms, LANES), jnp.float32)
    moves = []
    for number, tile in enumerate(tiles):
        for at in range(tile.shape[0]):
            for first in range(0, tile.shape[3], rows_here):
                moves.append((tile, at, first))
    comps = [comp_of(*layout[k]) if layout else k for k in range(len(moves))]

    def collect(plane, carry):
        for (tile, at, first), comp in zip(moves, comps):
            real = tile[at, plane, 0, pl.ds(first, rows_here)]
            imag = tile[at, plane, 1, pl.ds(first, rows_here)]
            place = pl.ds(PAD + comp * rows_here, rows_here)
            spectrum[plane, 0, place] = real
            spectrum[plane, 1, place] = imag
            spectrum[plane, 2, place] = real + imag
        return carry

    lax.fori_loop(0, 2 * blocks, collect, 0)

    def step(at, sums, block, out_tile, whole):
        sums = list(sums)
        left_base = PAD + 4 * at
        right_base = PAD + 4 * (out_tile - at)
        for part in range(3):
            left = [spectrum[2 * block, part, left_base + k] for k in range(4)]
            right = {
                k: spectrum[2 * block + 1, part, right_base + k]
                for k in range(-3 if whole else 0, 4)
            }
            for row in range(4):
                for k in range(4 if whole else row + 1):
                    sums[row * 3 + part] += left[k] * right[row - k]
        return tuple(sums)

    def finish(sums, block, out_tile):
        for row in range(4):
            both_real, both_imag, crossed = sums[row * 3 : row * 3 + 3]
            base = (out_tile * 4 + row) * 2 * blocks + block
            product[base] = both_real - both_imag
            product[base + blocks] = crossed - both_real - both_imag

    zeros = (jnp.zeros((terms, LANES), jnp.float32),) * 12
    out_tiles = total_rows // 4

    def convolve_block(block, carry):
        for out_tile in range(out_tiles):
            sums = zeros
            for at in range(out_tile + 1):
                sums = step(at, sums, block, out_tile, at < out_tile)
            finish(sums, block, out_tile)
        return carry

    def convolve_tile(index, carry):
        block = lax.rem(index, blocks)
        out_tile = lax.div(index, blocks)
        sums = lax.fori_loop(
            0, out_tile + 1, lambda at, sums: step(at, sums, block, out_tile, True), zeros
        )
        finish(sums, block, out_tile)
        return carry

    if total_rows <= 32:
        lax.fori_loop(0, blocks, convolve_block, 0)
    else:
        lax.fori_loop(0, out_tiles * blocks, convolve_tile, 0)

    def gather_terms(at, carry):
        tiles = [product[at * 8 + k] for k in range(8)]
        summed = jnp.sum(jnp.stack(tiles), axis=1)
        if blocks == 4:
            turned = jnp.concatenate([summed[blocks:], -summed[:blocks]], axis=0)
        else:
            swapped = [
                tiles[k + blocks] if (k // blocks) % 2 == 0 else -tiles[k - blocks]
                for k in range(8)
            ]
            turned = jnp.sum(jnp.stack(swapped), axis=1)
        place = pl.ds(pl.multiple_of(at * 8, 8), 8)
        mixed[place, pl.ds(0, LANES)] = summed
        mixed[place, pl.ds(LANES, LANES)] = turned
        return carry

    lax.fori_loop(0, total_rows * 2 * blocks // 8, gather_terms, 0, unroll=4)
    out[...] = dot_split(mixed[...], back[...])


def final_kernel(scaling, spread, inner_cos, inner_sin, outer, out):
    values = spread[...]
    stacked = jnp.concatenate([values * inner_cos[...], values * inner_sin[...]], axis=0)
    high, low = split_parts(stacked)
    joined = jnp.concatenate([high, low, high], axis=0)
    total = jnp.dot(outer[...], joined, preferred_element_type=jnp.float32)
    out[...] = total * scaling


def in_hbm(array):
    return pltpu.with_memory_space_constraint(array, pltpu.HBM)


def whole_call(kernel, out_shapes, scratch, operands, tables=(), kept=True):
    out_type = pltpu.VMEM if kept else jax.ShapeDtypeStruct
    operands = [pltpu.with_memory_space_constraint(operand, pltpu.VMEM) for operand in operands]
    return pl.pallas_call(
        kernel,
        out_shape=[out_type(shape, jnp.float32) for shape in out_shapes],
        in_specs=[pl.BlockSpec(memory_space=pltpu.VMEM)] * len(operands)
        + [pl.BlockSpec(memory_space=pltpu.HBM)] * len(tables),
        out_specs=[pl.BlockSpec(memory_space=pltpu.VMEM)] * len(out_shapes),
        scratch_shapes=scratch,
        compiler_params=pltpu.CompilerParams(vmem_limit_bytes=VMEM_BYTES),
    )(*operands, *[in_hbm(table) for table in tables])


def row_scratch(blocks, rows, terms, width, tables):
    return [
        pltpu.VMEM((4, blocks, rows, terms, LANES), jnp.float32),
        pltpu.VMEM((2 * blocks * rows * terms, 6 * LANES), jnp.bfloat16),
        pltpu.VMEM((2, width // LANES, LANES), jnp.float32),
        pltpu.VMEM((4, terms, width), jnp.float32),
        *[pltpu.VMEM(table.shape, table.dtype) for table in tables],
        *([pltpu.SemaphoreType.DMA((len(tables),))] if tables else []),
    ]


def spectra_by_exchange(density, blocks, groups, columns, row_factors, tables):
    rows_here, width = density.shape
    comps, ranks = lax.axis_size("comp"), lax.axis_size("rank")
    part = width // ranks
    lines = comps // 2
    terms = row_factors[0].shape[0]
    mine = lax.dynamic_slice_in_dim(density, lax.axis_index("rank") * part, part, 1)

    def along(block, step):
        pairs = [(c, ((c // 2 + step) % lines) * 2 + c % 2) for c in range(comps)]
        return lax.ppermute(block, "comp", pairs)

    def across(block):
        return lax.ppermute(block, "comp", [(c, c ^ 1) for c in range(comps)])

    def swapped(block, other):
        return lax.ppermute(block, "rank", [(r, r ^ other) for r in range(ranks)])

    def spectra(kernel, sources, operands, fetched):
        rows = rows_here * len(sources)
        (tile,) = whole_call(
            lambda *refs: kernel(blocks, groups, sources, *refs),
            [(2 * blocks, 2, rows, terms, LANES)],
            row_scratch(blocks, rows, terms, width, fetched),
            (*operands, *row_factors),
            fetched,
        )
        return tile

    def joined_spectra(pieces, sources):
        def kernel(blocks, groups, sources, *refs):
            pieces_kernel(blocks, groups, sources, len(pieces), *refs)

        return spectra(kernel, sources, (*pieces, *columns), tables)

    own_source = (None, 0, False)
    early = [(0, True)] + [(step, False) for step in range(1, lines)]
    late = [(step, True) for step in range(1, lines)]

    def quartered(places):
        return [(tuple((q, k) for q in range(4)), *place) for k, place in enumerate(places)]

    lined = [along(mine, step) for step in range(1, lines)]
    near = jnp.stack([across(mine), *lined])
    flipped = across(jnp.stack(lined))
    beyond, beside = swapped(near, 2), swapped(near, 1)
    flipped_beyond, flipped_beside = swapped(flipped, 2), swapped(flipped, 1)
    own = spectra(own_kernel, [own_source], (near,), (*tables, density, *columns))
    (beyond,) = after([beyond], own)
    first = joined_spectra([near, beyond, beside, swapped(beyond, 1)], quartered(early))
    (flipped_beyond,) = after([flipped_beyond], first)
    late_sources = quartered(late)
    ahead = whole_call(
        lambda *refs: ahead_kernel(blocks, groups, late_sources, *refs),
        [(4, blocks, rows_here * len(late), terms, LANES), (4, terms, part)],
        row_scratch(blocks, rows_here, terms, width, ())[2:4],
        (flipped, flipped_beyond, flipped_beside, *columns),
    )
    last = swapped(flipped_beyond, 1)
    second = spectra(last_kernel, late_sources, (last, *ahead), tables)
    layout = [own_source[1:]] + early + late
    return [own[None], first[None], second[None]], layout


def spectra_by_gather(density, blocks, groups, columns, row_factors, tables):
    rows_here, width = density.shape
    comps, ranks = lax.axis_size("comp"), lax.axis_size("rank")
    terms = row_factors[0].shape[0]
    total_rows = rows_here * comps
    part = width // ranks
    mine = lax.dynamic_slice_in_dim(density, lax.axis_index("rank") * part, part, 1)
    gathered = lax.all_gather(mine, AXES, axis=0).reshape(comps, ranks, rows_here, part)
    tile_shape = (2 * blocks, 2, 8, terms, LANES)
    spectra = pl.pallas_call(
        lambda *refs: gathered_kernel(blocks, groups, *refs),
        grid=(total_rows // 8,),
        out_shape=jax.ShapeDtypeStruct((total_rows // 8, *tile_shape), jnp.float32),
        in_specs=[pl.BlockSpec((8 // rows_here, ranks, rows_here, part), lambda t: (t, 0, 0, 0))]
        + [pl.BlockSpec(memory_space=pltpu.VMEM)] * 4
        + [pl.BlockSpec(memory_space=pltpu.HBM)] * len(tables),
        out_specs=pl.BlockSpec((1, *tile_shape), lambda t: (t, 0, 0, 0, 0, 0)),
        scratch_shapes=row_scratch(blocks, 8, terms, width, tables),
        compiler_params=pltpu.CompilerParams(vmem_limit_bytes=VMEM_BYTES),
    )(gathered, *columns, *row_factors, *[in_hbm(table) for table in tables])
    return [spectra], None


def body(density, row_left, col_left, row_right, col_right):
    rows_here, width = density.shape
    comps = lax.axis_size("comp")
    devices = comps * lax.axis_size("rank")
    total_rows = rows_here * comps
    terms = row_left.shape[0]
    groups = min(devices, width // LANES)
    term_groups = devices // groups
    blocks = width // (groups * LANES)
    device_at = lax.axis_index(AXES)
    if term_groups > 1:
        term_at = lax.broadcasted_iota(jnp.int32, (terms, 1), 0)
        chosen = lax.div(term_at, terms // term_groups) == lax.div(device_at, groups)
        col_left = jnp.where(chosen, col_left, 0.0)
        col_right = jnp.where(chosen, col_right, 0.0)
    columns = (col_left, col_right)
    row_factors = (row_left, row_right)
    tables = (block_twiddles(blocks), split_rows(forward_table()))
    spectra = spectra_by_exchange if comps <= 8 else spectra_by_gather
    tiles, layout = spectra(density, blocks, groups, columns, row_factors, tables)

    out_rows = total_rows * 2 * blocks
    (sent,) = whole_call(
        lambda *refs: convolve_kernel(blocks, rows_here, layout, len(tiles), *refs),
        [(out_rows, LANES)],
        [
            pltpu.VMEM((2 * blocks, 3, PAD + total_rows, terms, LANES), jnp.float32),
            pltpu.VMEM((out_rows, terms, LANES), jnp.float32),
            pltpu.VMEM((out_rows, 2 * LANES), jnp.float32),
        ],
        (*tiles, split_rows(inverse_table())),
    )
    spread = lax.all_to_all(sent, AXES, split_axis=0, concat_axis=0, tiled=True)
    inner_cos, inner_sin, outer_table = final_tables(devices, groups, blocks, width)
    scaling = 0.5 / (math.sqrt(total_rows * width) * width)
    (result,) = whole_call(
        lambda *refs: final_kernel(scaling, *refs),
        [(width // LANES, LANES)],
        [],
        (
            spread,
            jnp.asarray(inner_cos, jnp.float32),
            jnp.asarray(inner_sin, jnp.float32),
            split_columns(outer_table),
        ),
        kept=False,
    )
    return result.reshape(1, width)


def solution(mesh):
    return jax.shard_map(
        body,
        mesh=mesh,
        in_specs=(P("comp", None), P(), P(), P(), P()),
        out_specs=P(AXES, None),
        check_vma=False,
    )
```

```python
import math

import jax
import jax.numpy as jnp
import numpy as np
from jax import lax
from jax.experimental import pallas as pl
from jax.experimental.pallas import tpu as pltpu
from jax.sharding import PartitionSpec as P

LANES = 128
VMEM_BYTES = 16 * 1024 * 1024
AXES = ("comp", "rank")
PAD = 4
HELD_PARTS = (0, 2, 1, 3)


def split_parts(values):
    high = values.astype(jnp.bfloat16)
    low = (values - high.astype(jnp.float32)).astype(jnp.bfloat16)
    return high, low


def split_rows(table):
    high, low = split_parts(jnp.asarray(table, jnp.float32))
    return jnp.concatenate([high, high, low], axis=0)


def split_columns(table):
    high, low = split_parts(jnp.asarray(table, jnp.float32))
    return jnp.concatenate([high, high, low], axis=1)


def dot_split(rows, table):
    high, low = split_parts(rows)
    joined = jnp.concatenate([high, low, high], axis=1)
    return jnp.dot(joined, table, preferred_element_type=jnp.float32)


def forward_table():
    angles = 2.0 * np.pi * np.outer(np.arange(LANES), np.arange(LANES)) / LANES
    cosine, sine = np.cos(angles), np.sin(angles)
    return np.block([[cosine, -sine], [sine, cosine]])


def inverse_table():
    angles = 2.0 * np.pi * np.outer(np.arange(LANES), np.arange(LANES)) / LANES
    return np.concatenate([np.cos(angles), -np.sin(angles)], axis=0)


def block_twiddles(blocks):
    angles = 2.0 * np.pi * np.outer(np.arange(blocks), np.arange(LANES)) / (blocks * LANES)
    table = np.stack([np.cos(angles), -np.sin(angles)], axis=1)
    return jnp.asarray(
        np.broadcast_to(table[:, :, None, :], (blocks, 2, 8, LANES)), jnp.float32
    )


def final_tables(devices, groups, blocks, width):
    owner = np.arange(devices) % groups
    frequency = (owner[:, None] + groups * np.arange(blocks)[None, :]).astype(np.float64) + 0.25
    frequency = np.broadcast_to(frequency[:, None, :], (devices, 2, blocks))
    inner = 2.0 * np.pi * frequency[..., None] * np.arange(LANES) / width
    rows = devices * 2 * blocks
    inner_cos = np.cos(inner).reshape(rows, LANES)
    inner_sin = np.sin(inner).reshape(rows, LANES)
    outer_count = width // LANES
    outer = 2.0 * np.pi * frequency * LANES / width
    outer = np.arange(outer_count)[:, None] * outer.reshape(1, rows)
    is_real = np.broadcast_to(np.array([True, False])[None, :, None], (devices, 2, blocks))
    is_real = is_real.reshape(1, rows)
    with_cos = np.where(is_real, np.cos(outer), -np.sin(outer))
    with_sin = np.where(is_real, -np.sin(outer), -np.cos(outer))
    return inner_cos, inner_sin, np.concatenate([with_cos, with_sin], axis=1)


def block_fourier(reals, imags):
    count = len(reals)
    if count == 1:
        return reals, imags
    if count == 2:
        return (
            [reals[0] + reals[1], reals[0] - reals[1]],
            [imags[0] + imags[1], imags[0] - imags[1]],
        )
    even_real, odd_real = reals[0] + reals[2], reals[0] - reals[2]
    even_imag, odd_imag = imags[0] + imags[2], imags[0] - imags[2]
    pair_real, gap_real = reals[1] + reals[3], reals[1] - reals[3]
    pair_imag, gap_imag = imags[1] + imags[3], imags[1] - imags[3]
    return (
        [even_real + pair_real, odd_real + gap_imag, even_real - pair_real, odd_real - gap_imag],
        [even_imag + pair_imag, odd_imag - gap_real, even_imag - pair_imag, odd_imag + gap_real],
    )


def reduce_rows(blocks, rows, terms, fetch, factors_at, starts, span, partial):
    inner = blocks * LANES
    outer = span // inner
    unroll = math.gcd(16, outer)

    def reduce_block(block, first, count):
        sums = (jnp.zeros((terms, LANES), jnp.float32),) * (4 * count)
        for part, start in enumerate(starts):

            def step(at, sums, part=part, start=start):
                sums = list(sums)
                for extra in range(unroll):
                    lane = (at * unroll + extra) * inner + block * LANES
                    factors = factors_at(start + lane, first == 0)
                    for row in range(count):
                        value = fetch(part, first + row, lane)
                        value = jnp.broadcast_to(value, (terms, LANES))
                        for k in range(4):
                            sums[row * 4 + k] += value * factors[k]
                return tuple(sums)

            sums = lax.fori_loop(0, outer // unroll, step, sums)
        for row in range(count):
            for k in range(4):
                partial[k, block, first + row] = sums[row * 4 + k]

    def reduce_tiles(block, carry):
        for first in range(0, rows, 8):
            reduce_block(block, first, min(8, rows - first))
        return carry

    lax.fori_loop(0, blocks, reduce_tiles, 0)


def transform_rows(blocks, rows, row_at, row_factors, twiddle, table, out, partial, joined):
    terms, total_rows = row_factors[0].shape
    lanes = lax.broadcasted_iota(jnp.int32, (terms, total_rows), 1)

    def butterfly(row, side):
        picked = jnp.where(lanes == row_at(row), row_factors[side][...], 0.0)
        factor = jnp.sum(picked, axis=1, keepdims=True)
        factor = jnp.broadcast_to(factor, (terms, LANES))
        reals = [partial[2 * side, block, row] * factor for block in range(blocks)]
        imags = [partial[2 * side + 1, block, row] * factor for block in range(blocks)]
        reals, imags = block_fourier(reals, imags)
        for block in range(1, blocks):
            real, imag = reals[block], imags[block]
            cosine, sine = twiddle[block, 0], twiddle[block, 1]
            reals[block] = real * cosine - imag * sine
            imags[block] = real * sine + imag * cosine
        return reals, imags

    def butterfly_pair(pair):
        for side in range(2):
            both = [butterfly(pair * 2 + extra, side) for extra in range(2)]
            for block in range(blocks):
                base = ((block * 2 + side) * rows + pair * 2) * terms
                place = pl.ds(base, 2 * terms)
                for part in range(2):
                    values = jnp.concatenate([both[0][part][block], both[1][part][block]], axis=0)
                    high, low = split_parts(values)
                    for third, piece in enumerate((high, low, high)):
                        joined[place, pl.ds((third * 2 + part) * LANES, LANES)] = piece

    for pair in range(rows // 2):
        butterfly_pair(pair)
    planes = 2 * blocks
    step = planes * rows * terms
    while step > 512:
        step //= 2
    plane_step = step // (rows * terms)

    def transform(at, carry):
        place = pl.ds(pl.multiple_of(at * step, 16), step)
        total = jnp.dot(joined[place, :], table[...], preferred_element_type=jnp.float32)
        total = total.reshape(plane_step, rows, terms, 2 * LANES)
        place = pl.ds(at * plane_step, plane_step)
        out[place, 0] = total[..., :LANES]
        out[place, 1] = total[..., LANES:]
        return carry

    lax.fori_loop(0, planes // plane_step, transform, 0)


def comp_of(step, flipped):
    lines = lax.axis_size("comp") // 2
    comp_at = lax.axis_index("comp")
    line = lax.rem(lax.div(comp_at, 2) + lines - step, lines)
    side = lax.rem(comp_at, 2)
    return line * 2 + (1 - side if flipped else side)


def make_phases(groups, phases):
    width = phases.shape[1] * LANES
    device_at = lax.axis_index("comp") * lax.axis_size("rank") + lax.axis_index("rank")
    odd = 4 * lax.rem(device_at, groups) + 1

    def turned(cells):
        turns = (cells * odd) & (4 * width - 1)
        turns = jnp.where(turns >= 2 * width, turns - 4 * width, turns)
        angles = turns.astype(jnp.float32) * (2.0 * math.pi / (4 * width))
        return jnp.cos(angles), -jnp.sin(angles)

    count = phases.shape[1] // 8
    rows = lax.broadcasted_iota(jnp.int32, (8, LANES), 0)
    fine_cos, fine_sin = turned(rows * LANES + lax.broadcasted_iota(jnp.int32, (8, LANES), 1))
    rows = lax.broadcasted_iota(jnp.int32, (count, LANES), 0)
    coarse_cos, coarse_sin = turned(rows * (8 * LANES))
    for tile in range(count):
        cosine = jnp.broadcast_to(coarse_cos[tile : tile + 1], (8, LANES))
        sine = jnp.broadcast_to(coarse_sin[tile : tile + 1], (8, LANES))
        phases[0, pl.ds(tile * 8, 8), :] = fine_cos * cosine - fine_sin * sine
        phases[1, pl.ds(tile * 8, 8), :] = fine_cos * sine + fine_sin * cosine


def made_factors(columns, phases, kept):
    terms = columns[0].shape[0]

    def factors_at(lane, first):
        place = pl.ds(pl.multiple_of(lane, LANES), LANES)
        if not first:
            return [kept[k, :, place] for k in range(4)]
        turn = pl.ds(lax.div(lane, LANES), 1)
        factors = [
            column[:, place] * jnp.broadcast_to(phases[part, turn, :], (terms, LANES))
            for column in columns
            for part in range(2)
        ]
        for k in range(4):
            kept[k, :, place] = factors[k]
        return factors

    return factors_at


def start_tables(tables, held, arrivals):
    copies = [
        pltpu.make_async_copy(table, place, arrivals.at[k])
        for k, (table, place) in enumerate(zip(tables, held))
    ]
    for copy in copies:
        copy.start()
    return copies


def pieces_kernel(blocks, groups, sources, count, *refs):
    pieces, refs = refs[:count], refs[count:]
    columns, row_factors, tables, refs = refs[0:2], refs[2:4], refs[4:6], refs[6:]
    out, partial, joined, phases, weights, twiddle, table, arrivals = refs
    copies = start_tables(tables, (twiddle, table), arrivals)
    make_phases(groups, phases)
    reduce_pieces(blocks, sources, pieces, columns, phases, weights, partial)
    finish_pieces(
        blocks, sources, copies, row_factors, twiddle, table, out, partial, joined
    )


def own_kernel(blocks, groups, sources, *refs):
    row_factors, sent, refs = refs[1:3], refs[3:8], refs[8:]
    out, partial, joined, phases, weights = refs[:5]
    held, arrivals = refs[5:10], refs[10]
    copies = start_tables(sent, held, arrivals)
    make_phases(groups, phases)
    for copy in copies[2:]:
        copy.wait()
    twiddle, table, own, *columns = held
    reduce_pieces(blocks, sources, [own], columns, phases, weights, partial)
    finish_pieces(
        blocks, sources, copies[:2], row_factors, twiddle, table, out, partial, joined
    )


def reduce_pieces(blocks, sources, pieces, columns, phases, weights, partial):
    rows_here = pieces[0].shape[-2]
    terms, width = columns[0].shape
    ranks = lax.axis_size("rank")
    span = width // ranks
    rank_at = lax.axis_index("rank")
    starts = [(rank_at ^ other) * span for other in HELD_PARTS]

    def fetch(part, row, lane):
        quarters, _, _ = sources[row // rows_here]
        row = pl.ds(row % rows_here, 1)
        if quarters is None:
            return pieces[0][row, pl.ds(pl.multiple_of(starts[part] + lane, LANES), LANES)]
        number, index = quarters[part]
        return pieces[number][index, row, pl.ds(pl.multiple_of(lane, LANES), LANES)]

    factors_at = made_factors(columns, phases, weights)
    rows = len(sources) * rows_here
    reduce_rows(blocks, rows, terms, fetch, factors_at, starts, span, partial)


def finish_pieces(blocks, sources, copies, row_factors, twiddle, table, out, partial, joined):
    rows = partial.shape[2]
    rows_here = rows // len(sources)
    bases = [comp_of(step, flipped) * rows_here for _, step, flipped in sources]

    def row_at(row):
        return bases[row // rows_here] + row % rows_here

    for copy in copies:
        copy.wait()
    transform_rows(blocks, rows, row_at, row_factors, twiddle, table, out, partial, joined)


def gathered_kernel(blocks, groups, pieces, *refs):
    columns, row_factors, tables, refs = refs[0:2], refs[2:4], refs[4:6], refs[6:]
    out, partial, joined, phases, weights, twiddle, table, arrivals = refs
    copies = start_tables(tables, (twiddle, table), arrivals)
    make_phases(groups, phases)
    parts, rows_here, span = pieces.shape[1:]

    def fetch(part, row, lane):
        place = pl.ds(pl.multiple_of(lane, LANES), LANES)
        return pieces[row // rows_here, part, pl.ds(row % rows_here, 1), place]

    base = pl.program_id(0) * 8
    starts = [part * span for part in range(parts)]
    terms = columns[0].shape[0]
    factors_at = made_factors(columns, phases, weights)
    reduce_rows(blocks, 8, terms, fetch, factors_at, starts, span, partial)
    for copy in copies:
        copy.wait()
    transform_rows(
        blocks,
        8,
        lambda row: base + row,
        row_factors,
        twiddle,
        table,
        out.at[0],
        partial,
        joined,
    )


def pass_kernel(*refs):
    del refs


def after(values, earlier):
    anywhere = pl.BlockSpec(memory_space=pl.ANY)
    operands = [pltpu.with_memory_space_constraint(x, pltpu.VMEM) for x in (*values, earlier)]
    return pl.pallas_call(
        pass_kernel,
        out_shape=[jax.ShapeDtypeStruct(value.shape, value.dtype) for value in values],
        in_specs=[anywhere] * len(operands),
        out_specs=[anywhere] * len(values),
        input_output_aliases={k: k for k in range(len(values))},
    )(*operands)


def convolve_kernel(blocks, rows_here, layout, tile_count, *refs):
    tiles = refs[:tile_count]
    back, out, spectrum, product, mixed = refs[tile_count:]
    total_rows = spectrum.shape[2] - PAD
    terms = spectrum.shape[3]
    spectrum[:, :, pl.ds(0, PAD)] = jnp.zeros((2 * blocks, 3, PAD, terms, LANES), jnp.float32)
    moves = []
    for number, tile in enumerate(tiles):
        for at in range(tile.shape[0]):
            for first in range(0, tile.shape[3], rows_here):
                moves.append((tile, at, first))
    comps = [comp_of(*layout[k]) if layout else k for k in range(len(moves))]

    def collect(plane, carry):
        for (tile, at, first), comp in zip(moves, comps):
            real = tile[at, plane, 0, pl.ds(first, rows_here)]
            imag = tile[at, plane, 1, pl.ds(first, rows_here)]
            place = pl.ds(PAD + comp * rows_here, rows_here)
            spectrum[plane, 0, place] = real
            spectrum[plane, 1, place] = imag
            spectrum[plane, 2, place] = real + imag
        return carry

    lax.fori_loop(0, 2 * blocks, collect, 0)

    def step(at, sums, block, out_tile, whole):
        sums = list(sums)
        left_base = PAD + 4 * at
        right_base = PAD + 4 * (out_tile - at)
        for part in range(3):
            left = [spectrum[2 * block, part, left_base + k] for k in range(4)]
            right = {
                k: spectrum[2 * block + 1, part, right_base + k]
                for k in range(-3 if whole else 0, 4)
            }
            for row in range(4):
                for k in range(4 if whole else row + 1):
                    sums[row * 3 + part] += left[k] * right[row - k]
        return tuple(sums)

    def finish(sums, block, out_tile):
        for row in range(4):
            both_real, both_imag, crossed = sums[row * 3 : row * 3 + 3]
            base = (out_tile * 4 + row) * 2 * blocks + block
            product[base] = both_real - both_imag
            product[base + blocks] = crossed - both_real - both_imag

    zeros = (jnp.zeros((terms, LANES), jnp.float32),) * 12
    out_tiles = total_rows // 4

    def convolve_block(block, carry):
        for out_tile in range(out_tiles):
            sums = zeros
            for at in range(out_tile + 1):
                sums = step(at, sums, block, out_tile, at < out_tile)
            finish(sums, block, out_tile)
        return carry

    def convolve_tile(index, carry):
        block = lax.rem(index, blocks)
        out_tile = lax.div(index, blocks)
        sums = lax.fori_loop(
            0, out_tile + 1, lambda at, sums: step(at, sums, block, out_tile, True), zeros
        )
        finish(sums, block, out_tile)
        return carry

    if total_rows <= 32:
        lax.fori_loop(0, blocks, convolve_block, 0)
    else:
        lax.fori_loop(0, out_tiles * blocks, convolve_tile, 0)

    def gather_terms(at, carry):
        tiles = [product[at * 8 + k] for k in range(8)]
        summed = jnp.sum(jnp.stack(tiles), axis=1)
        if blocks == 4:
            turned = jnp.concatenate([summed[blocks:], -summed[:blocks]], axis=0)
        else:
            swapped = [
                tiles[k + blocks] if (k // blocks) % 2 == 0 else -tiles[k - blocks]
                for k in range(8)
            ]
            turned = jnp.sum(jnp.stack(swapped), axis=1)
        place = pl.ds(pl.multiple_of(at * 8, 8), 8)
        mixed[place, pl.ds(0, LANES)] = summed
        mixed[place, pl.ds(LANES, LANES)] = turned
        return carry

    lax.fori_loop(0, total_rows * 2 * blocks // 8, gather_terms, 0, unroll=4)
    out[...] = dot_split(mixed[...], back[...])


def final_kernel(scaling, spread, inner_cos, inner_sin, outer, out):
    values = spread[...]
    stacked = jnp.concatenate([values * inner_cos[...], values * inner_sin[...]], axis=0)
    high, low = split_parts(stacked)
    joined = jnp.concatenate([high, low, high], axis=0)
    total = jnp.dot(outer[...], joined, preferred_element_type=jnp.float32)
    out[...] = total * scaling


def in_hbm(array):
    return pltpu.with_memory_space_constraint(array, pltpu.HBM)


def whole_call(kernel, out_shapes, scratch, operands, tables=(), kept=True):
    out_type = pltpu.VMEM if kept else jax.ShapeDtypeStruct
    operands = [pltpu.with_memory_space_constraint(operand, pltpu.VMEM) for operand in operands]
    return pl.pallas_call(
        kernel,
        out_shape=[out_type(shape, jnp.float32) for shape in out_shapes],
        in_specs=[pl.BlockSpec(memory_space=pltpu.VMEM)] * len(operands)
        + [pl.BlockSpec(memory_space=pltpu.HBM)] * len(tables),
        out_specs=[pl.BlockSpec(memory_space=pltpu.VMEM)] * len(out_shapes),
        scratch_shapes=scratch,
        compiler_params=pltpu.CompilerParams(vmem_limit_bytes=VMEM_BYTES),
    )(*operands, *[in_hbm(table) for table in tables])


def row_scratch(blocks, rows, terms, width, tables):
    return [
        pltpu.VMEM((4, blocks, rows, terms, LANES), jnp.float32),
        pltpu.VMEM((2 * blocks * rows * terms, 6 * LANES), jnp.bfloat16),
        pltpu.VMEM((2, width // LANES, LANES), jnp.float32),
        pltpu.VMEM((4, terms, width), jnp.float32),
        *[pltpu.VMEM(table.shape, table.dtype) for table in tables],
        pltpu.SemaphoreType.DMA((len(tables),)),
    ]


def spectra_by_exchange(density, blocks, groups, columns, row_factors, tables):
    rows_here, width = density.shape
    comps, ranks = lax.axis_size("comp"), lax.axis_size("rank")
    part = width // ranks
    lines = comps // 2
    terms = row_factors[0].shape[0]
    mine = lax.dynamic_slice_in_dim(density, lax.axis_index("rank") * part, part, 1)

    def along(block, step):
        pairs = [(c, ((c // 2 + step) % lines) * 2 + c % 2) for c in range(comps)]
        return lax.ppermute(block, "comp", pairs)

    def across(block):
        return lax.ppermute(block, "comp", [(c, c ^ 1) for c in range(comps)])

    def swapped(block, other):
        return lax.ppermute(block, "rank", [(r, r ^ other) for r in range(ranks)])

    def spectra(kernel, sources, operands, fetched):
        rows = rows_here * len(sources)
        (tile,) = whole_call(
            lambda *refs: kernel(blocks, groups, sources, *refs),
            [(2 * blocks, 2, rows, terms, LANES)],
            row_scratch(blocks, rows, terms, width, fetched),
            (*operands, *row_factors),
            fetched,
        )
        return tile

    def joined_spectra(pieces, sources):
        def kernel(blocks, groups, sources, *refs):
            pieces_kernel(blocks, groups, sources, len(pieces), *refs)

        return spectra(kernel, sources, (*pieces, *columns), tables)

    own_source = (None, 0, False)
    early = [(0, True)] + [(step, False) for step in range(1, lines)]
    late = [(step, True) for step in range(1, lines)]

    def quartered(places):
        return [(tuple((q, k) for q in range(4)), *place) for k, place in enumerate(places)]

    lined = [along(mine, step) for step in range(1, lines)]
    near = jnp.stack([across(mine), *lined])
    flipped = across(jnp.stack(lined))
    beyond, beside = swapped(near, 2), swapped(near, 1)
    flipped_beyond, flipped_beside = swapped(flipped, 2), swapped(flipped, 1)
    own = spectra(own_kernel, [own_source], (near,), (*tables, density, *columns))
    (beyond,) = after([beyond], own)
    first = joined_spectra([near, beyond, beside, swapped(beyond, 1)], quartered(early))
    (flipped_beyond,) = after([flipped_beyond], first)
    second = joined_spectra(
        [flipped, flipped_beyond, flipped_beside, swapped(flipped_beyond, 1)], quartered(late)
    )
    layout = [own_source[1:]] + early + late
    return [own[None], first[None], second[None]], layout


def spectra_by_gather(density, blocks, groups, columns, row_factors, tables):
    rows_here, width = density.shape
    comps, ranks = lax.axis_size("comp"), lax.axis_size("rank")
    terms = row_factors[0].shape[0]
    total_rows = rows_here * comps
    part = width // ranks
    mine = lax.dynamic_slice_in_dim(density, lax.axis_index("rank") * part, part, 1)
    gathered = lax.all_gather(mine, AXES, axis=0).reshape(comps, ranks, rows_here, part)
    tile_shape = (2 * blocks, 2, 8, terms, LANES)
    spectra = pl.pallas_call(
        lambda *refs: gathered_kernel(blocks, groups, *refs),
        grid=(total_rows // 8,),
        out_shape=jax.ShapeDtypeStruct((total_rows // 8, *tile_shape), jnp.float32),
        in_specs=[pl.BlockSpec((8 // rows_here, ranks, rows_here, part), lambda t: (t, 0, 0, 0))]
        + [pl.BlockSpec(memory_space=pltpu.VMEM)] * 4
        + [pl.BlockSpec(memory_space=pltpu.HBM)] * len(tables),
        out_specs=pl.BlockSpec((1, *tile_shape), lambda t: (t, 0, 0, 0, 0, 0)),
        scratch_shapes=row_scratch(blocks, 8, terms, width, tables),
        compiler_params=pltpu.CompilerParams(vmem_limit_bytes=VMEM_BYTES),
    )(gathered, *columns, *row_factors, *[in_hbm(table) for table in tables])
    return [spectra], None


def body(density, row_left, col_left, row_right, col_right):
    rows_here, width = density.shape
    comps = lax.axis_size("comp")
    devices = comps * lax.axis_size("rank")
    total_rows = rows_here * comps
    terms = row_left.shape[0]
    groups = min(devices, width // LANES)
    term_groups = devices // groups
    blocks = width // (groups * LANES)
    device_at = lax.axis_index(AXES)
    if term_groups > 1:
        term_at = lax.broadcasted_iota(jnp.int32, (terms, 1), 0)
        chosen = lax.div(term_at, terms // term_groups) == lax.div(device_at, groups)
        col_left = jnp.where(chosen, col_left, 0.0)
        col_right = jnp.where(chosen, col_right, 0.0)
    columns = (col_left, col_right)
    row_factors = (row_left, row_right)
    tables = (block_twiddles(blocks), split_rows(forward_table()))
    spectra = spectra_by_exchange if comps <= 8 else spectra_by_gather
    tiles, layout = spectra(density, blocks, groups, columns, row_factors, tables)

    out_rows = total_rows * 2 * blocks
    (sent,) = whole_call(
        lambda *refs: convolve_kernel(blocks, rows_here, layout, len(tiles), *refs),
        [(out_rows, LANES)],
        [
            pltpu.VMEM((2 * blocks, 3, PAD + total_rows, terms, LANES), jnp.float32),
            pltpu.VMEM((out_rows, terms, LANES), jnp.float32),
            pltpu.VMEM((out_rows, 2 * LANES), jnp.float32),
        ],
        (*tiles, split_rows(inverse_table())),
    )
    spread = lax.all_to_all(sent, AXES, split_axis=0, concat_axis=0, tiled=True)
    inner_cos, inner_sin, outer_table = final_tables(devices, groups, blocks, width)
    scaling = 0.5 / (math.sqrt(total_rows * width) * width)
    (result,) = whole_call(
        lambda *refs: final_kernel(scaling, *refs),
        [(width // LANES, LANES)],
        [],
        (
            spread,
            jnp.asarray(inner_cos, jnp.float32),
            jnp.asarray(inner_sin, jnp.float32),
            split_columns(outer_table),
        ),
        kept=False,
    )
    return result.reshape(1, width)


def solution(mesh):
    return jax.shard_map(
        body,
        mesh=mesh,
        in_specs=(P("comp", None), P(), P(), P(), P()),
        out_specs=P(AXES, None),
        check_vma=False,
    )
```

```python
import math

import jax
import jax.numpy as jnp
import numpy as np
from jax import lax
from jax.experimental import pallas as pl
from jax.experimental.pallas import tpu as pltpu
from jax.sharding import PartitionSpec as P

LANES = 128
VMEM_BYTES = 16 * 1024 * 1024
AXES = ("comp", "rank")
PAD = 4
HELD_PARTS = (0, 2, 1, 3)


def split_parts(values):
    high = values.astype(jnp.bfloat16)
    low = (values - high.astype(jnp.float32)).astype(jnp.bfloat16)
    return high, low


def split_rows(table):
    high, low = split_parts(jnp.asarray(table, jnp.float32))
    return jnp.concatenate([high, high, low], axis=0)


def split_columns(table):
    high, low = split_parts(jnp.asarray(table, jnp.float32))
    return jnp.concatenate([high, high, low], axis=1)


def dot_split(rows, table):
    high, low = split_parts(rows)
    joined = jnp.concatenate([high, low, high], axis=1)
    return jnp.dot(joined, table, preferred_element_type=jnp.float32)


def forward_table():
    angles = 2.0 * np.pi * np.outer(np.arange(LANES), np.arange(LANES)) / LANES
    cosine, sine = np.cos(angles), np.sin(angles)
    return np.block([[cosine, -sine], [sine, cosine]])


def inverse_table():
    angles = 2.0 * np.pi * np.outer(np.arange(LANES), np.arange(LANES)) / LANES
    return np.concatenate([np.cos(angles), -np.sin(angles)], axis=0)


def block_twiddles(blocks):
    angles = 2.0 * np.pi * np.outer(np.arange(blocks), np.arange(LANES)) / (blocks * LANES)
    table = np.stack([np.cos(angles), -np.sin(angles)], axis=1)
    return jnp.asarray(
        np.broadcast_to(table[:, :, None, :], (blocks, 2, 8, LANES)), jnp.float32
    )


def final_tables(devices, groups, blocks, width):
    owner = np.arange(devices) % groups
    frequency = (owner[:, None] + groups * np.arange(blocks)[None, :]).astype(np.float64) + 0.25
    frequency = np.broadcast_to(frequency[:, None, :], (devices, 2, blocks))
    inner = 2.0 * np.pi * frequency[..., None] * np.arange(LANES) / width
    rows = devices * 2 * blocks
    inner_cos = np.cos(inner).reshape(rows, LANES)
    inner_sin = np.sin(inner).reshape(rows, LANES)
    outer_count = width // LANES
    outer = 2.0 * np.pi * frequency * LANES / width
    outer = np.arange(outer_count)[:, None] * outer.reshape(1, rows)
    is_real = np.broadcast_to(np.array([True, False])[None, :, None], (devices, 2, blocks))
    is_real = is_real.reshape(1, rows)
    with_cos = np.where(is_real, np.cos(outer), -np.sin(outer))
    with_sin = np.where(is_real, -np.sin(outer), -np.cos(outer))
    return inner_cos, inner_sin, np.concatenate([with_cos, with_sin], axis=1)


def block_fourier(reals, imags):
    count = len(reals)
    if count == 1:
        return reals, imags
    if count == 2:
        return (
            [reals[0] + reals[1], reals[0] - reals[1]],
            [imags[0] + imags[1], imags[0] - imags[1]],
        )
    even_real, odd_real = reals[0] + reals[2], reals[0] - reals[2]
    even_imag, odd_imag = imags[0] + imags[2], imags[0] - imags[2]
    pair_real, gap_real = reals[1] + reals[3], reals[1] - reals[3]
    pair_imag, gap_imag = imags[1] + imags[3], imags[1] - imags[3]
    return (
        [even_real + pair_real, odd_real + gap_imag, even_real - pair_real, odd_real - gap_imag],
        [even_imag + pair_imag, odd_imag - gap_real, even_imag - pair_imag, odd_imag + gap_real],
    )


def reduce_rows(blocks, rows, terms, fetch, factors_at, starts, span, partial):
    inner = blocks * LANES
    outer = span // inner
    unroll = math.gcd(16, outer)

    def reduce_block(block, first, count):
        sums = (jnp.zeros((terms, LANES), jnp.float32),) * (4 * count)
        for part, start in enumerate(starts):

            def step(at, sums, part=part, start=start):
                sums = list(sums)
                for extra in range(unroll):
                    lane = (at * unroll + extra) * inner + block * LANES
                    factors = factors_at(start + lane, first == 0)
                    for row in range(count):
                        value = fetch(part, first + row, lane)
                        value = jnp.broadcast_to(value, (terms, LANES))
                        for k in range(4):
                            sums[row * 4 + k] += value * factors[k]
                return tuple(sums)

            sums = lax.fori_loop(0, outer // unroll, step, sums)
        for row in range(count):
            for k in range(4):
                partial[k, block, first + row] = sums[row * 4 + k]

    def reduce_tiles(block, carry):
        for first in range(0, rows, 8):
            reduce_block(block, first, min(8, rows - first))
        return carry

    lax.fori_loop(0, blocks, reduce_tiles, 0)


def transform_rows(blocks, rows, row_at, row_factors, twiddle, table, out, partial, joined):
    terms, total_rows = row_factors[0].shape
    lanes = lax.broadcasted_iota(jnp.int32, (terms, total_rows), 1)

    def butterfly(row, side):
        picked = jnp.where(lanes == row_at(row), row_factors[side][...], 0.0)
        factor = jnp.sum(picked, axis=1, keepdims=True)
        factor = jnp.broadcast_to(factor, (terms, LANES))
        reals = [partial[2 * side, block, row] * factor for block in range(blocks)]
        imags = [partial[2 * side + 1, block, row] * factor for block in range(blocks)]
        reals, imags = block_fourier(reals, imags)
        for block in range(1, blocks):
            real, imag = reals[block], imags[block]
            cosine, sine = twiddle[block, 0], twiddle[block, 1]
            reals[block] = real * cosine - imag * sine
            imags[block] = real * sine + imag * cosine
        return reals, imags

    def butterfly_pair(pair):
        for side in range(2):
            both = [butterfly(pair * 2 + extra, side) for extra in range(2)]
            for block in range(blocks):
                base = ((block * 2 + side) * rows + pair * 2) * terms
                place = pl.ds(base, 2 * terms)
                for part in range(2):
                    values = jnp.concatenate([both[0][part][block], both[1][part][block]], axis=0)
                    high, low = split_parts(values)
                    for third, piece in enumerate((high, low, high)):
                        joined[place, pl.ds((third * 2 + part) * LANES, LANES)] = piece

    for pair in range(rows // 2):
        butterfly_pair(pair)
    planes = 2 * blocks
    step = planes * rows * terms
    while step > 512:
        step //= 2
    plane_step = step // (rows * terms)

    def transform(at, carry):
        place = pl.ds(pl.multiple_of(at * step, 16), step)
        total = jnp.dot(joined[place, :], table[...], preferred_element_type=jnp.float32)
        total = total.reshape(plane_step, rows, terms, 2 * LANES)
        place = pl.ds(at * plane_step, plane_step)
        out[place, 0] = total[..., :LANES]
        out[place, 1] = total[..., LANES:]
        return carry

    lax.fori_loop(0, planes // plane_step, transform, 0)


def comp_of(step, flipped):
    lines = lax.axis_size("comp") // 2
    comp_at = lax.axis_index("comp")
    line = lax.rem(lax.div(comp_at, 2) + lines - step, lines)
    side = lax.rem(comp_at, 2)
    return line * 2 + (1 - side if flipped else side)


def make_phases(groups, phases):
    width = phases.shape[1] * LANES
    device_at = lax.axis_index("comp") * lax.axis_size("rank") + lax.axis_index("rank")
    odd = 4 * lax.rem(device_at, groups) + 1

    def turned(cells):
        turns = (cells * odd) & (4 * width - 1)
        turns = jnp.where(turns >= 2 * width, turns - 4 * width, turns)
        angles = turns.astype(jnp.float32) * (2.0 * math.pi / (4 * width))
        return jnp.cos(angles), -jnp.sin(angles)

    count = phases.shape[1] // 8
    rows = lax.broadcasted_iota(jnp.int32, (8, LANES), 0)
    fine_cos, fine_sin = turned(rows * LANES + lax.broadcasted_iota(jnp.int32, (8, LANES), 1))
    rows = lax.broadcasted_iota(jnp.int32, (count, LANES), 0)
    coarse_cos, coarse_sin = turned(rows * (8 * LANES))
    for tile in range(count):
        cosine = jnp.broadcast_to(coarse_cos[tile : tile + 1], (8, LANES))
        sine = jnp.broadcast_to(coarse_sin[tile : tile + 1], (8, LANES))
        phases[0, pl.ds(tile * 8, 8), :] = fine_cos * cosine - fine_sin * sine
        phases[1, pl.ds(tile * 8, 8), :] = fine_cos * sine + fine_sin * cosine


def made_factors(columns, phases, kept):
    terms = columns[0].shape[0]

    def factors_at(lane, first):
        place = pl.ds(pl.multiple_of(lane, LANES), LANES)
        if not first:
            return [kept[k, :, place] for k in range(4)]
        turn = pl.ds(lax.div(lane, LANES), 1)
        factors = [
            column[:, place] * jnp.broadcast_to(phases[part, turn, :], (terms, LANES))
            for column in columns
            for part in range(2)
        ]
        for k in range(4):
            kept[k, :, place] = factors[k]
        return factors

    return factors_at


def start_tables(tables, held, arrivals):
    copies = [
        pltpu.make_async_copy(table, place, arrivals.at[k])
        for k, (table, place) in enumerate(zip(tables, held))
    ]
    for copy in copies:
        copy.start()
    return copies


def pieces_kernel(blocks, groups, sources, count, *refs):
    pieces, refs = refs[:count], refs[count:]
    columns, row_factors, tables, refs = refs[0:2], refs[2:4], refs[4:6], refs[6:]
    out, partial, joined, phases, weights, twiddle, table, arrivals = refs
    copies = start_tables(tables, (twiddle, table), arrivals)
    make_phases(groups, phases)
    reduce_pieces(blocks, sources, pieces, columns, phases, weights, partial)
    finish_pieces(
        blocks, sources, copies, row_factors, twiddle, table, out, partial, joined
    )


def own_kernel(blocks, groups, sources, *refs):
    row_factors, sent, refs = refs[0:2], refs[2:7], refs[7:]
    out, partial, joined, phases, weights = refs[:5]
    held, arrivals = refs[5:10], refs[10]
    copies = start_tables(sent, held, arrivals)
    make_phases(groups, phases)
    for copy in copies[2:]:
        copy.wait()
    twiddle, table, own, *columns = held
    reduce_pieces(blocks, sources, [own], columns, phases, weights, partial)
    finish_pieces(
        blocks, sources, copies[:2], row_factors, twiddle, table, out, partial, joined
    )


def reduce_pieces(blocks, sources, pieces, columns, phases, weights, partial):
    rows_here = pieces[0].shape[-2]
    terms, width = columns[0].shape
    ranks = lax.axis_size("rank")
    span = width // ranks
    rank_at = lax.axis_index("rank")
    starts = [(rank_at ^ other) * span for other in HELD_PARTS]

    def fetch(part, row, lane):
        quarters, _, _ = sources[row // rows_here]
        row = pl.ds(row % rows_here, 1)
        if quarters is None:
            return pieces[0][row, pl.ds(pl.multiple_of(starts[part] + lane, LANES), LANES)]
        number, index = quarters[part]
        return pieces[number][index, row, pl.ds(pl.multiple_of(lane, LANES), LANES)]

    factors_at = made_factors(columns, phases, weights)
    rows = len(sources) * rows_here
    reduce_rows(blocks, rows, terms, fetch, factors_at, starts, span, partial)


def finish_pieces(blocks, sources, copies, row_factors, twiddle, table, out, partial, joined):
    rows = partial.shape[2]
    rows_here = rows // len(sources)
    bases = [comp_of(step, flipped) * rows_here for _, step, flipped in sources]

    def row_at(row):
        return bases[row // rows_here] + row % rows_here

    for copy in copies:
        copy.wait()
    transform_rows(blocks, rows, row_at, row_factors, twiddle, table, out, partial, joined)


def gathered_kernel(blocks, groups, pieces, *refs):
    columns, row_factors, tables, refs = refs[0:2], refs[2:4], refs[4:6], refs[6:]
    out, partial, joined, phases, weights, twiddle, table, arrivals = refs
    copies = start_tables(tables, (twiddle, table), arrivals)
    make_phases(groups, phases)
    parts, rows_here, span = pieces.shape[1:]

    def fetch(part, row, lane):
        place = pl.ds(pl.multiple_of(lane, LANES), LANES)
        return pieces[row // rows_here, part, pl.ds(row % rows_here, 1), place]

    base = pl.program_id(0) * 8
    starts = [part * span for part in range(parts)]
    terms = columns[0].shape[0]
    factors_at = made_factors(columns, phases, weights)
    reduce_rows(blocks, 8, terms, fetch, factors_at, starts, span, partial)
    for copy in copies:
        copy.wait()
    transform_rows(
        blocks,
        8,
        lambda row: base + row,
        row_factors,
        twiddle,
        table,
        out.at[0],
        partial,
        joined,
    )


def pass_kernel(*refs):
    del refs


def after(values, earlier):
    anywhere = pl.BlockSpec(memory_space=pl.ANY)
    operands = [pltpu.with_memory_space_constraint(x, pltpu.VMEM) for x in (*values, earlier)]
    return pl.pallas_call(
        pass_kernel,
        out_shape=[jax.ShapeDtypeStruct(value.shape, value.dtype) for value in values],
        in_specs=[anywhere] * len(operands),
        out_specs=[anywhere] * len(values),
        input_output_aliases={k: k for k in range(len(values))},
    )(*operands)


def convolve_kernel(blocks, rows_here, layout, tile_count, *refs):
    tiles = refs[:tile_count]
    back, out, spectrum, product, mixed = refs[tile_count:]
    total_rows = spectrum.shape[2] - PAD
    terms = spectrum.shape[3]
    spectrum[:, :, pl.ds(0, PAD)] = jnp.zeros((2 * blocks, 3, PAD, terms, LANES), jnp.float32)
    moves = []
    for number, tile in enumerate(tiles):
        for at in range(tile.shape[0]):
            for first in range(0, tile.shape[3], rows_here):
                moves.append((tile, at, first))
    comps = [comp_of(*layout[k]) if layout else k for k in range(len(moves))]

    def collect(plane, carry):
        for (tile, at, first), comp in zip(moves, comps):
            real = tile[at, plane, 0, pl.ds(first, rows_here)]
            imag = tile[at, plane, 1, pl.ds(first, rows_here)]
            place = pl.ds(PAD + comp * rows_here, rows_here)
            spectrum[plane, 0, place] = real
            spectrum[plane, 1, place] = imag
            spectrum[plane, 2, place] = real + imag
        return carry

    lax.fori_loop(0, 2 * blocks, collect, 0)

    def step(at, sums, block, out_tile, whole):
        sums = list(sums)
        left_base = PAD + 4 * at
        right_base = PAD + 4 * (out_tile - at)
        for part in range(3):
            left = [spectrum[2 * block, part, left_base + k] for k in range(4)]
            right = {
                k: spectrum[2 * block + 1, part, right_base + k]
                for k in range(-3 if whole else 0, 4)
            }
            for row in range(4):
                for k in range(4 if whole else row + 1):
                    sums[row * 3 + part] += left[k] * right[row - k]
        return tuple(sums)

    def finish(sums, block, out_tile):
        for row in range(4):
            both_real, both_imag, crossed = sums[row * 3 : row * 3 + 3]
            base = (out_tile * 4 + row) * 2 * blocks + block
            product[base] = both_real - both_imag
            product[base + blocks] = crossed - both_real - both_imag

    zeros = (jnp.zeros((terms, LANES), jnp.float32),) * 12
    out_tiles = total_rows // 4

    def convolve_block(block, carry):
        for out_tile in range(out_tiles):
            sums = zeros
            for at in range(out_tile + 1):
                sums = step(at, sums, block, out_tile, at < out_tile)
            finish(sums, block, out_tile)
        return carry

    def convolve_tile(index, carry):
        block = lax.rem(index, blocks)
        out_tile = lax.div(index, blocks)
        sums = lax.fori_loop(
            0, out_tile + 1, lambda at, sums: step(at, sums, block, out_tile, True), zeros
        )
        finish(sums, block, out_tile)
        return carry

    if total_rows <= 32:
        lax.fori_loop(0, blocks, convolve_block, 0)
    else:
        lax.fori_loop(0, out_tiles * blocks, convolve_tile, 0)

    def gather_terms(at, carry):
        tiles = [product[at * 8 + k] for k in range(8)]
        summed = jnp.sum(jnp.stack(tiles), axis=1)
        if blocks == 4:
            turned = jnp.concatenate([summed[blocks:], -summed[:blocks]], axis=0)
        else:
            swapped = [
                tiles[k + blocks] if (k // blocks) % 2 == 0 else -tiles[k - blocks]
                for k in range(8)
            ]
            turned = jnp.sum(jnp.stack(swapped), axis=1)
        place = pl.ds(pl.multiple_of(at * 8, 8), 8)
        mixed[place, pl.ds(0, LANES)] = summed
        mixed[place, pl.ds(LANES, LANES)] = turned
        return carry

    lax.fori_loop(0, total_rows * 2 * blocks // 8, gather_terms, 0, unroll=4)
    out[...] = dot_split(mixed[...], back[...])


def final_kernel(scaling, spread, inner_cos, inner_sin, outer, out):
    values = spread[...]
    stacked = jnp.concatenate([values * inner_cos[...], values * inner_sin[...]], axis=0)
    high, low = split_parts(stacked)
    joined = jnp.concatenate([high, low, high], axis=0)
    total = jnp.dot(outer[...], joined, preferred_element_type=jnp.float32)
    out[...] = total * scaling


def in_hbm(array):
    return pltpu.with_memory_space_constraint(array, pltpu.HBM)


def whole_call(kernel, out_shapes, scratch, operands, tables=(), kept=True):
    out_type = pltpu.VMEM if kept else jax.ShapeDtypeStruct
    operands = [pltpu.with_memory_space_constraint(operand, pltpu.VMEM) for operand in operands]
    return pl.pallas_call(
        kernel,
        out_shape=[out_type(shape, jnp.float32) for shape in out_shapes],
        in_specs=[pl.BlockSpec(memory_space=pltpu.VMEM)] * len(operands)
        + [pl.BlockSpec(memory_space=pltpu.HBM)] * len(tables),
        out_specs=[pl.BlockSpec(memory_space=pltpu.VMEM)] * len(out_shapes),
        scratch_shapes=scratch,
        compiler_params=pltpu.CompilerParams(vmem_limit_bytes=VMEM_BYTES),
    )(*operands, *[in_hbm(table) for table in tables])


def row_scratch(blocks, rows, terms, width, tables):
    return [
        pltpu.VMEM((4, blocks, rows, terms, LANES), jnp.float32),
        pltpu.VMEM((2 * blocks * rows * terms, 6 * LANES), jnp.bfloat16),
        pltpu.VMEM((2, width // LANES, LANES), jnp.float32),
        pltpu.VMEM((4, terms, width), jnp.float32),
        *[pltpu.VMEM(table.shape, table.dtype) for table in tables],
        pltpu.SemaphoreType.DMA((len(tables),)),
    ]


def spectra_by_exchange(density, blocks, groups, columns, row_factors, tables):
    rows_here, width = density.shape
    comps, ranks = lax.axis_size("comp"), lax.axis_size("rank")
    part = width // ranks
    lines = comps // 2
    terms = row_factors[0].shape[0]
    mine = lax.dynamic_slice_in_dim(density, lax.axis_index("rank") * part, part, 1)

    def along(block, step):
        pairs = [(c, ((c // 2 + step) % lines) * 2 + c % 2) for c in range(comps)]
        return lax.ppermute(block, "comp", pairs)

    def across(block):
        return lax.ppermute(block, "comp", [(c, c ^ 1) for c in range(comps)])

    def swapped(block, other):
        return lax.ppermute(block, "rank", [(r, r ^ other) for r in range(ranks)])

    def spectra(kernel, sources, operands, fetched):
        rows = rows_here * len(sources)
        (tile,) = whole_call(
            lambda *refs: kernel(blocks, groups, sources, *refs),
            [(2 * blocks, 2, rows, terms, LANES)],
            row_scratch(blocks, rows, terms, width, fetched),
            (*operands, *row_factors),
            fetched,
        )
        return tile

    def joined_spectra(pieces, sources):
        def kernel(blocks, groups, sources, *refs):
            pieces_kernel(blocks, groups, sources, len(pieces), *refs)

        return spectra(kernel, sources, (*pieces, *columns), tables)

    own_source = (None, 0, False)
    early = [(0, True)] + [(step, False) for step in range(1, lines)]
    late = [(step, True) for step in range(1, lines)]

    def quartered(places):
        return [(tuple((q, k) for q in range(4)), *place) for k, place in enumerate(places)]

    lined = [along(mine, step) for step in range(1, lines)]
    flipped_own = across(mine)
    own = spectra(own_kernel, [own_source], (), (*tables, density, *columns))
    (lined[lines // 2 - 1],) = after([lined[lines // 2 - 1]], own)
    near = jnp.stack([flipped_own, *lined])
    flipped = across(jnp.stack(lined))
    beyond = swapped(near, 2)
    ready = [near, beyond, swapped(near, 1), swapped(beyond, 1)]
    flipped_beyond = swapped(flipped, 2)
    flipped_beside = swapped(flipped, 1)
    first = joined_spectra(ready, quartered(early))
    (flipped_beyond,) = after([flipped_beyond], first)
    second = joined_spectra(
        [flipped, flipped_beyond, flipped_beside, swapped(flipped_beyond, 1)], quartered(late)
    )
    layout = [own_source[1:]] + early + late
    return [own[None], first[None], second[None]], layout


def spectra_by_gather(density, blocks, groups, columns, row_factors, tables):
    rows_here, width = density.shape
    comps, ranks = lax.axis_size("comp"), lax.axis_size("rank")
    terms = row_factors[0].shape[0]
    total_rows = rows_here * comps
    part = width // ranks
    mine = lax.dynamic_slice_in_dim(density, lax.axis_index("rank") * part, part, 1)
    gathered = lax.all_gather(mine, AXES, axis=0).reshape(comps, ranks, rows_here, part)
    tile_shape = (2 * blocks, 2, 8, terms, LANES)
    spectra = pl.pallas_call(
        lambda *refs: gathered_kernel(blocks, groups, *refs),
        grid=(total_rows // 8,),
        out_shape=jax.ShapeDtypeStruct((total_rows // 8, *tile_shape), jnp.float32),
        in_specs=[pl.BlockSpec((8 // rows_here, ranks, rows_here, part), lambda t: (t, 0, 0, 0))]
        + [pl.BlockSpec(memory_space=pltpu.VMEM)] * 4
        + [pl.BlockSpec(memory_space=pltpu.HBM)] * len(tables),
        out_specs=pl.BlockSpec((1, *tile_shape), lambda t: (t, 0, 0, 0, 0, 0)),
        scratch_shapes=row_scratch(blocks, 8, terms, width, tables),
        compiler_params=pltpu.CompilerParams(vmem_limit_bytes=VMEM_BYTES),
    )(gathered, *columns, *row_factors, *[in_hbm(table) for table in tables])
    return [spectra], None


def body(density, row_left, col_left, row_right, col_right):
    rows_here, width = density.shape
    comps = lax.axis_size("comp")
    devices = comps * lax.axis_size("rank")
    total_rows = rows_here * comps
    terms = row_left.shape[0]
    groups = min(devices, width // LANES)
    term_groups = devices // groups
    blocks = width // (groups * LANES)
    device_at = lax.axis_index(AXES)
    if term_groups > 1:
        term_at = lax.broadcasted_iota(jnp.int32, (terms, 1), 0)
        chosen = lax.div(term_at, terms // term_groups) == lax.div(device_at, groups)
        col_left = jnp.where(chosen, col_left, 0.0)
        col_right = jnp.where(chosen, col_right, 0.0)
    columns = (col_left, col_right)
    row_factors = (row_left, row_right)
    tables = (block_twiddles(blocks), split_rows(forward_table()))
    spectra = spectra_by_exchange if comps <= 8 else spectra_by_gather
    tiles, layout = spectra(density, blocks, groups, columns, row_factors, tables)

    out_rows = total_rows * 2 * blocks
    (sent,) = whole_call(
        lambda *refs: convolve_kernel(blocks, rows_here, layout, len(tiles), *refs),
        [(out_rows, LANES)],
        [
            pltpu.VMEM((2 * blocks, 3, PAD + total_rows, terms, LANES), jnp.float32),
            pltpu.VMEM((out_rows, terms, LANES), jnp.float32),
            pltpu.VMEM((out_rows, 2 * LANES), jnp.float32),
        ],
        (*tiles, split_rows(inverse_table())),
    )
    spread = lax.all_to_all(sent, AXES, split_axis=0, concat_axis=0, tiled=True)
    inner_cos, inner_sin, outer_table = final_tables(devices, groups, blocks, width)
    scaling = 0.5 / (math.sqrt(total_rows * width) * width)
    (result,) = whole_call(
        lambda *refs: final_kernel(scaling, *refs),
        [(width // LANES, LANES)],
        [],
        (
            spread,
            jnp.asarray(inner_cos, jnp.float32),
            jnp.asarray(inner_sin, jnp.float32),
            split_columns(outer_table),
        ),
        kept=False,
    )
    return result.reshape(1, width)


def solution(mesh):
    return jax.shard_map(
        body,
        mesh=mesh,
        in_specs=(P("comp", None), P(), P(), P(), P()),
        out_specs=P(AXES, None),
        check_vma=False,
    )
```

```python
import math

import jax
import jax.numpy as jnp
import numpy as np
from jax import lax
from jax.experimental import pallas as pl
from jax.experimental.pallas import tpu as pltpu
from jax.sharding import PartitionSpec as P

LANES = 128
VMEM_BYTES = 16 * 1024 * 1024
AXES = ("comp", "rank")
PAD = 4
HELD_PARTS = (0, 2, 1, 3)


def split_parts(values):
    high = values.astype(jnp.bfloat16)
    low = (values - high.astype(jnp.float32)).astype(jnp.bfloat16)
    return high, low


def split_rows(table):
    high, low = split_parts(jnp.asarray(table, jnp.float32))
    return jnp.concatenate([high, high, low], axis=0)


def split_columns(table):
    high, low = split_parts(jnp.asarray(table, jnp.float32))
    return jnp.concatenate([high, high, low], axis=1)


def dot_split(rows, table):
    high, low = split_parts(rows)
    joined = jnp.concatenate([high, low, high], axis=1)
    return jnp.dot(joined, table, preferred_element_type=jnp.float32)


def forward_table():
    angles = 2.0 * np.pi * np.outer(np.arange(LANES), np.arange(LANES)) / LANES
    cosine, sine = np.cos(angles), np.sin(angles)
    return np.block([[cosine, -sine], [sine, cosine]])


def inverse_table():
    angles = 2.0 * np.pi * np.outer(np.arange(LANES), np.arange(LANES)) / LANES
    return np.concatenate([np.cos(angles), -np.sin(angles)], axis=0)


def block_twiddles(blocks):
    angles = 2.0 * np.pi * np.outer(np.arange(blocks), np.arange(LANES)) / (blocks * LANES)
    table = np.stack([np.cos(angles), -np.sin(angles)], axis=1)
    return jnp.asarray(
        np.broadcast_to(table[:, :, None, :], (blocks, 2, 8, LANES)), jnp.float32
    )


def final_tables(devices, groups, blocks, width):
    owner = np.arange(devices) % groups
    frequency = (owner[:, None] + groups * np.arange(blocks)[None, :]).astype(np.float64) + 0.25
    frequency = np.broadcast_to(frequency[:, None, :], (devices, 2, blocks))
    inner = 2.0 * np.pi * frequency[..., None] * np.arange(LANES) / width
    rows = devices * 2 * blocks
    inner_cos = np.cos(inner).reshape(rows, LANES)
    inner_sin = np.sin(inner).reshape(rows, LANES)
    outer_count = width // LANES
    outer = 2.0 * np.pi * frequency * LANES / width
    outer = np.arange(outer_count)[:, None] * outer.reshape(1, rows)
    is_real = np.broadcast_to(np.array([True, False])[None, :, None], (devices, 2, blocks))
    is_real = is_real.reshape(1, rows)
    with_cos = np.where(is_real, np.cos(outer), -np.sin(outer))
    with_sin = np.where(is_real, -np.sin(outer), -np.cos(outer))
    return inner_cos, inner_sin, np.concatenate([with_cos, with_sin], axis=1)


def block_fourier(reals, imags):
    count = len(reals)
    if count == 1:
        return reals, imags
    if count == 2:
        return (
            [reals[0] + reals[1], reals[0] - reals[1]],
            [imags[0] + imags[1], imags[0] - imags[1]],
        )
    even_real, odd_real = reals[0] + reals[2], reals[0] - reals[2]
    even_imag, odd_imag = imags[0] + imags[2], imags[0] - imags[2]
    pair_real, gap_real = reals[1] + reals[3], reals[1] - reals[3]
    pair_imag, gap_imag = imags[1] + imags[3], imags[1] - imags[3]
    return (
        [even_real + pair_real, odd_real + gap_imag, even_real - pair_real, odd_real - gap_imag],
        [even_imag + pair_imag, odd_imag - gap_real, even_imag - pair_imag, odd_imag + gap_real],
    )


def reduce_rows(blocks, rows, terms, fetch, factors_at, starts, span, partial):
    inner = blocks * LANES
    outer = span // inner
    unroll = math.gcd(16, outer)

    def reduce_block(block, first, count):
        sums = (jnp.zeros((terms, LANES), jnp.float32),) * (4 * count)
        for part, start in enumerate(starts):

            def step(at, sums, part=part, start=start):
                sums = list(sums)
                for extra in range(unroll):
                    lane = (at * unroll + extra) * inner + block * LANES
                    factors = factors_at(start + lane, first == 0)
                    for row in range(count):
                        value = fetch(part, first + row, lane)
                        value = jnp.broadcast_to(value, (terms, LANES))
                        for k in range(4):
                            sums[row * 4 + k] += value * factors[k]
                return tuple(sums)

            sums = lax.fori_loop(0, outer // unroll, step, sums)
        for row in range(count):
            for k in range(4):
                partial[k, block, first + row] = sums[row * 4 + k]

    def reduce_tiles(block, carry):
        for first in range(0, rows, 8):
            reduce_block(block, first, min(8, rows - first))
        return carry

    lax.fori_loop(0, blocks, reduce_tiles, 0)


def transform_rows(blocks, rows, row_at, row_factors, twiddle, table, out, partial, joined):
    terms, total_rows = row_factors[0].shape
    lanes = lax.broadcasted_iota(jnp.int32, (terms, total_rows), 1)

    def butterfly(row, side):
        picked = jnp.where(lanes == row_at(row), row_factors[side][...], 0.0)
        factor = jnp.sum(picked, axis=1, keepdims=True)
        factor = jnp.broadcast_to(factor, (terms, LANES))
        reals = [partial[2 * side, block, row] * factor for block in range(blocks)]
        imags = [partial[2 * side + 1, block, row] * factor for block in range(blocks)]
        reals, imags = block_fourier(reals, imags)
        for block in range(1, blocks):
            real, imag = reals[block], imags[block]
            cosine, sine = twiddle[block, 0], twiddle[block, 1]
            reals[block] = real * cosine - imag * sine
            imags[block] = real * sine + imag * cosine
        return reals, imags

    def butterfly_pair(pair):
        for side in range(2):
            both = [butterfly(pair * 2 + extra, side) for extra in range(2)]
            for block in range(blocks):
                base = ((block * 2 + side) * rows + pair * 2) * terms
                place = pl.ds(base, 2 * terms)
                for part in range(2):
                    values = jnp.concatenate([both[0][part][block], both[1][part][block]], axis=0)
                    high, low = split_parts(values)
                    for third, piece in enumerate((high, low, high)):
                        joined[place, pl.ds((third * 2 + part) * LANES, LANES)] = piece

    for pair in range(rows // 2):
        butterfly_pair(pair)
    planes = 2 * blocks
    step = planes * rows * terms
    while step > 512:
        step //= 2
    plane_step = step // (rows * terms)

    def transform(at, carry):
        place = pl.ds(pl.multiple_of(at * step, 16), step)
        total = jnp.dot(joined[place, :], table[...], preferred_element_type=jnp.float32)
        total = total.reshape(plane_step, rows, terms, 2 * LANES)
        place = pl.ds(at * plane_step, plane_step)
        out[place, 0] = total[..., :LANES]
        out[place, 1] = total[..., LANES:]
        return carry

    lax.fori_loop(0, planes // plane_step, transform, 0)


def comp_of(step, flipped):
    lines = lax.axis_size("comp") // 2
    comp_at = lax.axis_index("comp")
    line = lax.rem(lax.div(comp_at, 2) + lines - step, lines)
    side = lax.rem(comp_at, 2)
    return line * 2 + (1 - side if flipped else side)


def make_phases(groups, phases):
    width = phases.shape[1] * LANES
    device_at = lax.axis_index("comp") * lax.axis_size("rank") + lax.axis_index("rank")
    odd = 4 * lax.rem(device_at, groups) + 1

    def turned(cells):
        turns = (cells * odd) & (4 * width - 1)
        turns = jnp.where(turns >= 2 * width, turns - 4 * width, turns)
        angles = turns.astype(jnp.float32) * (2.0 * math.pi / (4 * width))
        return jnp.cos(angles), -jnp.sin(angles)

    count = phases.shape[1] // 8
    rows = lax.broadcasted_iota(jnp.int32, (8, LANES), 0)
    fine_cos, fine_sin = turned(rows * LANES + lax.broadcasted_iota(jnp.int32, (8, LANES), 1))
    rows = lax.broadcasted_iota(jnp.int32, (count, LANES), 0)
    coarse_cos, coarse_sin = turned(rows * (8 * LANES))
    for tile in range(count):
        cosine = jnp.broadcast_to(coarse_cos[tile : tile + 1], (8, LANES))
        sine = jnp.broadcast_to(coarse_sin[tile : tile + 1], (8, LANES))
        phases[0, pl.ds(tile * 8, 8), :] = fine_cos * cosine - fine_sin * sine
        phases[1, pl.ds(tile * 8, 8), :] = fine_cos * sine + fine_sin * cosine


def made_factors(columns, phases, kept):
    terms = columns[0].shape[0]

    def factors_at(lane, first):
        place = pl.ds(pl.multiple_of(lane, LANES), LANES)
        if not first:
            return [kept[k, :, place] for k in range(4)]
        turn = pl.ds(lax.div(lane, LANES), 1)
        factors = [
            column[:, place] * jnp.broadcast_to(phases[part, turn, :], (terms, LANES))
            for column in columns
            for part in range(2)
        ]
        for k in range(4):
            kept[k, :, place] = factors[k]
        return factors

    return factors_at


def start_tables(tables, held, arrivals):
    copies = [
        pltpu.make_async_copy(table, place, arrivals.at[k])
        for k, (table, place) in enumerate(zip(tables, held))
    ]
    for copy in copies:
        copy.start()
    return copies


def pieces_kernel(blocks, groups, sources, count, *refs):
    pieces, refs = refs[:count], refs[count:]
    columns, row_factors, tables, refs = refs[0:2], refs[2:4], refs[4:6], refs[6:]
    out, partial, joined, phases, weights, twiddle, table, arrivals = refs
    copies = start_tables(tables, (twiddle, table), arrivals)
    make_phases(groups, phases)
    reduce_pieces(blocks, sources, pieces, columns, phases, weights, partial)
    finish_pieces(
        blocks, sources, copies, row_factors, twiddle, table, out, partial, joined
    )


def own_kernel(blocks, groups, sources, *refs):
    row_factors, sent, refs = refs[0:2], refs[2:7], refs[7:]
    out, partial, joined, phases, weights = refs[:5]
    held, arrivals = refs[5:10], refs[10]
    copies = start_tables(sent, held, arrivals)
    make_phases(groups, phases)
    for copy in copies[2:]:
        copy.wait()
    twiddle, table, own, *columns = held
    reduce_pieces(blocks, sources, [own], columns, phases, weights, partial)
    finish_pieces(
        blocks, sources, copies[:2], row_factors, twiddle, table, out, partial, joined
    )


def reduce_pieces(blocks, sources, pieces, columns, phases, weights, partial):
    rows_here = pieces[0].shape[-2]
    terms, width = columns[0].shape
    ranks = lax.axis_size("rank")
    span = width // ranks
    rank_at = lax.axis_index("rank")
    starts = [(rank_at ^ other) * span for other in HELD_PARTS]

    def fetch(part, row, lane):
        quarters, _, _ = sources[row // rows_here]
        row = pl.ds(row % rows_here, 1)
        if quarters is None:
            return pieces[0][row, pl.ds(pl.multiple_of(starts[part] + lane, LANES), LANES)]
        number, index = quarters[part]
        return pieces[number][index, row, pl.ds(pl.multiple_of(lane, LANES), LANES)]

    factors_at = made_factors(columns, phases, weights)
    rows = len(sources) * rows_here
    reduce_rows(blocks, rows, terms, fetch, factors_at, starts, span, partial)


def finish_pieces(blocks, sources, copies, row_factors, twiddle, table, out, partial, joined):
    rows = partial.shape[2]
    rows_here = rows // len(sources)
    bases = [comp_of(step, flipped) * rows_here for _, step, flipped in sources]

    def row_at(row):
        return bases[row // rows_here] + row % rows_here

    for copy in copies:
        copy.wait()
    transform_rows(blocks, rows, row_at, row_factors, twiddle, table, out, partial, joined)


def gathered_kernel(blocks, groups, pieces, *refs):
    columns, row_factors, tables, refs = refs[0:2], refs[2:4], refs[4:6], refs[6:]
    out, partial, joined, phases, weights, twiddle, table, arrivals = refs
    copies = start_tables(tables, (twiddle, table), arrivals)
    make_phases(groups, phases)
    parts, rows_here, span = pieces.shape[1:]

    def fetch(part, row, lane):
        place = pl.ds(pl.multiple_of(lane, LANES), LANES)
        return pieces[row // rows_here, part, pl.ds(row % rows_here, 1), place]

    base = pl.program_id(0) * 8
    starts = [part * span for part in range(parts)]
    terms = columns[0].shape[0]
    factors_at = made_factors(columns, phases, weights)
    reduce_rows(blocks, 8, terms, fetch, factors_at, starts, span, partial)
    for copy in copies:
        copy.wait()
    transform_rows(
        blocks,
        8,
        lambda row: base + row,
        row_factors,
        twiddle,
        table,
        out.at[0],
        partial,
        joined,
    )


def pass_kernel(*refs):
    del refs


def after(values, earlier):
    anywhere = pl.BlockSpec(memory_space=pl.ANY)
    operands = [pltpu.with_memory_space_constraint(x, pltpu.VMEM) for x in (*values, earlier)]
    return pl.pallas_call(
        pass_kernel,
        out_shape=[jax.ShapeDtypeStruct(value.shape, value.dtype) for value in values],
        in_specs=[anywhere] * len(operands),
        out_specs=[anywhere] * len(values),
        input_output_aliases={k: k for k in range(len(values))},
    )(*operands)


def convolve_kernel(blocks, rows_here, layout, tile_count, *refs):
    tiles = refs[:tile_count]
    back, out, spectrum, product, mixed = refs[tile_count:]
    total_rows = spectrum.shape[2] - PAD
    terms = spectrum.shape[3]
    spectrum[:, :, pl.ds(0, PAD)] = jnp.zeros((2 * blocks, 3, PAD, terms, LANES), jnp.float32)
    moves = []
    for number, tile in enumerate(tiles):
        for at in range(tile.shape[0]):
            for first in range(0, tile.shape[3], rows_here):
                moves.append((tile, at, first))
    comps = [comp_of(*layout[k]) if layout else k for k in range(len(moves))]

    def collect(plane, carry):
        for (tile, at, first), comp in zip(moves, comps):
            real = tile[at, plane, 0, pl.ds(first, rows_here)]
            imag = tile[at, plane, 1, pl.ds(first, rows_here)]
            place = pl.ds(PAD + comp * rows_here, rows_here)
            spectrum[plane, 0, place] = real
            spectrum[plane, 1, place] = imag
            spectrum[plane, 2, place] = real + imag
        return carry

    lax.fori_loop(0, 2 * blocks, collect, 0)

    def step(at, sums, block, out_tile, whole):
        sums = list(sums)
        left_base = PAD + 4 * at
        right_base = PAD + 4 * (out_tile - at)
        for part in range(3):
            left = [spectrum[2 * block, part, left_base + k] for k in range(4)]
            right = {
                k: spectrum[2 * block + 1, part, right_base + k]
                for k in range(-3 if whole else 0, 4)
            }
            for row in range(4):
                for k in range(4 if whole else row + 1):
                    sums[row * 3 + part] += left[k] * right[row - k]
        return tuple(sums)

    def finish(sums, block, out_tile):
        for row in range(4):
            both_real, both_imag, crossed = sums[row * 3 : row * 3 + 3]
            base = (out_tile * 4 + row) * 2 * blocks + block
            product[base] = both_real - both_imag
            product[base + blocks] = crossed - both_real - both_imag

    zeros = (jnp.zeros((terms, LANES), jnp.float32),) * 12
    out_tiles = total_rows // 4

    def convolve_block(block, carry):
        for out_tile in range(out_tiles):
            sums = zeros
            for at in range(out_tile + 1):
                sums = step(at, sums, block, out_tile, at < out_tile)
            finish(sums, block, out_tile)
        return carry

    def convolve_tile(index, carry):
        block = lax.rem(index, blocks)
        out_tile = lax.div(index, blocks)
        sums = lax.fori_loop(
            0, out_tile + 1, lambda at, sums: step(at, sums, block, out_tile, True), zeros
        )
        finish(sums, block, out_tile)
        return carry

    if total_rows <= 32:
        lax.fori_loop(0, blocks, convolve_block, 0)
    else:
        lax.fori_loop(0, out_tiles * blocks, convolve_tile, 0)

    def gather_terms(at, carry):
        tiles = [product[at * 8 + k] for k in range(8)]
        summed = jnp.sum(jnp.stack(tiles), axis=1)
        if blocks == 4:
            turned = jnp.concatenate([summed[blocks:], -summed[:blocks]], axis=0)
        else:
            swapped = [
                tiles[k + blocks] if (k // blocks) % 2 == 0 else -tiles[k - blocks]
                for k in range(8)
            ]
            turned = jnp.sum(jnp.stack(swapped), axis=1)
        place = pl.ds(pl.multiple_of(at * 8, 8), 8)
        mixed[place, pl.ds(0, LANES)] = summed
        mixed[place, pl.ds(LANES, LANES)] = turned
        return carry

    lax.fori_loop(0, total_rows * 2 * blocks // 8, gather_terms, 0, unroll=4)
    out[...] = dot_split(mixed[...], back[...])


def final_kernel(scaling, spread, inner_cos, inner_sin, outer, out):
    values = spread[...]
    stacked = jnp.concatenate([values * inner_cos[...], values * inner_sin[...]], axis=0)
    high, low = split_parts(stacked)
    joined = jnp.concatenate([high, low, high], axis=0)
    total = jnp.dot(outer[...], joined, preferred_element_type=jnp.float32)
    out[...] = total * scaling


def in_hbm(array):
    return pltpu.with_memory_space_constraint(array, pltpu.HBM)


def whole_call(kernel, out_shapes, scratch, operands, tables=(), kept=True):
    out_type = pltpu.VMEM if kept else jax.ShapeDtypeStruct
    operands = [pltpu.with_memory_space_constraint(operand, pltpu.VMEM) for operand in operands]
    return pl.pallas_call(
        kernel,
        out_shape=[out_type(shape, jnp.float32) for shape in out_shapes],
        in_specs=[pl.BlockSpec(memory_space=pltpu.VMEM)] * len(operands)
        + [pl.BlockSpec(memory_space=pltpu.HBM)] * len(tables),
        out_specs=[pl.BlockSpec(memory_space=pltpu.VMEM)] * len(out_shapes),
        scratch_shapes=scratch,
        compiler_params=pltpu.CompilerParams(vmem_limit_bytes=VMEM_BYTES),
    )(*operands, *[in_hbm(table) for table in tables])


def row_scratch(blocks, rows, terms, width, tables):
    return [
        pltpu.VMEM((4, blocks, rows, terms, LANES), jnp.float32),
        pltpu.VMEM((2 * blocks * rows * terms, 6 * LANES), jnp.bfloat16),
        pltpu.VMEM((2, width // LANES, LANES), jnp.float32),
        pltpu.VMEM((4, terms, width), jnp.float32),
        *[pltpu.VMEM(table.shape, table.dtype) for table in tables],
        pltpu.SemaphoreType.DMA((len(tables),)),
    ]


def spectra_by_exchange(density, blocks, groups, columns, row_factors, tables):
    rows_here, width = density.shape
    comps, ranks = lax.axis_size("comp"), lax.axis_size("rank")
    part = width // ranks
    lines = comps // 2
    terms = row_factors[0].shape[0]
    mine = lax.dynamic_slice_in_dim(density, lax.axis_index("rank") * part, part, 1)

    def along(block, step):
        pairs = [(c, ((c // 2 + step) % lines) * 2 + c % 2) for c in range(comps)]
        return lax.ppermute(block, "comp", pairs)

    def across(block):
        return lax.ppermute(block, "comp", [(c, c ^ 1) for c in range(comps)])

    def swapped(block, other):
        return lax.ppermute(block, "rank", [(r, r ^ other) for r in range(ranks)])

    def spectra(kernel, sources, operands, fetched):
        rows = rows_here * len(sources)
        (tile,) = whole_call(
            lambda *refs: kernel(blocks, groups, sources, *refs),
            [(2 * blocks, 2, rows, terms, LANES)],
            row_scratch(blocks, rows, terms, width, fetched),
            (*operands, *row_factors),
            fetched,
        )
        return tile

    def joined_spectra(pieces, sources):
        def kernel(blocks, groups, sources, *refs):
            pieces_kernel(blocks, groups, sources, len(pieces), *refs)

        return spectra(kernel, sources, (*pieces, *columns), tables)

    own_source = (None, 0, False)
    early = [(0, True)] + [(step, False) for step in range(1, lines)]
    late = [(step, True) for step in range(1, lines)]

    def quartered(places):
        return [(tuple((q, k) for q in range(4)), *place) for k, place in enumerate(places)]

    lined = [along(mine, step) for step in range(1, lines)]
    flipped_own = across(mine)
    own = spectra(own_kernel, [own_source], (), (*tables, density, *columns))
    (lined[lines // 2 - 1],) = after([lined[lines // 2 - 1]], own)
    near = jnp.stack([flipped_own, *lined])
    flipped = across(jnp.stack(lined))
    beyond = swapped(near, 2)
    beside = swapped(jnp.concatenate([near, beyond]), 1)
    count = len(early)
    joined = [
        (((0, k), (1, k), (2, k), (2, count + k)), *place) for k, place in enumerate(early)
    ]
    flipped_beyond = swapped(flipped, 2)
    flipped_beside = swapped(flipped, 1)
    first = joined_spectra([near, beyond, beside], joined)
    (flipped_beyond,) = after([flipped_beyond], first)
    second = joined_spectra(
        [flipped, flipped_beyond, flipped_beside, swapped(flipped_beyond, 1)], quartered(late)
    )
    layout = [own_source[1:]] + early + late
    return [own[None], first[None], second[None]], layout


def spectra_by_gather(density, blocks, groups, columns, row_factors, tables):
    rows_here, width = density.shape
    comps, ranks = lax.axis_size("comp"), lax.axis_size("rank")
    terms = row_factors[0].shape[0]
    total_rows = rows_here * comps
    part = width // ranks
    mine = lax.dynamic_slice_in_dim(density, lax.axis_index("rank") * part, part, 1)
    gathered = lax.all_gather(mine, AXES, axis=0).reshape(comps, ranks, rows_here, part)
    tile_shape = (2 * blocks, 2, 8, terms, LANES)
    spectra = pl.pallas_call(
        lambda *refs: gathered_kernel(blocks, groups, *refs),
        grid=(total_rows // 8,),
        out_shape=jax.ShapeDtypeStruct((total_rows // 8, *tile_shape), jnp.float32),
        in_specs=[pl.BlockSpec((8 // rows_here, ranks, rows_here, part), lambda t: (t, 0, 0, 0))]
        + [pl.BlockSpec(memory_space=pltpu.VMEM)] * 4
        + [pl.BlockSpec(memory_space=pltpu.HBM)] * len(tables),
        out_specs=pl.BlockSpec((1, *tile_shape), lambda t: (t, 0, 0, 0, 0, 0)),
        scratch_shapes=row_scratch(blocks, 8, terms, width, tables),
        compiler_params=pltpu.CompilerParams(vmem_limit_bytes=VMEM_BYTES),
    )(gathered, *columns, *row_factors, *[in_hbm(table) for table in tables])
    return [spectra], None


def body(density, row_left, col_left, row_right, col_right):
    rows_here, width = density.shape
    comps = lax.axis_size("comp")
    devices = comps * lax.axis_size("rank")
    total_rows = rows_here * comps
    terms = row_left.shape[0]
    groups = min(devices, width // LANES)
    term_groups = devices // groups
    blocks = width // (groups * LANES)
    device_at = lax.axis_index(AXES)
    if term_groups > 1:
        term_at = lax.broadcasted_iota(jnp.int32, (terms, 1), 0)
        chosen = lax.div(term_at, terms // term_groups) == lax.div(device_at, groups)
        col_left = jnp.where(chosen, col_left, 0.0)
        col_right = jnp.where(chosen, col_right, 0.0)
    columns = (col_left, col_right)
    row_factors = (row_left, row_right)
    tables = (block_twiddles(blocks), split_rows(forward_table()))
    spectra = spectra_by_exchange if comps <= 8 else spectra_by_gather
    tiles, layout = spectra(density, blocks, groups, columns, row_factors, tables)

    out_rows = total_rows * 2 * blocks
    (sent,) = whole_call(
        lambda *refs: convolve_kernel(blocks, rows_here, layout, len(tiles), *refs),
        [(out_rows, LANES)],
        [
            pltpu.VMEM((2 * blocks, 3, PAD + total_rows, terms, LANES), jnp.float32),
            pltpu.VMEM((out_rows, terms, LANES), jnp.float32),
            pltpu.VMEM((out_rows, 2 * LANES), jnp.float32),
        ],
        (*tiles, split_rows(inverse_table())),
    )
    spread = lax.all_to_all(sent, AXES, split_axis=0, concat_axis=0, tiled=True)
    inner_cos, inner_sin, outer_table = final_tables(devices, groups, blocks, width)
    scaling = 0.5 / (math.sqrt(total_rows * width) * width)
    (result,) = whole_call(
        lambda *refs: final_kernel(scaling, *refs),
        [(width // LANES, LANES)],
        [],
        (
            spread,
            jnp.asarray(inner_cos, jnp.float32),
            jnp.asarray(inner_sin, jnp.float32),
            split_columns(outer_table),
        ),
        kept=False,
    )
    return result.reshape(1, width)


def solution(mesh):
    return jax.shard_map(
        body,
        mesh=mesh,
        in_specs=(P("comp", None), P(), P(), P(), P()),
        out_specs=P(AXES, None),
        check_vma=False,
    )
```
